768 devices in a mesh: dp: 256 (over y, z_hi, x, core), space: 3 (over z_lo).
Axes of the slice: x: 4, y: 8, z: 12 (z_hi: 4, z_lo: 3; z = z_hi * 3 + z_lo), core: 2. Of those that a mesh axis runs over, the one named last changes fastest.
Arguments:
- images: bfloat16 [256, 24, 288, 256], P('dp', 'space'), may hold values from -12 to 12
- w_reduce: bfloat16 [256, 64], replicated, may hold values from -0.375 to 0.375
- w_dilated: bfloat16 [3, 3, 64, 64], replicated, may hold values from -0.25 to 0.25
- w_expand: bfloat16 [64, 256], replicated, may hold values from -0.75 to 0.75
- gain_one: float32 [64], replicated, may hold values from 0.25 to 1.75
- shift_one: float32 [64], replicated, may hold values from -3 to 3
- gain_two: float32 [64], replicated, may hold values from 0.25 to 1.75
- shift_two: float32 [64], replicated, may hold values from -3 to 3
- gain_three: float32 [256], replicated, may hold values from 0.25 to 1.75
- shift_three: float32 [256], replicated, may hold values from -3 to 3
- cotangent: bfloat16 [256, 24, 288, 256], P('dp', 'space'), may hold values from -6 to 6
Outputs:
- result: bfloat16 [256, 24, 288, 256], P('dp', 'space')
- grad_images: bfloat16 [256, 24, 288, 256], P('dp', 'space')
- grad_reduce: float32 [256, 64], replicated
- grad_dilated: float32 [3, 3, 64, 64], replicated
- grad_expand: float32 [64, 256], replicated
- grad_gain_one: float32 [64], replicated
- grad_shift_one: float32 [64], replicated
- grad_gain_two: float32 [64], replicated
- grad_shift_two: float32 [64], replicated
- grad_gain_three: float32 [256], replicated
- grad_shift_three: float32 [256], replicated
The draws below stay inside these ranges and needn't reach their ends.
All inputs are finite; a program needn't handle non-finite values.
Results may differ from the reference program's by a relative error of at most 0.012.
Values may be sent and summed in bfloat16 or wider, within the bound.
A program may use at most 32 MiB of HBM per device.

```python
import jax
import jax.numpy as jnp
from jax import lax

C = 256
M = 64
W = 288
H = 24
B = 256


def draw_images(key, part):
    key_base = jax.random.fold_in(key, 11)
    key_scale = jax.random.fold_in(key, 23)
    row_pos = jnp.arange(H, dtype=jnp.float32)
    row_scale = 1.0 + 2.0 * row_pos / max(H - 1, 1)
    pixel_scale = jnp.exp(jax.random.uniform(key_scale, (B, H, W, 1), jnp.float32, minval=-1.0986, maxval=0.0))
    base_vals = jax.random.truncated_normal(key_base, -4.0, 4.0, (B, H, W, C), jnp.float32)
    return (base_vals * pixel_scale * row_scale[None, :, None, None]).astype(jnp.bfloat16)


def shard_levels(own_key, dims, cuts, least, largest):
    level = 1.0
    for position, parts in cuts:
        draws = jax.random.uniform(jax.random.fold_in(jax.random.fold_in(own_key, 6), position), (parts,), jnp.float32, least / len(cuts), largest / len(cuts))
        level = level * jnp.repeat(jnp.exp(draws), dims[position] // parts).reshape((-1,) + (1,) * (len(dims) - 1 - position))
    return level


def scatter_about(stream_key, extent, spread, most, split=(), kind=jnp.bfloat16):
    values = spread * jax.random.normal(stream_key, extent, jnp.float32)
    if split:
        values = values * shard_levels(stream_key, extent, split, -0.22, 0.18)
    return jnp.clip(values, -most, most).astype(kind)


def setup_inputs(seed: int = 0) -> dict:
    arg_keys = jax.random.split(jax.random.key(seed), 12)
    images = draw_images(jax.random.fold_in(arg_keys[11], 71), 0)
    w_reduce = scatter_about(arg_keys[1], (C, M), C ** -0.5, 0.375)
    w_dilated = scatter_about(arg_keys[2], (3, 3, M, M), (9 * M) ** -0.5, 0.25)
    w_expand = scatter_about(arg_keys[3], (M, C), M ** -0.5, 0.75)
    gain_one = jnp.clip(1.0 + 0.15 * jax.random.normal(arg_keys[4], (M,), jnp.float32), 0.25, 1.75)
    shift_one = scatter_about(arg_keys[5], (M,), 0.5, 3.0, (), jnp.float32)
    gain_two = jnp.clip(1.0 + 0.15 * jax.random.normal(arg_keys[6], (M,), jnp.float32), 0.25, 1.75)
    shift_two = scatter_about(arg_keys[7], (M,), 0.5, 3.0, (), jnp.float32)
    gain_three = jnp.clip(1.0 + 0.15 * jax.random.normal(arg_keys[8], (C,), jnp.float32), 0.25, 1.75)
    shift_three = scatter_about(arg_keys[9], (C,), 0.5, 3.0, (), jnp.float32)
    cotangent = scatter_about(arg_keys[10], (B, H, W, C), 1.0, 6.0, ((0, 256), (1, 3)))
    return {"images": images, "w_reduce": w_reduce, "w_dilated": w_dilated, "w_expand": w_expand, "gain_one": gain_one, "shift_one": shift_one, "gain_two": gain_two, "shift_two": shift_two, "gain_three": gain_three, "shift_three": shift_three, "cotangent": cotangent}


epsilon = 1e-05

def smooth_act(value):
    return value * jax.nn.sigmoid(value)

def smooth_slope(value):
    sig = jax.nn.sigmoid(value)
    return sig * (1.0 + value * (1.0 - sig))

def norm_fwd(pre, gain, shift):
    count = pre.shape[0]
    average = lax.optimization_barrier(jnp.sum(pre, 0)) / count
    centred = pre - average
    variance = lax.optimization_barrier(jnp.sum(centred * centred, 0)) / count
    inv_std = lax.rsqrt(variance + epsilon)
    normed = centred * inv_std
    return (normed, inv_std, gain * normed + shift)

def norm_bwd(grad, normed, inv_std, gain):
    count = grad.shape[0]
    grad_sum = lax.optimization_barrier(jnp.sum(grad, 0))
    grad_cross = lax.optimization_barrier(jnp.sum(grad * normed, 0))
    back = (gain * inv_std * (grad - grad_sum / count - normed * grad_cross / count)).astype(jnp.bfloat16)
    return (back, grad_cross, grad_sum)

def dilated(padded, kernel, rows, cols):
    output = jnp.zeros((rows * cols, kernel.shape[3]), jnp.float32)
    for tap_row in range(3):
        for tap_col in range(3):
            window = padded[2 * tap_row:2 * tap_row + rows, 2 * tap_col:2 * tap_col + cols].reshape(rows * cols, -1)
            output = output + jnp.dot(window, kernel[tap_row, tap_col], preferred_element_type=jnp.float32)
    return output

def contract(left, right):
    return lax.dot_general(left, right, (((0,), (0,)), ((), ())), preferred_element_type=jnp.float32)

def one_sample(inputs, w_reduce, w_dilated, w_expand, gain_one, shift_one, gain_two, shift_two, gain_three, shift_three):
    images, cotangent = inputs
    rows, cols, chans = images.shape
    mids = w_reduce.shape[1]
    flat_in = images.reshape(rows * cols, chans)
    pre_one = jnp.dot(flat_in, w_reduce, preferred_element_type=jnp.float32)
    normed_one, istd_one, out_one = norm_fwd(pre_one, gain_one, shift_one)
    act_one = smooth_act(out_one).astype(jnp.bfloat16)
    padded_one = jnp.pad(act_one.reshape(rows, cols, mids), ((2, 2), (2, 2), (0, 0)))
    pre_two = dilated(padded_one, w_dilated, rows, cols)
    normed_two, istd_two, out_two = norm_fwd(pre_two, gain_two, shift_two)
    act_two = smooth_act(out_two).astype(jnp.bfloat16)
    pre_three = jnp.dot(act_two, w_expand, preferred_element_type=jnp.float32)
    normed_three, istd_three, out_three = norm_fwd(pre_three, gain_three, shift_three)
    summed = out_three + flat_in.astype(jnp.float32)
    result = smooth_act(summed).astype(jnp.bfloat16)
    grad_three = cotangent.reshape(rows * cols, chans).astype(jnp.float32) * smooth_slope(summed)
    dh_three, gg_three, gs_three = norm_bwd(grad_three, normed_three, istd_three, gain_three)
    gw_expand = contract(act_two, dh_three)
    back_two = lax.dot_general(dh_three, w_expand, (((1,), (1,)), ((), ())), preferred_element_type=jnp.float32)
    grad_two = back_two * smooth_slope(out_two)
    dh_two, gg_two, gs_two = norm_bwd(grad_two, normed_two, istd_two, gain_two)
    taps = []
    for tap_row in range(3):
        for tap_col in range(3):
            window = padded_one[2 * tap_row:2 * tap_row + rows, 2 * tap_col:2 * tap_col + cols].reshape(rows * cols, mids)
            taps.append(contract(window, dh_two))
    gw_dilated = jnp.stack(taps).reshape(3, 3, mids, mids)
    padded_back = jnp.pad(dh_two.reshape(rows, cols, mids), ((2, 2), (2, 2), (0, 0)))
    flipped = jnp.transpose(w_dilated[::-1, ::-1], (0, 1, 3, 2))
    grad_one = dilated(padded_back, flipped, rows, cols) * smooth_slope(out_one)
    dh_one, gg_one, gs_one = norm_bwd(grad_one, normed_one, istd_one, gain_one)
    gw_reduce = contract(flat_in, dh_one)
    back_in = lax.dot_general(dh_one, w_reduce, (((1,), (1,)), ((), ())), preferred_element_type=jnp.float32)
    grad_images = (back_in + grad_three).astype(jnp.bfloat16)
    return (result.reshape(rows, cols, chans), grad_images.reshape(rows, cols, chans), gw_reduce, gw_dilated, gw_expand, gg_one, gs_one, gg_two, gs_two, gg_three, gs_three)

def reference(images, w_reduce, w_dilated, w_expand, gain_one, shift_one, gain_two, shift_two, gain_three, shift_three, cotangent):

    def runner(inputs):
        return one_sample(inputs, w_reduce, w_dilated, w_expand, gain_one, shift_one, gain_two, shift_two, gain_three, shift_three)
    outputs = lax.map(runner, (images, cotangent))
    batch = images.shape[0]
    grads = [lax.optimization_barrier(jnp.sum(item, 0)) / batch for item in outputs[2:]]
    return (outputs[0], outputs[1], grads[0], grads[1], grads[2], grads[3], grads[4], grads[5], grads[6], grads[7], grads[8])
```

```python
import functools

import jax
import jax.numpy as jnp
from jax import lax
from jax.experimental import pallas as pl
from jax.experimental.pallas import tpu as pltpu
from jax.sharding import PartitionSpec as P

MESH = pl.DeviceIdType.MESH
f32 = jnp.float32
bf16 = jnp.bfloat16
epsilon = 1e-05

SPLITS = {256: (8, 8, 4), 4: (2, 2, 1)}
MAIN_ROWS = 512
LATE_ROWS = 128
VEC = 448


def part_sum(x):
    n, lanes = x.shape
    return jnp.sum(x.reshape(n // 8, 8, lanes), axis=0)


def both(v8):
    v8 = v8 + pltpu.roll(v8, 64, 1)
    return jnp.sum(v8, axis=0, keepdims=True)


def total(v8):
    return jnp.sum(v8, axis=0, keepdims=True)


def gates(v):
    half = 0.5 * v
    t = jnp.tanh(half)
    act = half * t + half
    sig = 0.5 * t + 0.5
    slope = sig + act * (0.5 - 0.5 * t)
    return act, slope


def dotf(a, b):
    return jnp.dot(a, b, preferred_element_type=f32)


def dot_t(a, b):
    return lax.dot_general(a, b, (((1,), (1,)), ((), ())), preferred_element_type=f32)


def kernel(
    splits,
    images, wr, wd, we, g1, s1, g2, s2, g3, s3, cot,
    result, gimages, o_reduce, o_dilated, o_expand, o_vec,
    img_v, cot_v, res_v, gi_v,
    w_in, w_out, w_fwd, w_bwd,
    pre1, slope1, pre2, slope2, act2, x3, e3, dh3, grad2, grad1, dh1,
    edge1, edge2, halo1, halo2, wide1, wide2,
    xbuf,
    main_a, main_ra, main_b, main_rb, main_c, main_gb, main_ga,
    late_a, late_ra, late_b, late_c, late_ga,
    in_sem, out_sem, hs_sem, hr_sem, xs_sem, xr_sem, send_sem, recv_sem,
):
    ends, ys, highs = splits
    spaces = lax.axis_size("space")
    zs = highs * spaces
    d = lax.axis_index("dp")
    s = lax.axis_index("space")
    end = lax.rem(d, ends)
    high = lax.rem(lax.div(d, ends), highs)
    y = lax.div(d, ends * highs)
    z = high * spaces + s
    cols = 288
    local = 2304.0
    count = local * spaces

    def id_a(k):
        return (d - end + k, s)

    def id_b(k):
        return (d + (k - y) * (ends * highs), s)

    def id_c(k):
        kh = lax.div(k, spaces)
        return (d + (kh - high) * ends, lax.rem(k, spaces))

    groups = {"a": (ends, end, id_a), "b": (ys, y, id_b), "c": (zs, z, id_c)}

    in_copies = []
    for r in range(8):
        c = pltpu.make_async_copy(images.at[0, r], img_v.at[r % 2, r // 2], in_sem.at[r])
        c.start()
        in_copies.append(c)
    cot_copy = pltpu.make_async_copy(cot.at[0], cot_v, in_sem.at[8])
    cot_copy.start()

    barrier = pltpu.get_barrier_semaphore()
    partners = 0
    for name in "abc":
        n, me, ident = groups[name]
        for k in range(1, n):
            pl.semaphore_signal(
                barrier, inc=1, device_id=ident(lax.rem(me + k, n)), device_id_type=MESH
            )
            partners += 1

    zero_in = jnp.zeros((256, 64), bf16)
    w_in[0] = jnp.concatenate([wr[...], zero_in], axis=1)
    w_in[1] = jnp.concatenate([zero_in, wr[...]], axis=1)
    zero_out = jnp.zeros((64, 256), bf16)
    w_out[0] = jnp.concatenate([we[...], zero_out], axis=0)
    w_out[1] = jnp.concatenate([zero_out, we[...]], axis=0)
    zero_mid = jnp.zeros((64, 64), bf16)
    for a in range(3):
        for b in range(3):
            w = wd[a, b]
            diag = jnp.concatenate(
                [
                    jnp.concatenate([w, zero_mid], axis=1),
                    jnp.concatenate([zero_mid, w], axis=1),
                ],
                axis=0,
            )
            w_fwd[a, b * 128 : (b + 1) * 128, :] = diag
            w_bwd[2 - a, :, (2 - b) * 128 : (3 - b) * 128] = diag

    @pl.when(s == 0)
    def _():
        wide1[0:cols, :] = jnp.zeros((cols, 384), bf16)
        wide2[0:cols, :] = jnp.zeros((cols, 384), bf16)

    @pl.when(s == spaces - 1)
    def _():
        wide1[5 * cols : 6 * cols, :] = jnp.zeros((cols, 384), bf16)
        wide2[5 * cols : 6 * cols, :] = jnp.zeros((cols, 384), bf16)

    def twice(ref):
        v = ref[...]
        return jnp.concatenate([v, v], axis=1)

    def send_stats(idx, first, second):
        lanes = first.shape[1]
        xbuf[idx, s, 0:1, 0:lanes] = first
        xbuf[idx, s, 1:2, 0:lanes] = second
        for k in range(1, 3):
            pltpu.make_async_remote_copy(
                src_ref=xbuf.at[idx, s],
                dst_ref=xbuf.at[idx, s],
                send_sem=xs_sem.at[idx, k - 1],
                recv_sem=xr_sem.at[idx, s],
                device_id=(d, lax.rem(s + k, spaces)),
                device_id_type=MESH,
            ).start()

    def wait_stats(idx, lanes):
        for k in range(1, 3):
            f = lax.rem(s + k, spaces)
            pltpu.make_async_remote_copy(
                src_ref=xbuf.at[idx, f],
                dst_ref=xbuf.at[idx, f],
                send_sem=xs_sem.at[idx, k - 1],
                recv_sem=xr_sem.at[idx, f],
                device_id=(d, f),
                device_id_type=MESH,
            ).wait_recv()
        firsts = [xbuf[idx, j, 0:1, 0:lanes] for j in range(3)]
        seconds = [xbuf[idx, j, 1:2, 0:lanes] for j in range(3)]
        return firsts, seconds

    def moments(idx, lanes):
        means, squares = wait_stats(idx, lanes)
        mu = (means[0] + means[1] + means[2]) * (1.0 / 3.0)
        spread = sum((m - mu) * (m - mu) for m in means)
        var = (squares[0] + squares[1] + squares[2] + local * spread) * (1.0 / count)
        return mu, lax.rsqrt(var + epsilon)

    def sums(idx, lanes):
        firsts, seconds = wait_stats(idx, lanes)
        return firsts[0] + firsts[1] + firsts[2], seconds[0] + seconds[1] + seconds[2]

    def halo(edge, halos, which):
        @pl.when(s > 0)
        def _():
            pltpu.make_async_remote_copy(
                src_ref=edge.at[0], dst_ref=halos.at[1],
                send_sem=hs_sem.at[which, 0], recv_sem=hr_sem.at[which, 1],
                device_id=(d, s - 1), device_id_type=MESH,
            ).start()

        @pl.when(s < spaces - 1)
        def _():
            pltpu.make_async_remote_copy(
                src_ref=edge.at[1], dst_ref=halos.at[0],
                send_sem=hs_sem.at[which, 1], recv_sem=hr_sem.at[which, 0],
                device_id=(d, s + 1), device_id_type=MESH,
            ).start()

    def widen(wide, pair, x):
        at = pair * cols
        spot = lax.broadcasted_iota(jnp.int32, (cols, 128), 0)
        before = jnp.where(spot >= 2, pltpu.roll(x, 2, 0), 0.0)
        after = jnp.where(spot < cols - 2, pltpu.roll(x, cols - 2, 0), 0.0)
        wide[at : at + cols, 0:128] = before.astype(bf16)
        wide[at : at + cols, 128:256] = x.astype(bf16)
        wide[at : at + cols, 256:384] = after.astype(bf16)

    def take_halo(edge, halos, wide, which):
        @pl.when(s > 0)
        def _():
            pltpu.make_async_remote_copy(
                src_ref=edge.at[1], dst_ref=halos.at[0],
                send_sem=hs_sem.at[which, 0], recv_sem=hr_sem.at[which, 0],
                device_id=(d, s - 1), device_id_type=MESH,
            ).wait_recv()
            widen(wide, 0, halos[0].astype(f32))

        @pl.when(s < spaces - 1)
        def _():
            pltpu.make_async_remote_copy(
                src_ref=edge.at[0], dst_ref=halos.at[1],
                send_sem=hs_sem.at[which, 1], recv_sem=hr_sem.at[which, 1],
                device_id=(d, s + 1), device_id_type=MESH,
            ).wait_recv()
            widen(wide, 5, halos[1].astype(f32))

    def end_halo(edge, halos, which):
        @pl.when(s > 0)
        def _():
            pltpu.make_async_remote_copy(
                src_ref=edge.at[0], dst_ref=halos.at[1],
                send_sem=hs_sem.at[which, 0], recv_sem=hr_sem.at[which, 1],
                device_id=(d, s - 1), device_id_type=MESH,
            ).wait_send()

        @pl.when(s < spaces - 1)
        def _():
            pltpu.make_async_remote_copy(
                src_ref=edge.at[1], dst_ref=halos.at[0],
                send_sem=hs_sem.at[which, 1], recv_sem=hr_sem.at[which, 0],
                device_id=(d, s + 1), device_id_type=MESH,
            ).wait_send()

    def conv_fwd(pair, n):
        acc = dotf(wide1[pair * cols : (pair + n) * cols, :], w_fwd[0])
        for a in range(1, 3):
            acc += dotf(wide1[(pair + a) * cols : (pair + a + n) * cols, :], w_fwd[a])
        return acc

    def conv_bwd(pair, n):
        acc = dot_t(wide2[pair * cols : (pair + n) * cols, :], w_bwd[0])
        for a in range(1, 3):
            acc += dot_t(wide2[(pair + a) * cols : (pair + a + n) * cols, :], w_bwd[a])
        return acc

    def local_moments(idx, pre, acc):
        mean = both(acc) * (1.0 / local)
        sq = jnp.zeros((8, 128), f32)
        for p in range(4):
            c = pre[p] - mean
            sq += part_sum(c * c)
        send_stats(idx, mean, both(sq))

    def copy_to(stage, name, src, dst, k):
        n, me, ident = groups[name]
        t = lax.rem(me + k, n)
        return pltpu.make_async_remote_copy(
            src_ref=src(t), dst_ref=dst(me),
            send_sem=send_sem.at[stage, k], recv_sem=recv_sem.at[stage, me],
            device_id=ident(t), device_id_type=MESH,
        )

    def spread_out(stage, name, src, dst):
        for k in range(1, groups[name][0]):
            copy_to(stage, name, src, dst, k).start()

    def collect(stage, name, src, dst):
        n, me, ident = groups[name]
        for k in range(1, n):
            f = lax.rem(me + k, n)
            pltpu.make_async_remote_copy(
                src_ref=src(f), dst_ref=dst(f),
                send_sem=send_sem.at[stage, k], recv_sem=recv_sem.at[stage, f],
                device_id=ident(f), device_id_type=MESH,
            ).wait_recv()

    def added(ref, n):
        acc = ref[0].astype(f32)
        for k in range(1, n):
            acc += ref[k].astype(f32)
        return acc

    acc = jnp.zeros((8, 128), f32)
    for p in range(4):
        in_copies[2 * p].wait()
        in_copies[2 * p + 1].wait()
        v = dotf(img_v[0, p], w_in[0]) + dotf(img_v[1, p], w_in[1])
        pre1[p] = v
        acc += part_sum(v)
    gain1, shift1 = twice(g1), twice(s1)
    gain2, shift2 = twice(g2), twice(s2)
    pl.semaphore_wait(barrier, partners)
    local_moments(0, pre1, acc)
    mu, istd1 = moments(0, 128)
    for p in (0, 3, 1, 2):
        xhat = (pre1[p] - mu) * istd1
        act, slope = gates(gain1 * xhat + shift1)
        pre1[p] = xhat
        slope1[p] = slope
        if p == 0:
            edge1[0] = act.astype(bf16)
        if p == 3:
            edge1[1] = act.astype(bf16)
            halo(edge1, halo1, 0)
        widen(wide1, p + 1, act)

    v = conv_fwd(1, 2)
    pre2[1] = v[0:cols]
    pre2[2] = v[cols : 2 * cols]
    acc = part_sum(v)
    take_halo(edge1, halo1, wide1, 0)
    for p in (0, 3):
        v = conv_fwd(p, 1)
        pre2[p] = v
        acc += part_sum(v)
    local_moments(1, pre2, acc)
    mu, istd2 = moments(1, 128)
    acc3 = jnp.zeros((8, 256), f32)
    for p in range(4):
        xhat = (pre2[p] - mu) * istd2
        act, slope = gates(gain2 * xhat + shift2)
        pre2[p] = xhat
        slope2[p] = slope
        act = act.astype(bf16)
        act2[p] = act
        for q in range(2):
            v = dotf(act, w_out[q])
            x3[2 * p + q] = v
            acc3 += part_sum(v)

    mean = total(acc3) * (1.0 / local)

    def square(r, acc):
        c = x3[r] - mean
        return acc + part_sum(c * c)

    sq = lax.fori_loop(0, 8, square, jnp.zeros((8, 256), f32))
    send_stats(2, mean, total(sq))
    cot_copy.wait()
    gain3, shift3 = g3[...], s3[...]
    mu, istd3 = moments(2, 256)

    def third(r, carry):
        sd, sx = carry
        p, q = lax.div(r, 2), lax.rem(r, 2)
        xhat = (x3[r] - mu) * istd3
        act, slope = gates(gain3 * xhat + shift3 + img_v[q, p].astype(f32))
        res_v[r] = act.astype(bf16)
        e = cot_v[r].astype(f32) * slope
        x3[r] = xhat
        e3[r] = e
        pltpu.make_async_copy(res_v.at[r], result.at[0, r], out_sem.at[0, r]).start()
        return sd + part_sum(e), sx + part_sum(e * xhat)

    zero8 = jnp.zeros((8, 256), f32)
    sd, sx = lax.fori_loop(0, 8, third, (zero8, zero8))
    sd3, sx3 = total(sd), total(sx)
    send_stats(3, sd3, sx3)
    sd, sx = sums(3, 256)
    k0 = gain3 * istd3
    k1 = k0 * sd * (1.0 / count)
    k2 = k0 * sx * (1.0 / count)
    sd_acc = jnp.zeros((8, 128), f32)
    sx_acc = jnp.zeros((8, 128), f32)
    for p in range(4):
        for q in range(2):
            r = 2 * p + q
            dh3[q, p] = (k0 * e3[r] - k1 - k2 * x3[r]).astype(bf16)
        back = dot_t(dh3[0, p], w_out[0]) + dot_t(dh3[1, p], w_out[1])
        g = back * slope2[p]
        grad2[p] = g
        sd_acc += part_sum(g)
        sx_acc += part_sum(g * pre2[p])
    sd2, sx2 = both(sd_acc), both(sx_acc)
    send_stats(4, sd2, sx2)
    rows = 4 * cols
    act_t = act2[...].reshape(rows, 128).T
    expand = dotf(act_t[0:64], dh3[0].reshape(rows, 256)) + dotf(
        act_t[64:128], dh3[1].reshape(rows, 256)
    )
    sd, sx = sums(4, 128)
    k0 = gain2 * istd2
    k1 = k0 * sd * (1.0 / count)
    k2 = k0 * sx * (1.0 / count)
    pieces = []
    for p in (0, 3, 1, 2):
        dh = k0 * grad2[p] - k1 - k2 * pre2[p]
        if p == 0:
            edge2[0] = dh.astype(bf16)
        if p == 3:
            edge2[1] = dh.astype(bf16)
            halo(edge2, halo2, 1)
        widen(wide2, p + 1, dh)

    sd_acc = jnp.zeros((8, 128), f32)
    sx_acc = jnp.zeros((8, 128), f32)

    def first_back(p, v, sd_acc, sx_acc):
        g = v * slope1[p]
        grad1[p] = g
        return sd_acc + part_sum(g), sx_acc + part_sum(g * pre1[p])

    v = conv_bwd(1, 2)
    sd_acc, sx_acc = first_back(1, v[0:cols], sd_acc, sx_acc)
    sd_acc, sx_acc = first_back(2, v[cols : 2 * cols], sd_acc, sx_acc)
    take_halo(edge2, halo2, wide2, 1)
    for p in (0, 3):
        sd_acc, sx_acc = first_back(p, conv_bwd(p, 1), sd_acc, sx_acc)
    sd1, sx1 = both(sd_acc), both(sx_acc)
    send_stats(5, sd1, sx1)

    main_rows = MAIN_ROWS // ends
    late_rows = LATE_ROWS // ends

    def put_main(row, block):
        n = block.shape[0]
        done = 0
        while done < n:
            piece, off = divmod(row + done, main_rows)
            size = min(n - done, main_rows - off)
            main_a[piece, off : off + size, :] = block[done : done + size].astype(bf16)
            done += size

    dh2_t = wide2[cols : cols + rows, 128:256].T
    low = lax.broadcasted_iota(jnp.int32, (64, 128), 1) < 64
    taps = []
    for a in range(3):
        g = dotf(dh2_t, wide1[a * cols : a * cols + rows, :])
        for b in range(3):
            g0 = g[0:64, b * 128 : (b + 1) * 128]
            g1v = g[64:128, b * 128 : (b + 1) * 128]
            if (3 * a + b) % 2 == 0:
                taps.append(g0 + pltpu.roll(g1v, 64, 1))
            else:
                taps.append(pltpu.roll(g0, 64, 1) + g1v)
    taps.append(jnp.zeros((64, 128), f32))
    for u in range(5):
        put_main(64 * u, jnp.where(low, taps[2 * u], taps[2 * u + 1]))
    put_main(320, expand[:, 0:128])
    put_main(384, expand[:, 128:256])
    low1 = lax.broadcasted_iota(jnp.int32, (1, 128), 1) < 64
    vec = jnp.concatenate(
        [
            sx3[:, 0:128], sx3[:, 128:256], sd3[:, 0:128], sd3[:, 128:256],
            jnp.where(low1, sx2, sd2), jnp.where(low1, sx1, sd1),
            jnp.zeros((2, 128), f32),
        ],
        axis=0,
    )
    vec_high = vec.astype(bf16)
    vec_low = vec - vec_high.astype(f32)
    put_main(VEC, jnp.concatenate([vec_high.astype(f32), vec_low], axis=0))
    put_main(VEC + 16, jnp.zeros((48, 128), f32))
    main_ra[end] = main_a[end]

    a_src, a_dst = (lambda t: main_a.at[t]), (lambda me: main_ra.at[me])
    spread_out(0, "a", a_src, a_dst)

    sd, sx = sums(5, 128)
    k0 = gain1 * istd1
    k1 = k0 * sd * (1.0 / count)
    k2 = k0 * sx * (1.0 / count)
    for p in range(4):
        dh1[p] = (k0 * grad1[p] - k1 - k2 * pre1[p]).astype(bf16)
    dh1_t = dh1[...].reshape(rows, 128).T
    reduce = dotf(dh1_t[0:64], img_v[0].reshape(rows, 256)) + dotf(
        dh1_t[64:128], img_v[1].reshape(rows, 256)
    )
    for h in range(2):
        for piece in range(ends):
            lo, hi = piece * late_rows, (piece + 1) * late_rows
            a, b = max(lo, 64 * h), min(hi, 64 * h + 64)
            if a < b:
                late_a[piece, a - lo : b - lo, :] = reduce[
                    a - 64 * h : b - 64 * h, 128 * h : 128 * h + 128
                ].astype(bf16)
    late_ra[end] = late_a[end]
    la_src, la_dst = (lambda t: late_a.at[t]), (lambda me: late_ra.at[me])
    spread_out(5, "a", la_src, la_dst)

    def last(p, carry):
        dh = dh1[p]
        for q in range(2):
            r = 2 * p + q
            gi_v[r] = (dot_t(dh, w_in[q]) + e3[r]).astype(bf16)
            pltpu.make_async_copy(gi_v.at[r], gimages.at[0, r], out_sem.at[1, r]).start()
        return carry

    collect(0, "a", a_src, a_dst)
    part = added(main_ra, ends)
    sub = main_rows // ys
    for k in range(ys):
        main_b[k] = part[k * sub : (k + 1) * sub]
    main_rb[y] = main_b[y]
    b_src, b_dst = (lambda t: main_b.at[t]), (lambda me: main_rb.at[me])
    spread_out(1, "b", b_src, b_dst)

    lax.fori_loop(0, 2, last, 0)

    collect(5, "a", la_src, la_dst)
    late_b[y] = added(late_ra, ends).astype(bf16)
    lb_src, lb_dst = (lambda t: late_b.at[y]), (lambda me: late_b.at[me])
    spread_out(6, "b", lb_src, lb_dst)

    collect(1, "b", b_src, b_dst)
    main_c[z] = added(main_rb, ys)
    c_src, c_dst = (lambda t: main_c.at[z]), (lambda me: main_c.at[me])
    spread_out(2, "c", c_src, c_dst)

    lax.fori_loop(2, 4, last, 0)

    collect(6, "b", lb_src, lb_dst)
    late_c[z] = added(late_b, ys).astype(bf16)
    lc_src, lc_dst = (lambda t: late_c.at[z]), (lambda me: late_c.at[me])
    spread_out(7, "c", lc_src, lc_dst)

    collect(2, "c", c_src, c_dst)
    main_gb[y] = added(main_c, zs)
    gb_src, gb_dst = (lambda t: main_gb.at[y]), (lambda me: main_gb.at[me])
    spread_out(3, "b", gb_src, gb_dst)

    collect(7, "c", lc_src, lc_dst)
    late_ga[end] = added(late_c, zs).astype(bf16)
    lg_src, lg_dst = (lambda t: late_ga.at[end]), (lambda me: late_ga.at[me])
    spread_out(8, "a", lg_src, lg_dst)

    collect(3, "b", gb_src, gb_dst)
    whole = main_gb[...].reshape(main_rows, 128)
    main_ga[end] = whole.astype(bf16)

    @pl.when(end == VEC // main_rows)
    def _():
        at = VEC % main_rows
        v = whole[at : at + 8] + whole[at + 8 : at + 16]
        v_high = v.astype(bf16).astype(f32)
        main_ga[end, at : at + 16, :] = jnp.concatenate([v_high, v - v_high], axis=0).astype(bf16)

    ga_src, ga_dst = (lambda t: main_ga.at[end]), (lambda me: main_ga.at[me])
    spread_out(4, "a", ga_src, ga_dst)

    scale = 1.0 / lax.axis_size("dp")
    collect(8, "a", lg_src, lg_dst)
    late = late_ga[...].reshape(LATE_ROWS, 128).astype(f32).T * scale
    o_reduce[0:128, :] = late[:, 0:64]
    o_reduce[128:256, :] = late[:, 64:128]

    collect(4, "a", ga_src, ga_dst)
    main = main_ga[...].reshape(MAIN_ROWS, 128).astype(f32) * scale
    for u in range(5):
        pair = main[64 * u : 64 * u + 64]
        pair = jnp.concatenate([pair, pair], axis=0).T
        o_dilated[2 * u] = pair[0:64, 0:64]
        if u < 4:
            o_dilated[2 * u + 1] = pair[64:128, 0:64]
    o_expand[:, 0:128] = main[320:384]
    o_expand[:, 128:256] = main[384:448]
    o_vec[...] = main[VEC : VEC + 8] + main[VEC + 8 : VEC + 16]

    for idx in range(6):
        for k in range(1, 3):
            pltpu.make_async_remote_copy(
                src_ref=xbuf.at[idx, s], dst_ref=xbuf.at[idx, s],
                send_sem=xs_sem.at[idx, k - 1], recv_sem=xr_sem.at[idx, s],
                device_id=(d, lax.rem(s + k, spaces)), device_id_type=MESH,
            ).wait_send()
    end_halo(edge1, halo1, 0)
    end_halo(edge2, halo2, 1)
    for stage, name, src, dst in (
        (0, "a", a_src, a_dst), (1, "b", b_src, b_dst), (2, "c", c_src, c_dst),
        (3, "b", gb_src, gb_dst), (4, "a", ga_src, ga_dst), (5, "a", la_src, la_dst),
        (6, "b", lb_src, lb_dst), (7, "c", lc_src, lc_dst), (8, "a", lg_src, lg_dst),
    ):
        for k in range(1, groups[name][0]):
            copy_to(stage, name, src, dst, k).wait_send()
    for r in range(8):
        pltpu.make_async_copy(res_v.at[r], result.at[0, r], out_sem.at[0, r]).wait()
        pltpu.make_async_copy(gi_v.at[r], gimages.at[0, r], out_sem.at[1, r]).wait()


def solution(mesh):
    splits = SPLITS[mesh.shape["dp"]]
    ends, ys, highs = splits
    zs = highs * mesh.shape["space"]
    main_rows = MAIN_ROWS // ends
    late_rows = LATE_ROWS // ends
    sub = main_rows // ys

    def shards(images, wr, wd, we, g1, s1, g2, s2, g3, s3, cot):
        vmem = pl.BlockSpec(memory_space=pltpu.VMEM)
        hbm = pl.BlockSpec(memory_space=pl.ANY)
        big = jax.ShapeDtypeStruct(images.shape, bf16)
        maps = lambda: pltpu.VMEM((4, 288, 128), f32)
        outs = pl.pallas_call(
            functools.partial(kernel, splits),
            out_shape=(
                big, big,
                jax.ShapeDtypeStruct((256, 64), f32),
                jax.ShapeDtypeStruct((9, 64, 64), f32),
                jax.ShapeDtypeStruct((64, 256), f32),
                jax.ShapeDtypeStruct((8, 128), f32),
            ),
            in_specs=[hbm] + [vmem] * 9 + [hbm],
            out_specs=(hbm, hbm, vmem, vmem, vmem, vmem),
            scratch_shapes=[
                pltpu.VMEM((2, 4, 288, 256), bf16),
                pltpu.VMEM((8, 288, 256), bf16),
                pltpu.VMEM((8, 288, 256), bf16),
                pltpu.VMEM((8, 288, 256), bf16),
                pltpu.VMEM((2, 256, 128), bf16),
                pltpu.VMEM((2, 128, 256), bf16),
                pltpu.VMEM((3, 384, 128), bf16),
                pltpu.VMEM((3, 128, 384), bf16),
                maps(), maps(), maps(), maps(),
                pltpu.VMEM((4, 288, 128), bf16),
                pltpu.VMEM((8, 288, 256), f32),
                pltpu.VMEM((8, 288, 256), f32),
                pltpu.VMEM((2, 4, 288, 256), bf16),
                maps(), maps(),
                pltpu.VMEM((4, 288, 128), bf16),
                pltpu.VMEM((2, 288, 128), bf16),
                pltpu.VMEM((2, 288, 128), bf16),
                pltpu.VMEM((2, 288, 128), bf16),
                pltpu.VMEM((2, 288, 128), bf16),
                pltpu.VMEM((6 * 288, 384), bf16),
                pltpu.VMEM((6 * 288, 384), bf16),
                pltpu.VMEM((6, 3, 8, 256), f32),
                pltpu.VMEM((ends, main_rows, 128), bf16),
                pltpu.VMEM((ends, main_rows, 128), bf16),
                pltpu.VMEM((ys, sub, 128), f32),
                pltpu.VMEM((ys, sub, 128), f32),
                pltpu.VMEM((zs, sub, 128), f32),
                pltpu.VMEM((ys, sub, 128), f32),
                pltpu.VMEM((ends, main_rows, 128), bf16),
                pltpu.VMEM((ends, late_rows, 128), bf16),
                pltpu.VMEM((ends, late_rows, 128), bf16),
                pltpu.VMEM((ys, late_rows, 128), bf16),
                pltpu.VMEM((zs, late_rows, 128), bf16),
                pltpu.VMEM((ends, late_rows, 128), bf16),
                pltpu.SemaphoreType.DMA((9,)),
                pltpu.SemaphoreType.DMA((2, 8)),
                pltpu.SemaphoreType.DMA((2, 2)),
                pltpu.SemaphoreType.DMA((2, 2)),
                pltpu.SemaphoreType.DMA((6, 2)),
                pltpu.SemaphoreType.DMA((6, 3)),
                pltpu.SemaphoreType.DMA((9, 12)),
                pltpu.SemaphoreType.DMA((9, 12)),
            ],
            compiler_params=pltpu.CompilerParams(
                collective_id=0, has_side_effects=True, vmem_limit_bytes=48 * 1024 * 1024
            ),
        )(
            images, wr, wd, we,
            g1.reshape(1, 64), s1.reshape(1, 64), g2.reshape(1, 64), s2.reshape(1, 64),
            g3.reshape(1, 256), s3.reshape(1, 256), cot,
        )
        res, gi, g_reduce, g_dilated, g_expand, vec = outs
        return (
            res, gi, g_reduce, g_dilated.reshape(3, 3, 64, 64), g_expand,
            vec[5, 0:64], vec[5, 64:128], vec[4, 0:64], vec[4, 64:128],
            vec[0:2].reshape(256), vec[2:4].reshape(256),
        )

    placed = (P("dp", "space", None, None),) + (P(),) * 9 + (P("dp", "space", None, None),)
    return jax.shard_map(
        shards,
        mesh=mesh,
        in_specs=placed,
        out_specs=(P("dp", "space", None, None),) * 2 + (P(),) * 9,
        check_vma=False,
    )
```

```python
import functools

import jax
import jax.numpy as jnp
from jax import lax
from jax.experimental import pallas as pl
from jax.experimental.pallas import tpu as pltpu
from jax.sharding import PartitionSpec as P

MESH = pl.DeviceIdType.MESH
f32 = jnp.float32
bf16 = jnp.bfloat16
epsilon = 1e-05

SPLITS = {256: (8, 8, 4), 4: (2, 2, 1)}
MAIN_ROWS = 512
LATE_ROWS = 128
VEC = 448


def part_sum(x):
    n, lanes = x.shape
    return jnp.sum(x.reshape(n // 8, 8, lanes), axis=0)


def both(v8):
    v8 = v8 + pltpu.roll(v8, 64, 1)
    return jnp.sum(v8, axis=0, keepdims=True)


def total(v8):
    return jnp.sum(v8, axis=0, keepdims=True)


def gates(v):
    half = 0.5 * v
    t = jnp.tanh(half)
    act = half * t + half
    sig = 0.5 * t + 0.5
    slope = sig + act * (0.5 - 0.5 * t)
    return act, slope


def dotf(a, b):
    return jnp.dot(a, b, preferred_element_type=f32)


def dot_t(a, b):
    return lax.dot_general(a, b, (((1,), (1,)), ((), ())), preferred_element_type=f32)


def kernel(
    splits,
    images, wr_h, wd_h, we_h, g1_h, s1_h, g2_h, s2_h, g3_h, s3_h, cot,
    result, gimages, h_reduce, h_dilated, h_expand, h_vec,
    res_v, gi_v, o_reduce, o_dilated, o_expand, o_vec, img_v, cot_v, wr, wd, we, g1, s1, g2, s2, g3, s3,
    w_in, w_out, w_fwd, w_bwd,
    pre1, slope1, pre2, slope2, act2, x3, e3, dh3, grad2, grad1, dh1,
    edge1, edge2, halo1, halo2, wide1, wide2,
    xbuf, cross,
    main_a, main_ra, main_b, main_rb, main_c, main_gb, main_ga,
    late_a, late_ra, late_b, late_c, late_ga,
    in_sem, out_sem, hs_sem, hr_sem, xs_sem, xr_sem, cs_sem, cr_sem, send_sem, recv_sem,
):
    ends, ys, highs = splits
    spaces = lax.axis_size("space")
    zs = highs * spaces
    d = lax.axis_index("dp")
    s = lax.axis_index("space")
    end = lax.rem(d, ends)
    high = lax.rem(lax.div(d, ends), highs)
    y = lax.div(d, ends * highs)
    z = high * spaces + s
    cols = 288
    local = 2304.0
    count = local * spaces

    def id_a(k):
        return (d - end + k, s)

    def id_b(k):
        return (d + (k - y) * (ends * highs), s)

    def id_c(k):
        kh = lax.div(k, spaces)
        return (d + (kh - high) * ends, lax.rem(k, spaces))

    groups = {"a": (ends, end, id_a), "b": (ys, y, id_b), "c": (zs, z, id_c)}

    in_copies = []
    for r in range(8):
        c = pltpu.make_async_copy(images.at[0, r], img_v.at[r % 2, r // 2], in_sem.at[r])
        c.start()
        in_copies.append(c)
    small = []
    pairs = (
        (wr_h, wr), (wd_h, wd), (we_h, we), (g1_h, g1), (s1_h, s1),
        (g2_h, g2), (s2_h, s2), (g3_h, g3), (s3_h, s3),
    )
    for k, (src, dst) in enumerate(pairs):
        c = pltpu.make_async_copy(src, dst, in_sem.at[9 + k])
        c.start()
        small.append(c)
    cot_copy = pltpu.make_async_copy(cot.at[0], cot_v, in_sem.at[8])
    cot_copy.start()

    barrier = pltpu.get_barrier_semaphore()
    partners = 0
    for name in "cba":
        n, me, ident = groups[name]
        for k in sorted(range(1, n), key=lambda k: -min(k, n - k)):
            pl.semaphore_signal(
                barrier, inc=1, device_id=ident(lax.rem(me + k, n)), device_id_type=MESH
            )
            partners += 1

    for c in small:
        c.wait()
    zero_out = jnp.zeros((64, 256), bf16)
    w_in[0] = jnp.concatenate([wr[...], zero_out], axis=0)
    w_in[1] = jnp.concatenate([zero_out, wr[...]], axis=0)
    w_out[0] = jnp.concatenate([we[...], zero_out], axis=0)
    w_out[1] = jnp.concatenate([zero_out, we[...]], axis=0)
    zero_mid = jnp.zeros((64, 64), bf16)
    for a in range(3):
        for b in range(3):
            w = wd[a, b]
            diag = jnp.concatenate(
                [
                    jnp.concatenate([w, zero_mid], axis=1),
                    jnp.concatenate([zero_mid, w], axis=1),
                ],
                axis=0,
            )
            w_fwd[a, b * 128 : (b + 1) * 128, :] = diag
            w_bwd[2 - a, :, (2 - b) * 128 : (3 - b) * 128] = diag

    @pl.when(s == 0)
    def _():
        wide1[0:cols, :] = jnp.zeros((cols, 384), bf16)
        wide2[0:cols, :] = jnp.zeros((cols, 384), bf16)

    @pl.when(s == spaces - 1)
    def _():
        wide1[5 * cols : 6 * cols, :] = jnp.zeros((cols, 384), bf16)
        wide2[5 * cols : 6 * cols, :] = jnp.zeros((cols, 384), bf16)

    def twice(ref):
        v = ref[...]
        return jnp.concatenate([v, v], axis=1)

    def send_stats(idx, first, second):
        lanes = first.shape[1]
        xbuf[idx, s, 0:1, 0:lanes] = first
        xbuf[idx, s, 1:2, 0:lanes] = second
        for k in range(1, 3):
            pltpu.make_async_remote_copy(
                src_ref=xbuf.at[idx, s],
                dst_ref=xbuf.at[idx, s],
                send_sem=xs_sem.at[idx, k - 1],
                recv_sem=xr_sem.at[idx, s],
                device_id=(d, lax.rem(s + k, spaces)),
                device_id_type=MESH,
            ).start()

    def wait_stats(idx, lanes):
        for k in range(1, 3):
            f = lax.rem(s + k, spaces)
            pltpu.make_async_remote_copy(
                src_ref=xbuf.at[idx, f],
                dst_ref=xbuf.at[idx, f],
                send_sem=xs_sem.at[idx, k - 1],
                recv_sem=xr_sem.at[idx, f],
                device_id=(d, f),
                device_id_type=MESH,
            ).wait_recv()
        firsts = [xbuf[idx, j, 0:1, 0:lanes] for j in range(3)]
        seconds = [xbuf[idx, j, 1:2, 0:lanes] for j in range(3)]
        return firsts, seconds

    def moments(idx, lanes):
        means, squares = wait_stats(idx, lanes)
        mu = (means[0] + means[1] + means[2]) * (1.0 / 3.0)
        spread = sum((m - mu) * (m - mu) for m in means)
        var = (squares[0] + squares[1] + squares[2] + local * spread) * (1.0 / count)
        return mu, lax.rsqrt(var + epsilon)

    def sums(idx, lanes):
        firsts, seconds = wait_stats(idx, lanes)
        return firsts[0] + firsts[1] + firsts[2], seconds[0] + seconds[1] + seconds[2]

    def halo(edge, halos, which):
        @pl.when(s > 0)
        def _():
            pltpu.make_async_remote_copy(
                src_ref=edge.at[0], dst_ref=halos.at[1],
                send_sem=hs_sem.at[which, 0], recv_sem=hr_sem.at[which, 1],
                device_id=(d, s - 1), device_id_type=MESH,
            ).start()

        @pl.when(s < spaces - 1)
        def _():
            pltpu.make_async_remote_copy(
                src_ref=edge.at[1], dst_ref=halos.at[0],
                send_sem=hs_sem.at[which, 1], recv_sem=hr_sem.at[which, 0],
                device_id=(d, s + 1), device_id_type=MESH,
            ).start()

    def widen(wide, pair, x):
        at = pair * cols
        spot = lax.broadcasted_iota(jnp.int32, (cols, 128), 0)
        before = jnp.where(spot >= 2, pltpu.roll(x, 2, 0), 0.0)
        after = jnp.where(spot < cols - 2, pltpu.roll(x, cols - 2, 0), 0.0)
        wide[at : at + cols, 0:128] = before.astype(bf16)
        wide[at : at + cols, 128:256] = x.astype(bf16)
        wide[at : at + cols, 256:384] = after.astype(bf16)

    def take_halo(edge, halos, wide, which, finish):
        @pl.when(s > 0)
        def _():
            pltpu.make_async_remote_copy(
                src_ref=edge.at[1], dst_ref=halos.at[0],
                send_sem=hs_sem.at[which, 0], recv_sem=hr_sem.at[which, 0],
                device_id=(d, s - 1), device_id_type=MESH,
            ).wait_recv()
            widen(wide, 0, finish(halos[0].astype(f32), s - 1))

        @pl.when(s < spaces - 1)
        def _():
            pltpu.make_async_remote_copy(
                src_ref=edge.at[0], dst_ref=halos.at[1],
                send_sem=hs_sem.at[which, 1], recv_sem=hr_sem.at[which, 1],
                device_id=(d, s + 1), device_id_type=MESH,
            ).wait_recv()
            widen(wide, 5, finish(halos[1].astype(f32), s + 1))

    def end_halo(edge, halos, which):
        @pl.when(s > 0)
        def _():
            pltpu.make_async_remote_copy(
                src_ref=edge.at[0], dst_ref=halos.at[1],
                send_sem=hs_sem.at[which, 0], recv_sem=hr_sem.at[which, 1],
                device_id=(d, s - 1), device_id_type=MESH,
            ).wait_send()

        @pl.when(s < spaces - 1)
        def _():
            pltpu.make_async_remote_copy(
                src_ref=edge.at[1], dst_ref=halos.at[0],
                send_sem=hs_sem.at[which, 1], recv_sem=hr_sem.at[which, 0],
                device_id=(d, s + 1), device_id_type=MESH,
            ).wait_send()

    def conv_fwd(pair, n):
        acc = dotf(wide1[pair * cols : (pair + n) * cols, :], w_fwd[0])
        for a in range(1, 3):
            acc += dotf(wide1[(pair + a) * cols : (pair + a + n) * cols, :], w_fwd[a])
        return acc

    def conv_bwd(pair, n):
        acc = dot_t(wide2[pair * cols : (pair + n) * cols, :], w_bwd[0])
        for a in range(1, 3):
            acc += dot_t(wide2[(pair + a) * cols : (pair + a + n) * cols, :], w_bwd[a])
        return acc

    def local_moments(idx, pre, acc, early=None):
        mean = both(acc) * (1.0 / local)
        if early is not None:
            early(mean)
        sq = jnp.zeros((8, 128), f32)
        for p in range(4):
            c = pre[p] - mean
            sq += part_sum(c * c)
        send_stats(idx, mean, both(sq))

    def copy_to(stage, name, src, dst, k):
        n, me, ident = groups[name]
        t = lax.rem(me + k, n)
        return pltpu.make_async_remote_copy(
            src_ref=src(t), dst_ref=dst(me),
            send_sem=send_sem.at[stage, k], recv_sem=recv_sem.at[stage, me],
            device_id=ident(t), device_id_type=MESH,
        )

    def spread_out(stage, name, src, dst):
        for k in range(1, groups[name][0]):
            copy_to(stage, name, src, dst, k).start()

    def collect(stage, name, src, dst):
        n, me, ident = groups[name]
        for k in range(1, n):
            f = lax.rem(me + k, n)
            pltpu.make_async_remote_copy(
                src_ref=src(f), dst_ref=dst(f),
                send_sem=send_sem.at[stage, k], recv_sem=recv_sem.at[stage, f],
                device_id=ident(f), device_id_type=MESH,
            ).wait_recv()

    def added(ref, n):
        acc = ref[0].astype(f32)
        for k in range(1, n):
            acc += ref[k].astype(f32)
        return acc

    acc = jnp.zeros((8, 128), f32)
    for p in range(4):
        in_copies[2 * p].wait()
        in_copies[2 * p + 1].wait()
        v = dot_t(img_v[0, p], w_in[0]) + dot_t(img_v[1, p], w_in[1])
        pre1[p] = v
        acc += part_sum(v)
    gain1, shift1 = twice(g1), twice(s1)
    gain2, shift2 = twice(g2), twice(s2)
    pl.semaphore_wait(barrier, partners)

    def early(mean):
        edge1[0] = (pre1[0] - mean).astype(bf16)
        edge1[1] = (pre1[3] - mean).astype(bf16)
        halo(edge1, halo1, 0)

    local_moments(0, pre1, acc, early)
    image_sum = jnp.zeros((8, 256), f32)
    for q in range(2):
        for p in range(4):
            image_sum += part_sum(img_v[q, p].astype(f32))
    image_sum = total(image_sum)
    mu1, istd1 = moments(0, 128)
    mu = mu1
    for p in range(4):
        xhat = (pre1[p] - mu) * istd1
        act, slope = gates(gain1 * xhat + shift1)
        pre1[p] = xhat
        slope1[p] = slope
        widen(wide1, p + 1, act)

    v = conv_fwd(1, 2)
    pre2[1] = v[0:cols]
    pre2[2] = v[cols : 2 * cols]
    acc = part_sum(v)

    def halo_act(c, f):
        xhat = (c + (xbuf[0, f, 0:1, 0:128] - mu1)) * istd1
        return gates(gain1 * xhat + shift1)[0]

    take_halo(edge1, halo1, wide1, 0, halo_act)
    for p in (0, 3):
        v = conv_fwd(p, 1)
        pre2[p] = v
        acc += part_sum(v)
    local_moments(1, pre2, acc)

    rows = 4 * cols
    xhat = pre1[...].reshape(rows, 128).T
    xhat_high = xhat.astype(bf16)
    xhat_low = (xhat - xhat_high.astype(f32)).astype(bf16)
    even, odd = img_v[0].reshape(rows, 256), img_v[1].reshape(rows, 256)
    cross[s, 0:64, :] = (
        dotf(xhat_high[0:64], even) + dotf(xhat_high[64:128], odd)
        + dotf(xhat_low[0:64], even) + dotf(xhat_low[64:128], odd)
    )
    cross[s, 64:72, :] = jnp.broadcast_to(image_sum, (8, 256))

    def cross_copy(k):
        return pltpu.make_async_remote_copy(
            src_ref=cross.at[s], dst_ref=cross.at[s],
            send_sem=cs_sem.at[k], recv_sem=cr_sem.at[s],
            device_id=(d, lax.rem(s + k, spaces)), device_id_type=MESH,
        )

    for k in range(1, 3):
        cross_copy(k).start()
    mu, istd2 = moments(1, 128)
    acc3 = jnp.zeros((8, 256), f32)
    for p in range(4):
        xhat = (pre2[p] - mu) * istd2
        act, slope = gates(gain2 * xhat + shift2)
        pre2[p] = xhat
        slope2[p] = slope
        act = act.astype(bf16)
        act2[p] = act
        for q in range(2):
            v = dotf(act, w_out[q])
            x3[2 * p + q] = v
            acc3 += part_sum(v)

    mean = total(acc3) * (1.0 / local)

    def square(r, acc):
        c = x3[r] - mean
        return acc + part_sum(c * c)

    sq = lax.fori_loop(0, 8, square, jnp.zeros((8, 256), f32))
    send_stats(2, mean, total(sq))
    cot_copy.wait()
    gain3, shift3 = g3[...], s3[...]
    mu, istd3 = moments(2, 256)

    def third(r, carry):
        sd, sx = carry
        p, q = lax.div(r, 2), lax.rem(r, 2)
        xhat = (x3[r] - mu) * istd3
        act, slope = gates(gain3 * xhat + shift3 + img_v[q, p].astype(f32))
        res_v[r] = act.astype(bf16)
        pltpu.make_async_copy(res_v.at[r], result.at[0, r], out_sem.at[0, r]).start()
        e = cot_v[r].astype(f32) * slope
        x3[r] = xhat
        e3[r] = e
        return sd + part_sum(e), sx + part_sum(e * xhat)

    zero8 = jnp.zeros((8, 256), f32)
    sd, sx = lax.fori_loop(0, 8, third, (zero8, zero8))
    sd3, sx3 = total(sd), total(sx)
    send_stats(3, sd3, sx3)
    sd, sx = sums(3, 256)
    k0 = gain3 * istd3
    k1 = k0 * sd * (1.0 / count)
    k2 = k0 * sx * (1.0 / count)
    sd_acc = jnp.zeros((8, 128), f32)
    sx_acc = jnp.zeros((8, 128), f32)
    for p in range(4):
        for q in range(2):
            r = 2 * p + q
            dh3[q, p] = (k0 * e3[r] - k1 - k2 * x3[r]).astype(bf16)
        back = dot_t(dh3[0, p], w_out[0]) + dot_t(dh3[1, p], w_out[1])
        g = back * slope2[p]
        grad2[p] = g
        sd_acc += part_sum(g)
        sx_acc += part_sum(g * pre2[p])
    sd2, sx2 = both(sd_acc), both(sx_acc)
    send_stats(4, sd2, sx2)
    act_t = act2[...].reshape(rows, 128).T
    expand = dotf(act_t[0:64], dh3[0].reshape(rows, 256)) + dotf(
        act_t[64:128], dh3[1].reshape(rows, 256)
    )
    sd, sx = sums(4, 128)
    k0 = gain2 * istd2
    k1 = k0 * sd * (1.0 / count)
    k2 = k0 * sx * (1.0 / count)
    pieces = []
    for p in (0, 3, 1, 2):
        dh = k0 * grad2[p] - k1 - k2 * pre2[p]
        if p == 0:
            edge2[0] = dh.astype(bf16)
        if p == 3:
            edge2[1] = dh.astype(bf16)
            halo(edge2, halo2, 1)
        widen(wide2, p + 1, dh)

    sd_acc = jnp.zeros((8, 128), f32)
    sx_acc = jnp.zeros((8, 128), f32)

    def first_back(p, v, sd_acc, sx_acc):
        g = v * slope1[p]
        grad1[p] = g
        return sd_acc + part_sum(g), sx_acc + part_sum(g * pre1[p])

    v = conv_bwd(1, 2)
    sd_acc, sx_acc = first_back(1, v[0:cols], sd_acc, sx_acc)
    sd_acc, sx_acc = first_back(2, v[cols : 2 * cols], sd_acc, sx_acc)
    take_halo(edge2, halo2, wide2, 1, lambda c, f: c)
    for p in (0, 3):
        sd_acc, sx_acc = first_back(p, conv_bwd(p, 1), sd_acc, sx_acc)
    sd1, sx1 = both(sd_acc), both(sx_acc)
    send_stats(5, sd1, sx1)

    main_rows = MAIN_ROWS // ends
    late_rows = LATE_ROWS // ends

    def put_main(row, block):
        n = block.shape[0]
        done = 0
        while done < n:
            piece, off = divmod(row + done, main_rows)
            size = min(n - done, main_rows - off)
            main_a[piece, off : off + size, :] = block[done : done + size].astype(bf16)
            done += size

    dh2_t = wide2[cols : cols + rows, 128:256].T
    low = lax.broadcasted_iota(jnp.int32, (64, 128), 1) < 64
    taps = []
    for a in range(3):
        g = dotf(dh2_t, wide1[a * cols : a * cols + rows, :])
        for b in range(3):
            g0 = g[0:64, b * 128 : (b + 1) * 128]
            g1v = g[64:128, b * 128 : (b + 1) * 128]
            if (3 * a + b) % 2 == 0:
                taps.append(g0 + pltpu.roll(g1v, 64, 1))
            else:
                taps.append(pltpu.roll(g0, 64, 1) + g1v)
    taps.append(jnp.zeros((64, 128), f32))
    for u in range(5):
        put_main(64 * u, jnp.where(low, taps[2 * u], taps[2 * u + 1]))
    put_main(320, expand[:, 0:128])
    put_main(384, expand[:, 128:256])
    low1 = lax.broadcasted_iota(jnp.int32, (1, 128), 1) < 64
    vec = jnp.concatenate(
        [
            sx3[:, 0:128], sx3[:, 128:256], sd3[:, 0:128], sd3[:, 128:256],
            jnp.where(low1, sx2, sd2), jnp.where(low1, sx1, sd1),
            jnp.zeros((2, 128), f32),
        ],
        axis=0,
    )
    vec_high = vec.astype(bf16)
    vec_low = vec - vec_high.astype(f32)
    put_main(VEC, jnp.concatenate([vec_high.astype(f32), vec_low], axis=0))
    put_main(VEC + 16, jnp.zeros((48, 128), f32))
    main_ra[end] = main_a[end]

    a_src, a_dst = (lambda t: main_a.at[t]), (lambda me: main_ra.at[me])
    spread_out(0, "a", a_src, a_dst)

    k0 = gain1 * istd1
    own_sd = sd1 * (1.0 / local)
    own_sx = sx1 * (1.0 / local)
    for p in range(4):
        dh1[p] = (k0 * (grad1[p] - own_sd - pre1[p] * own_sx)).astype(bf16)
    rest_t = dh1[...].reshape(rows, 128).T
    reduce = dotf(rest_t[0:64], img_v[0].reshape(rows, 256)) + dotf(
        rest_t[64:128], img_v[1].reshape(rows, 256)
    )
    for k in range(1, 3):
        f = lax.rem(s + k, spaces)
        pltpu.make_async_remote_copy(
            src_ref=cross.at[f], dst_ref=cross.at[f],
            send_sem=cs_sem.at[k], recv_sem=cr_sem.at[f],
            device_id=(d, f), device_id_type=MESH,
        ).wait_recv()
    excess = cross[s] * (1.0 / local) - (cross[0] + cross[1] + cross[2]) * (1.0 / count)

    def down(row):
        column = jnp.broadcast_to(row, (128, 128)).T[0:64]
        return jnp.concatenate([column, column], axis=1)

    reduce += down(k0 * sd1) * excess[64:65] + down(k0 * sx1) * excess[0:64]
    for h in range(2):
        for piece in range(ends):
            lo, hi = piece * late_rows, (piece + 1) * late_rows
            a, b = max(lo, 64 * h), min(hi, 64 * h + 64)
            if a < b:
                late_a[piece, a - lo : b - lo, :] = reduce[
                    a - 64 * h : b - 64 * h, 128 * h : 128 * h + 128
                ].astype(bf16)
    late_ra[end] = late_a[end]
    la_src, la_dst = (lambda t: late_a.at[t]), (lambda me: late_ra.at[me])
    spread_out(5, "a", la_src, la_dst)

    collect(0, "a", a_src, a_dst)
    part = added(main_ra, ends)
    sub = main_rows // ys
    for k in range(ys):
        main_b[k] = part[k * sub : (k + 1) * sub]
    main_rb[y] = main_b[y]
    b_src, b_dst = (lambda t: main_b.at[t]), (lambda me: main_rb.at[me])
    spread_out(1, "b", b_src, b_dst)

    sd, sx = sums(5, 128)
    k1 = k0 * sd * (1.0 / count)
    k2 = k0 * sx * (1.0 / count)

    def last(p, carry):
        dh = (k0 * grad1[p] - k1 - k2 * pre1[p]).astype(bf16)
        for q in range(2):
            r = 2 * p + q
            gi_v[r] = (dotf(dh, w_in[q]) + e3[r]).astype(bf16)
            pltpu.make_async_copy(gi_v.at[r], gimages.at[0, r], out_sem.at[1, r]).start()
        return carry

    lax.fori_loop(0, 2, last, 0)

    collect(5, "a", la_src, la_dst)
    late_b[y] = added(late_ra, ends).astype(bf16)
    lb_src, lb_dst = (lambda t: late_b.at[y]), (lambda me: late_b.at[me])
    spread_out(6, "b", lb_src, lb_dst)

    collect(1, "b", b_src, b_dst)
    main_c[z] = added(main_rb, ys)
    c_src, c_dst = (lambda t: main_c.at[z]), (lambda me: main_c.at[me])
    spread_out(2, "c", c_src, c_dst)

    lax.fori_loop(2, 4, last, 0)

    collect(6, "b", lb_src, lb_dst)
    late_c[z] = added(late_b, ys).astype(bf16)
    lc_src, lc_dst = (lambda t: late_c.at[z]), (lambda me: late_c.at[me])
    spread_out(7, "c", lc_src, lc_dst)

    collect(2, "c", c_src, c_dst)
    main_gb[y] = added(main_c, zs)
    gb_src, gb_dst = (lambda t: main_gb.at[y]), (lambda me: main_gb.at[me])
    spread_out(3, "b", gb_src, gb_dst)

    collect(7, "c", lc_src, lc_dst)
    late_ga[end] = added(late_c, zs).astype(bf16)
    lg_src, lg_dst = (lambda t: late_ga.at[end]), (lambda me: late_ga.at[me])
    spread_out(8, "a", lg_src, lg_dst)

    collect(3, "b", gb_src, gb_dst)
    whole = main_gb[...].reshape(main_rows, 128)
    main_ga[end] = whole.astype(bf16)

    @pl.when(end == VEC // main_rows)
    def _():
        at = VEC % main_rows
        v = whole[at : at + 8] + whole[at + 8 : at + 16]
        v_high = v.astype(bf16).astype(f32)
        main_ga[end, at : at + 16, :] = jnp.concatenate([v_high, v - v_high], axis=0).astype(bf16)

    ga_src, ga_dst = (lambda t: main_ga.at[end]), (lambda me: main_ga.at[me])
    spread_out(4, "a", ga_src, ga_dst)

    scale = 1.0 / lax.axis_size("dp")
    collect(8, "a", lg_src, lg_dst)
    late = late_ga[...].reshape(LATE_ROWS, 128).astype(f32) * scale
    o_reduce[:, 0:128] = late[0:64]
    o_reduce[:, 128:256] = late[64:128]

    collect(4, "a", ga_src, ga_dst)
    main = main_ga[...].reshape(MAIN_ROWS, 128).astype(f32) * scale
    for u in range(5):
        pair = main[64 * u : 64 * u + 64]
        pair = jnp.concatenate([pair, pair], axis=0).T
        o_dilated[2 * u] = pair[0:64, 0:64]
        if u < 4:
            o_dilated[2 * u + 1] = pair[64:128, 0:64]
    o_expand[:, 0:128] = main[320:384]
    o_expand[:, 128:256] = main[384:448]
    o_vec[...] = main[VEC : VEC + 8] + main[VEC + 8 : VEC + 16]

    outs = []
    for k, (src, dst) in enumerate(
        ((o_reduce, h_reduce), (o_dilated, h_dilated), (o_expand, h_expand), (o_vec, h_vec))
    ):
        outs.append(pltpu.make_async_copy(src, dst, out_sem.at[2, k]))
        outs[-1].start()

    for idx in range(6):
        for k in range(1, 3):
            pltpu.make_async_remote_copy(
                src_ref=xbuf.at[idx, s], dst_ref=xbuf.at[idx, s],
                send_sem=xs_sem.at[idx, k - 1], recv_sem=xr_sem.at[idx, s],
                device_id=(d, lax.rem(s + k, spaces)), device_id_type=MESH,
            ).wait_send()
    for k in range(1, 3):
        cross_copy(k).wait_send()
    end_halo(edge1, halo1, 0)
    end_halo(edge2, halo2, 1)
    for stage, name, src, dst in (
        (0, "a", a_src, a_dst), (1, "b", b_src, b_dst), (2, "c", c_src, c_dst),
        (3, "b", gb_src, gb_dst), (4, "a", ga_src, ga_dst), (5, "a", la_src, la_dst),
        (6, "b", lb_src, lb_dst), (7, "c", lc_src, lc_dst), (8, "a", lg_src, lg_dst),
    ):
        for k in range(1, groups[name][0]):
            copy_to(stage, name, src, dst, k).wait_send()
    for r in range(8):
        pltpu.make_async_copy(res_v.at[r], result.at[0, r], out_sem.at[0, r]).wait()
        pltpu.make_async_copy(gi_v.at[r], gimages.at[0, r], out_sem.at[1, r]).wait()
    for c in outs:
        c.wait()


def store(*refs):
    ins, outs, (half, full, vec, sem) = refs[:6], refs[6:17], refs[17:]
    fetch = pltpu.make_async_copy(ins[5], vec, sem.at[19])
    fetch.start()
    copies = []
    for k in range(2):
        for r in range(4):
            rows = pl.ds(2 * r, 2)
            copies.append(
                pltpu.make_async_copy(ins[k].at[0, rows], outs[k].at[0, rows], sem.at[11 + 4 * k + r])
            )
    copies += [pltpu.make_async_copy(ins[k], outs[k], sem.at[k]) for k in range(2, 5)]
    for c in copies:
        c.start()
    fetch.wait()
    for k, row in enumerate((5, 4)):
        v = vec[row : row + 1, :]
        half[2 * k] = v[:, 0:64]
        half[2 * k + 1] = pltpu.roll(jnp.broadcast_to(v, (8, 128)), 64, 1)[0:1, 0:64]
    for k in range(2):
        full[k] = jnp.concatenate([vec[2 * k : 2 * k + 1, :], vec[2 * k + 1 : 2 * k + 2, :]], axis=1)
    for k in range(4):
        copies.append(pltpu.make_async_copy(half.at[k], outs[5 + k], sem.at[5 + k]))
        copies[-1].start()
    for k in range(2):
        copies.append(pltpu.make_async_copy(full.at[k], outs[9 + k], sem.at[9 + k]))
        copies[-1].start()
    for c in copies:
        c.wait()


def solution(mesh):
    splits = SPLITS[mesh.shape["dp"]]
    ends, ys, highs = splits
    zs = highs * mesh.shape["space"]
    main_rows = MAIN_ROWS // ends
    late_rows = LATE_ROWS // ends
    sub = main_rows // ys

    def shards(images, wr, wd, we, g1, s1, g2, s2, g3, s3, cot):
        vmem = pl.BlockSpec(memory_space=pltpu.VMEM)
        hbm = pl.BlockSpec(memory_space=pltpu.HBM)
        big = jax.ShapeDtypeStruct(images.shape, bf16)
        maps = lambda: pltpu.VMEM((4, 288, 128), f32)
        outs = pl.pallas_call(
            functools.partial(kernel, splits),
            out_shape=(
                big, big,
                jax.ShapeDtypeStruct((64, 256), f32),
                jax.ShapeDtypeStruct((9, 64, 64), f32),
                jax.ShapeDtypeStruct((64, 256), f32),
                jax.ShapeDtypeStruct((8, 128), f32),
            ),
            in_specs=[hbm] * 11,
            out_specs=(hbm,) * 6,
            scratch_shapes=[
                pltpu.VMEM((8, 288, 256), bf16),
                pltpu.VMEM((8, 288, 256), bf16),
                pltpu.VMEM((64, 256), f32),
                pltpu.VMEM((9, 64, 64), f32),
                pltpu.VMEM((64, 256), f32),
                pltpu.VMEM((8, 128), f32),
                pltpu.VMEM((2, 4, 288, 256), bf16),
                pltpu.VMEM((8, 288, 256), bf16),
                pltpu.VMEM((64, 256), bf16),
                pltpu.VMEM((3, 3, 64, 64), bf16),
                pltpu.VMEM((64, 256), bf16),
                pltpu.VMEM((1, 64), f32), pltpu.VMEM((1, 64), f32),
                pltpu.VMEM((1, 64), f32), pltpu.VMEM((1, 64), f32),
                pltpu.VMEM((1, 256), f32), pltpu.VMEM((1, 256), f32),
                pltpu.VMEM((2, 128, 256), bf16),
                pltpu.VMEM((2, 128, 256), bf16),
                pltpu.VMEM((3, 384, 128), bf16),
                pltpu.VMEM((3, 128, 384), bf16),
                maps(), maps(), maps(), maps(),
                pltpu.VMEM((4, 288, 128), bf16),
                pltpu.VMEM((8, 288, 256), f32),
                pltpu.VMEM((8, 288, 256), f32),
                pltpu.VMEM((2, 4, 288, 256), bf16),
                maps(), maps(),
                pltpu.VMEM((4, 288, 128), bf16),
                pltpu.VMEM((2, 288, 128), bf16),
                pltpu.VMEM((2, 288, 128), bf16),
                pltpu.VMEM((2, 288, 128), bf16),
                pltpu.VMEM((2, 288, 128), bf16),
                pltpu.VMEM((6 * 288, 384), bf16),
                pltpu.VMEM((6 * 288, 384), bf16),
                pltpu.VMEM((6, 3, 8, 256), f32),
                pltpu.VMEM((3, 72, 256), f32),
                pltpu.VMEM((ends, main_rows, 128), bf16),
                pltpu.VMEM((ends, main_rows, 128), bf16),
                pltpu.VMEM((ys, sub, 128), f32),
                pltpu.VMEM((ys, sub, 128), f32),
                pltpu.VMEM((zs, sub, 128), f32),
                pltpu.VMEM((ys, sub, 128), f32),
                pltpu.VMEM((ends, main_rows, 128), bf16),
                pltpu.VMEM((ends, late_rows, 128), bf16),
                pltpu.VMEM((ends, late_rows, 128), bf16),
                pltpu.VMEM((ys, late_rows, 128), bf16),
                pltpu.VMEM((zs, late_rows, 128), bf16),
                pltpu.VMEM((ends, late_rows, 128), bf16),
                pltpu.SemaphoreType.DMA((18,)),
                pltpu.SemaphoreType.DMA((3, 8)),
                pltpu.SemaphoreType.DMA((2, 2)),
                pltpu.SemaphoreType.DMA((2, 2)),
                pltpu.SemaphoreType.DMA((6, 2)),
                pltpu.SemaphoreType.DMA((6, 3)),
                pltpu.SemaphoreType.DMA((3,)),
                pltpu.SemaphoreType.DMA((3,)),
                pltpu.SemaphoreType.DMA((9, 12)),
                pltpu.SemaphoreType.DMA((9, 12)),
            ],
            compiler_params=pltpu.CompilerParams(
                collective_id=0, has_side_effects=True, vmem_limit_bytes=60 * 1024 * 1024
            ),
        )(
            images, wr.T, wd, we,
            g1.reshape(1, 64), s1.reshape(1, 64), g2.reshape(1, 64), s2.reshape(1, 64),
            g3.reshape(1, 256), s3.reshape(1, 256), cot,
        )
        res, gi, g_reduce, g_dilated, g_expand, v1, v2, v3, v4, v5, v6 = pl.pallas_call(
            store,
            out_shape=tuple(jax.ShapeDtypeStruct(x.shape, x.dtype) for x in outs[:5])
            + (jax.ShapeDtypeStruct((1, 64), f32),) * 4
            + (jax.ShapeDtypeStruct((1, 256), f32),) * 2,
            in_specs=[hbm] * 6,
            out_specs=(hbm,) * 11,
            scratch_shapes=[
                pltpu.VMEM((4, 1, 64), f32),
                pltpu.VMEM((2, 1, 256), f32),
                pltpu.VMEM((8, 128), f32),
                pltpu.SemaphoreType.DMA((20,)),
            ],
            compiler_params=pltpu.CompilerParams(vmem_limit_bytes=60 * 1024 * 1024),
        )(*outs)
        return (
            res, gi, g_reduce.T, g_dilated.reshape(3, 3, 64, 64), g_expand,
            v1.reshape(64), v2.reshape(64), v3.reshape(64), v4.reshape(64),
            v5.reshape(256), v6.reshape(256),
        )

    placed = (P("dp", "space", None, None),) + (P(),) * 9 + (P("dp", "space", None, None),)
    return jax.shard_map(
        shards,
        mesh=mesh,
        in_specs=placed,
        out_specs=(P("dp", "space", None, None),) * 2 + (P(),) * 9,
        check_vma=False,
    )
```

```python
import functools

import jax
import jax.numpy as jnp
from jax import lax
from jax.experimental import pallas as pl
from jax.experimental.pallas import tpu as pltpu
from jax.sharding import PartitionSpec as P

MESH = pl.DeviceIdType.MESH
f32 = jnp.float32
bf16 = jnp.bfloat16
epsilon = 1e-05

SPLITS = {256: (8, 8, 4), 4: (2, 2, 1)}
MAIN_ROWS = 512
LATE_ROWS = 128
VEC = 448


def part_sum(x):
    n, lanes = x.shape
    return jnp.sum(x.reshape(n // 8, 8, lanes), axis=0)


def both(v8):
    v8 = v8 + pltpu.roll(v8, 64, 1)
    return jnp.sum(v8, axis=0, keepdims=True)


def total(v8):
    return jnp.sum(v8, axis=0, keepdims=True)


def gates(v):
    half = 0.5 * v
    t = jnp.tanh(half)
    act = half * t + half
    sig = 0.5 * t + 0.5
    slope = sig + act * (0.5 - 0.5 * t)
    return act, slope


def dotf(a, b):
    return jnp.dot(a, b, preferred_element_type=f32)


def dot_t(a, b):
    return lax.dot_general(a, b, (((1,), (1,)), ((), ())), preferred_element_type=f32)


def kernel(
    splits,
    images, wr_h, wd_h, we_h, g1_h, s1_h, g2_h, s2_h, g3_h, s3_h, cot,
    result, gimages, h_reduce, h_dilated, h_expand, h_vec,
    res_v, gi_v, o_reduce, o_dilated, o_expand, o_vec, img_v, cot_v, wr, wd, we, g1, s1, g2, s2, g3, s3,
    w_in, w_out, w_fwd, w_bwd,
    pre1, slope1, pre2, slope2, act2, x3, e3, dh3, grad2, grad1, dh1,
    edge1, edge2, halo1, halo2, wide1, wide2,
    xbuf, cross,
    main_a, main_ra, main_b, main_rb, main_c, main_gb, main_ga,
    late_a, late_ra, late_b, late_c, late_ga,
    in_sem, out_sem, hs_sem, hr_sem, xs_sem, xr_sem, cs_sem, cr_sem, send_sem, recv_sem,
):
    ends, ys, highs = splits
    spaces = lax.axis_size("space")
    zs = highs * spaces
    d = lax.axis_index("dp")
    s = lax.axis_index("space")
    end = lax.rem(d, ends)
    high = lax.rem(lax.div(d, ends), highs)
    y = lax.div(d, ends * highs)
    z = high * spaces + s
    cols = 288
    local = 2304.0
    count = local * spaces

    def id_a(k):
        return (d - end + k, s)

    def id_b(k):
        return (d + (k - y) * (ends * highs), s)

    def id_c(k):
        kh = lax.div(k, spaces)
        return (d + (kh - high) * ends, lax.rem(k, spaces))

    groups = {"a": (ends, end, id_a), "b": (ys, y, id_b), "c": (zs, z, id_c)}

    in_copies = []
    for r in range(8):
        c = pltpu.make_async_copy(images.at[0, r], img_v.at[r % 2, r // 2], in_sem.at[r])
        c.start()
        in_copies.append(c)
    small = []
    pairs = (
        (wr_h, wr), (wd_h, wd), (we_h, we), (g1_h, g1), (s1_h, s1),
        (g2_h, g2), (s2_h, s2), (g3_h, g3), (s3_h, s3),
    )
    for k, (src, dst) in enumerate(pairs):
        c = pltpu.make_async_copy(src, dst, in_sem.at[9 + k])
        c.start()
        small.append(c)
    cot_copy = pltpu.make_async_copy(cot.at[0], cot_v, in_sem.at[8])
    cot_copy.start()

    barrier = pltpu.get_barrier_semaphore()
    partners = 0
    for name in "cba":
        n, me, ident = groups[name]
        for k in sorted(range(1, n), key=lambda k: -min(k, n - k)):
            pl.semaphore_signal(
                barrier, inc=1, device_id=ident(lax.rem(me + k, n)), device_id_type=MESH
            )
            partners += 1

    for c in small:
        c.wait()
    zero_out = jnp.zeros((64, 256), bf16)
    w_in[0] = jnp.concatenate([wr[...], zero_out], axis=0)
    w_in[1] = jnp.concatenate([zero_out, wr[...]], axis=0)
    w_out[0] = jnp.concatenate([we[...], zero_out], axis=0)
    w_out[1] = jnp.concatenate([zero_out, we[...]], axis=0)
    zero_mid = jnp.zeros((64, 64), bf16)
    for a in range(3):
        for b in range(3):
            w = wd[a, b]
            diag = jnp.concatenate(
                [
                    jnp.concatenate([w, zero_mid], axis=1),
                    jnp.concatenate([zero_mid, w], axis=1),
                ],
                axis=0,
            )
            w_fwd[a, b * 128 : (b + 1) * 128, :] = diag
            w_bwd[2 - a, :, (2 - b) * 128 : (3 - b) * 128] = diag

    @pl.when(s == 0)
    def _():
        wide1[0:cols, :] = jnp.zeros((cols, 384), bf16)
        wide2[0:cols, :] = jnp.zeros((cols, 384), bf16)

    @pl.when(s == spaces - 1)
    def _():
        wide1[5 * cols : 6 * cols, :] = jnp.zeros((cols, 384), bf16)
        wide2[5 * cols : 6 * cols, :] = jnp.zeros((cols, 384), bf16)

    def twice(ref):
        v = ref[...]
        return jnp.concatenate([v, v], axis=1)

    def send_stats(idx, first, second):
        lanes = first.shape[1]
        xbuf[idx, s, 0:1, 0:lanes] = first
        xbuf[idx, s, 1:2, 0:lanes] = second
        for k in range(1, 3):
            pltpu.make_async_remote_copy(
                src_ref=xbuf.at[idx, s],
                dst_ref=xbuf.at[idx, s],
                send_sem=xs_sem.at[idx, k - 1],
                recv_sem=xr_sem.at[idx, s],
                device_id=(d, lax.rem(s + k, spaces)),
                device_id_type=MESH,
            ).start()

    def wait_stats(idx, lanes):
        for k in range(1, 3):
            f = lax.rem(s + k, spaces)
            pltpu.make_async_remote_copy(
                src_ref=xbuf.at[idx, f],
                dst_ref=xbuf.at[idx, f],
                send_sem=xs_sem.at[idx, k - 1],
                recv_sem=xr_sem.at[idx, f],
                device_id=(d, f),
                device_id_type=MESH,
            ).wait_recv()
        firsts = [xbuf[idx, j, 0:1, 0:lanes] for j in range(3)]
        seconds = [xbuf[idx, j, 1:2, 0:lanes] for j in range(3)]
        return firsts, seconds

    def moments(idx, lanes):
        means, squares = wait_stats(idx, lanes)
        mu = (means[0] + means[1] + means[2]) * (1.0 / 3.0)
        spread = sum((m - mu) * (m - mu) for m in means)
        var = (squares[0] + squares[1] + squares[2] + local * spread) * (1.0 / count)
        return mu, lax.rsqrt(var + epsilon)

    def sums(idx, lanes):
        firsts, seconds = wait_stats(idx, lanes)
        return firsts[0] + firsts[1] + firsts[2], seconds[0] + seconds[1] + seconds[2]

    def halo(edge, halos, which):
        @pl.when(s > 0)
        def _():
            pltpu.make_async_remote_copy(
                src_ref=edge.at[0], dst_ref=halos.at[1],
                send_sem=hs_sem.at[which, 0], recv_sem=hr_sem.at[which, 1],
                device_id=(d, s - 1), device_id_type=MESH,
            ).start()

        @pl.when(s < spaces - 1)
        def _():
            pltpu.make_async_remote_copy(
                src_ref=edge.at[1], dst_ref=halos.at[0],
                send_sem=hs_sem.at[which, 1], recv_sem=hr_sem.at[which, 0],
                device_id=(d, s + 1), device_id_type=MESH,
            ).start()

    def widen(wide, pair, x):
        at = pair * cols
        spot = lax.broadcasted_iota(jnp.int32, (cols, 128), 0)
        before = jnp.where(spot >= 2, pltpu.roll(x, 2, 0), 0.0)
        after = jnp.where(spot < cols - 2, pltpu.roll(x, cols - 2, 0), 0.0)
        wide[at : at + cols, 0:128] = before.astype(bf16)
        wide[at : at + cols, 128:256] = x.astype(bf16)
        wide[at : at + cols, 256:384] = after.astype(bf16)

    def take_halo(edge, halos, wide, which, finish):
        @pl.when(s > 0)
        def _():
            pltpu.make_async_remote_copy(
                src_ref=edge.at[1], dst_ref=halos.at[0],
                send_sem=hs_sem.at[which, 0], recv_sem=hr_sem.at[which, 0],
                device_id=(d, s - 1), device_id_type=MESH,
            ).wait_recv()
            widen(wide, 0, finish(halos[0].astype(f32), s - 1))

        @pl.when(s < spaces - 1)
        def _():
            pltpu.make_async_remote_copy(
                src_ref=edge.at[0], dst_ref=halos.at[1],
                send_sem=hs_sem.at[which, 1], recv_sem=hr_sem.at[which, 1],
                device_id=(d, s + 1), device_id_type=MESH,
            ).wait_recv()
            widen(wide, 5, finish(halos[1].astype(f32), s + 1))

    def end_halo(edge, halos, which):
        @pl.when(s > 0)
        def _():
            pltpu.make_async_remote_copy(
                src_ref=edge.at[0], dst_ref=halos.at[1],
                send_sem=hs_sem.at[which, 0], recv_sem=hr_sem.at[which, 1],
                device_id=(d, s - 1), device_id_type=MESH,
            ).wait_send()

        @pl.when(s < spaces - 1)
        def _():
            pltpu.make_async_remote_copy(
                src_ref=edge.at[1], dst_ref=halos.at[0],
                send_sem=hs_sem.at[which, 1], recv_sem=hr_sem.at[which, 0],
                device_id=(d, s + 1), device_id_type=MESH,
            ).wait_send()

    def conv_fwd(pair, n):
        acc = dotf(wide1[pair * cols : (pair + n) * cols, :], w_fwd[0])
        for a in range(1, 3):
            acc += dotf(wide1[(pair + a) * cols : (pair + a + n) * cols, :], w_fwd[a])
        return acc

    def conv_bwd(pair, n):
        acc = dot_t(wide2[pair * cols : (pair + n) * cols, :], w_bwd[0])
        for a in range(1, 3):
            acc += dot_t(wide2[(pair + a) * cols : (pair + a + n) * cols, :], w_bwd[a])
        return acc

    def local_moments(idx, pre, acc, early=None):
        mean = both(acc) * (1.0 / local)
        if early is not None:
            early(mean)
        sq = jnp.zeros((8, 128), f32)
        for p in range(4):
            c = pre[p] - mean
            sq += part_sum(c * c)
        send_stats(idx, mean, both(sq))

    def copy_to(stage, name, src, dst, k):
        n, me, ident = groups[name]
        t = lax.rem(me + k, n)
        return pltpu.make_async_remote_copy(
            src_ref=src(t), dst_ref=dst(me),
            send_sem=send_sem.at[stage, k], recv_sem=recv_sem.at[stage, me],
            device_id=ident(t), device_id_type=MESH,
        )

    def spread_out(stage, name, src, dst):
        for k in range(1, groups[name][0]):
            copy_to(stage, name, src, dst, k).start()

    def collect(stage, name, src, dst):
        n, me, ident = groups[name]
        for k in range(1, n):
            f = lax.rem(me + k, n)
            pltpu.make_async_remote_copy(
                src_ref=src(f), dst_ref=dst(f),
                send_sem=send_sem.at[stage, k], recv_sem=recv_sem.at[stage, f],
                device_id=ident(f), device_id_type=MESH,
            ).wait_recv()

    def added(ref, n):
        acc = ref[0].astype(f32)
        for k in range(1, n):
            acc += ref[k].astype(f32)
        return acc

    acc = jnp.zeros((8, 128), f32)
    for p in range(4):
        in_copies[2 * p].wait()
        in_copies[2 * p + 1].wait()
        v = dot_t(img_v[0, p], w_in[0]) + dot_t(img_v[1, p], w_in[1])
        pre1[p] = v
        acc += part_sum(v)
    gain1, shift1 = twice(g1), twice(s1)
    gain2, shift2 = twice(g2), twice(s2)
    pl.semaphore_wait(barrier, partners)

    def early(mean):
        edge1[0] = (pre1[0] - mean).astype(bf16)
        edge1[1] = (pre1[3] - mean).astype(bf16)
        halo(edge1, halo1, 0)

    local_moments(0, pre1, acc, early)
    image_sum = jnp.zeros((8, 256), f32)
    for q in range(2):
        for p in range(4):
            image_sum += part_sum(img_v[q, p].astype(f32))
    image_sum = total(image_sum)
    mu1, istd1 = moments(0, 128)
    mu = mu1
    for p in range(4):
        xhat = (pre1[p] - mu) * istd1
        act, slope = gates(gain1 * xhat + shift1)
        pre1[p] = xhat
        slope1[p] = slope
        widen(wide1, p + 1, act)

    v = conv_fwd(1, 2)
    pre2[1] = v[0:cols]
    pre2[2] = v[cols : 2 * cols]
    acc = part_sum(v)

    def halo_act(c, f):
        xhat = (c + (xbuf[0, f, 0:1, 0:128] - mu1)) * istd1
        return gates(gain1 * xhat + shift1)[0]

    take_halo(edge1, halo1, wide1, 0, halo_act)
    for p in (0, 3):
        v = conv_fwd(p, 1)
        pre2[p] = v
        acc += part_sum(v)
    local_moments(1, pre2, acc)

    rows = 4 * cols
    xhat = pre1[...].reshape(rows, 128).T
    xhat_high = xhat.astype(bf16)
    xhat_low = (xhat - xhat_high.astype(f32)).astype(bf16)
    even, odd = img_v[0].reshape(rows, 256), img_v[1].reshape(rows, 256)
    cross[s, 0:64, :] = (
        dotf(xhat_high[0:64], even) + dotf(xhat_high[64:128], odd)
        + dotf(xhat_low[0:64], even) + dotf(xhat_low[64:128], odd)
    )
    cross[s, 64:72, :] = jnp.broadcast_to(image_sum, (8, 256))

    def cross_copy(k):
        return pltpu.make_async_remote_copy(
            src_ref=cross.at[s], dst_ref=cross.at[s],
            send_sem=cs_sem.at[k], recv_sem=cr_sem.at[s],
            device_id=(d, lax.rem(s + k, spaces)), device_id_type=MESH,
        )

    for k in range(1, 3):
        cross_copy(k).start()
    mu, istd2 = moments(1, 128)
    acc3 = jnp.zeros((8, 256), f32)
    for p in range(4):
        xhat = (pre2[p] - mu) * istd2
        act, slope = gates(gain2 * xhat + shift2)
        pre2[p] = xhat
        slope2[p] = slope
        act = act.astype(bf16)
        act2[p] = act
        for q in range(2):
            v = dotf(act, w_out[q])
            x3[2 * p + q] = v
            acc3 += part_sum(v)

    mean = total(acc3) * (1.0 / local)

    def square(r, acc):
        c = x3[r] - mean
        return acc + part_sum(c * c)

    sq = lax.fori_loop(0, 8, square, jnp.zeros((8, 256), f32))
    send_stats(2, mean, total(sq))
    cot_copy.wait()
    gain3, shift3 = g3[...], s3[...]
    mu, istd3 = moments(2, 256)

    def third(r, carry):
        sd, sx = carry
        p, q = lax.div(r, 2), lax.rem(r, 2)
        xhat = (x3[r] - mu) * istd3
        act, slope = gates(gain3 * xhat + shift3 + img_v[q, p].astype(f32))
        res_v[r] = act.astype(bf16)
        pltpu.make_async_copy(res_v.at[r], result.at[0, r], out_sem.at[0, r]).start()
        e = cot_v[r].astype(f32) * slope
        x3[r] = xhat
        e3[r] = e
        return sd + part_sum(e), sx + part_sum(e * xhat)

    zero8 = jnp.zeros((8, 256), f32)
    sd, sx = lax.fori_loop(0, 8, third, (zero8, zero8))
    sd3, sx3 = total(sd), total(sx)
    send_stats(3, sd3, sx3)
    sd, sx = sums(3, 256)
    k0 = gain3 * istd3
    k1 = k0 * sd * (1.0 / count)
    k2 = k0 * sx * (1.0 / count)
    sd_acc = jnp.zeros((8, 128), f32)
    sx_acc = jnp.zeros((8, 128), f32)
    for p in range(4):
        for q in range(2):
            r = 2 * p + q
            dh3[q, p] = (k0 * e3[r] - k1 - k2 * x3[r]).astype(bf16)
        back = dot_t(dh3[0, p], w_out[0]) + dot_t(dh3[1, p], w_out[1])
        g = back * slope2[p]
        grad2[p] = g
        sd_acc += part_sum(g)
        sx_acc += part_sum(g * pre2[p])
    sd2, sx2 = both(sd_acc), both(sx_acc)
    send_stats(4, sd2, sx2)
    act_t = act2[...].reshape(rows, 128).T
    expand = dotf(act_t[0:64], dh3[0].reshape(rows, 256)) + dotf(
        act_t[64:128], dh3[1].reshape(rows, 256)
    )
    sd, sx = sums(4, 128)
    k0 = gain2 * istd2
    k1 = k0 * sd * (1.0 / count)
    k2 = k0 * sx * (1.0 / count)
    pieces = []
    for p in (0, 3, 1, 2):
        dh = k0 * grad2[p] - k1 - k2 * pre2[p]
        if p == 0:
            edge2[0] = dh.astype(bf16)
        if p == 3:
            edge2[1] = dh.astype(bf16)
            halo(edge2, halo2, 1)
        widen(wide2, p + 1, dh)

    sd_acc = jnp.zeros((8, 128), f32)
    sx_acc = jnp.zeros((8, 128), f32)

    def first_back(p, v, sd_acc, sx_acc):
        g = v * slope1[p]
        grad1[p] = g
        return sd_acc + part_sum(g), sx_acc + part_sum(g * pre1[p])

    v = conv_bwd(1, 2)
    sd_acc, sx_acc = first_back(1, v[0:cols], sd_acc, sx_acc)
    sd_acc, sx_acc = first_back(2, v[cols : 2 * cols], sd_acc, sx_acc)
    take_halo(edge2, halo2, wide2, 1, lambda c, f: c)
    for p in (0, 3):
        sd_acc, sx_acc = first_back(p, conv_bwd(p, 1), sd_acc, sx_acc)
    sd1, sx1 = both(sd_acc), both(sx_acc)
    send_stats(5, sd1, sx1)

    main_rows = MAIN_ROWS // ends
    late_rows = LATE_ROWS // ends

    def put_main(row, block):
        n = block.shape[0]
        done = 0
        while done < n:
            piece, off = divmod(row + done, main_rows)
            size = min(n - done, main_rows - off)
            main_a[piece, off : off + size, :] = block[done : done + size].astype(bf16)
            done += size

    dh2_t = wide2[cols : cols + rows, 128:256].T
    low = lax.broadcasted_iota(jnp.int32, (64, 128), 1) < 64
    taps = []
    for a in range(3):
        g = dotf(dh2_t, wide1[a * cols : a * cols + rows, :])
        for b in range(3):
            g0 = g[0:64, b * 128 : (b + 1) * 128]
            g1v = g[64:128, b * 128 : (b + 1) * 128]
            if (3 * a + b) % 2 == 0:
                taps.append(g0 + pltpu.roll(g1v, 64, 1))
            else:
                taps.append(pltpu.roll(g0, 64, 1) + g1v)
    taps.append(jnp.zeros((64, 128), f32))
    for u in range(5):
        put_main(64 * u, jnp.where(low, taps[2 * u], taps[2 * u + 1]))
    put_main(320, expand[:, 0:128])
    put_main(384, expand[:, 128:256])
    low1 = lax.broadcasted_iota(jnp.int32, (1, 128), 1) < 64
    vec = jnp.concatenate(
        [
            sx3[:, 0:128], sx3[:, 128:256], sd3[:, 0:128], sd3[:, 128:256],
            jnp.where(low1, sx2, sd2), jnp.where(low1, sx1, sd1),
            jnp.zeros((2, 128), f32),
        ],
        axis=0,
    )
    vec_high = vec.astype(bf16)
    vec_low = vec - vec_high.astype(f32)
    put_main(VEC, jnp.concatenate([vec_high.astype(f32), vec_low], axis=0))
    put_main(VEC + 16, jnp.zeros((48, 128), f32))
    main_ra[end] = main_a[end]

    a_src, a_dst = (lambda t: main_a.at[t]), (lambda me: main_ra.at[me])
    spread_out(0, "a", a_src, a_dst)

    k0 = gain1 * istd1
    own_sd = sd1 * (1.0 / local)
    own_sx = sx1 * (1.0 / local)
    for p in range(4):
        dh1[p] = (k0 * (grad1[p] - own_sd - pre1[p] * own_sx)).astype(bf16)
    rest_t = dh1[...].reshape(rows, 128).T
    reduce = dotf(rest_t[0:64], img_v[0].reshape(rows, 256)) + dotf(
        rest_t[64:128], img_v[1].reshape(rows, 256)
    )
    for k in range(1, 3):
        f = lax.rem(s + k, spaces)
        pltpu.make_async_remote_copy(
            src_ref=cross.at[f], dst_ref=cross.at[f],
            send_sem=cs_sem.at[k], recv_sem=cr_sem.at[f],
            device_id=(d, f), device_id_type=MESH,
        ).wait_recv()
    excess = cross[s] * (1.0 / local) - (cross[0] + cross[1] + cross[2]) * (1.0 / count)

    def down(row):
        column = jnp.broadcast_to(row, (128, 128)).T[0:64]
        return jnp.concatenate([column, column], axis=1)

    reduce += down(k0 * sd1) * excess[64:65] + down(k0 * sx1) * excess[0:64]
    for h in range(2):
        for piece in range(ends):
            lo, hi = piece * late_rows, (piece + 1) * late_rows
            a, b = max(lo, 64 * h), min(hi, 64 * h + 64)
            if a < b:
                late_a[piece, a - lo : b - lo, :] = reduce[
                    a - 64 * h : b - 64 * h, 128 * h : 128 * h + 128
                ].astype(bf16)
    late_ra[end] = late_a[end]
    la_src, la_dst = (lambda t: late_a.at[t]), (lambda me: late_ra.at[me])
    spread_out(5, "a", la_src, la_dst)

    collect(0, "a", a_src, a_dst)
    part = added(main_ra, ends)
    sub = main_rows // ys
    for k in range(ys):
        main_b[k] = part[k * sub : (k + 1) * sub]
    main_rb[y] = main_b[y]
    b_src, b_dst = (lambda t: main_b.at[t]), (lambda me: main_rb.at[me])
    spread_out(1, "b", b_src, b_dst)

    sd, sx = sums(5, 128)
    k1 = k0 * sd * (1.0 / count)
    k2 = k0 * sx * (1.0 / count)

    def last(p, carry):
        dh = (k0 * grad1[p] - k1 - k2 * pre1[p]).astype(bf16)
        for q in range(2):
            r = 2 * p + q
            gi_v[r] = (dotf(dh, w_in[q]) + e3[r]).astype(bf16)
            pltpu.make_async_copy(gi_v.at[r], gimages.at[0, r], out_sem.at[1, r]).start()
        return carry

    lax.fori_loop(0, 2, last, 0)

    collect(5, "a", la_src, la_dst)
    late_b[y] = added(late_ra, ends).astype(bf16)
    lb_src, lb_dst = (lambda t: late_b.at[y]), (lambda me: late_b.at[me])
    spread_out(6, "b", lb_src, lb_dst)

    collect(1, "b", b_src, b_dst)
    main_c[z] = added(main_rb, ys)
    c_src, c_dst = (lambda t: main_c.at[z]), (lambda me: main_c.at[me])
    spread_out(2, "c", c_src, c_dst)

    lax.fori_loop(2, 4, last, 0)

    collect(6, "b", lb_src, lb_dst)
    late_c[z] = added(late_b, ys).astype(bf16)
    lc_src, lc_dst = (lambda t: late_c.at[z]), (lambda me: late_c.at[me])
    spread_out(7, "c", lc_src, lc_dst)

    collect(2, "c", c_src, c_dst)
    main_gb[y] = added(main_c, zs)
    gb_src, gb_dst = (lambda t: main_gb.at[y]), (lambda me: main_gb.at[me])
    spread_out(3, "b", gb_src, gb_dst)

    collect(7, "c", lc_src, lc_dst)
    late_ga[end] = added(late_c, zs).astype(bf16)
    lg_src, lg_dst = (lambda t: late_ga.at[end]), (lambda me: late_ga.at[me])
    spread_out(8, "a", lg_src, lg_dst)

    collect(3, "b", gb_src, gb_dst)
    whole = main_gb[...].reshape(main_rows, 128)
    main_ga[end] = whole.astype(bf16)

    @pl.when(end == VEC // main_rows)
    def _():
        at = VEC % main_rows
        v = whole[at : at + 8] + whole[at + 8 : at + 16]
        v_high = v.astype(bf16).astype(f32)
        main_ga[end, at : at + 16, :] = jnp.concatenate([v_high, v - v_high], axis=0).astype(bf16)

    ga_src, ga_dst = (lambda t: main_ga.at[end]), (lambda me: main_ga.at[me])
    spread_out(4, "a", ga_src, ga_dst)

    scale = 1.0 / lax.axis_size("dp")
    collect(8, "a", lg_src, lg_dst)
    late = late_ga[...].reshape(LATE_ROWS, 128).astype(f32) * scale
    o_reduce[:, 0:128] = late[0:64]
    o_reduce[:, 128:256] = late[64:128]

    collect(4, "a", ga_src, ga_dst)
    main = main_ga[...].reshape(MAIN_ROWS, 128).astype(f32) * scale
    for u in range(5):
        pair = main[64 * u : 64 * u + 64]
        pair = jnp.concatenate([pair, pair], axis=0).T
        o_dilated[2 * u] = pair[0:64, 0:64]
        if u < 4:
            o_dilated[2 * u + 1] = pair[64:128, 0:64]
    o_expand[:, 0:128] = main[320:384]
    o_expand[:, 128:256] = main[384:448]
    o_vec[...] = main[VEC : VEC + 8] + main[VEC + 8 : VEC + 16]

    outs = []
    for k, (src, dst) in enumerate(
        ((o_reduce, h_reduce), (o_dilated, h_dilated), (o_expand, h_expand), (o_vec, h_vec))
    ):
        outs.append(pltpu.make_async_copy(src, dst, out_sem.at[2, k]))
        outs[-1].start()

    for idx in range(6):
        for k in range(1, 3):
            pltpu.make_async_remote_copy(
                src_ref=xbuf.at[idx, s], dst_ref=xbuf.at[idx, s],
                send_sem=xs_sem.at[idx, k - 1], recv_sem=xr_sem.at[idx, s],
                device_id=(d, lax.rem(s + k, spaces)), device_id_type=MESH,
            ).wait_send()
    for k in range(1, 3):
        cross_copy(k).wait_send()
    end_halo(edge1, halo1, 0)
    end_halo(edge2, halo2, 1)
    for stage, name, src, dst in (
        (0, "a", a_src, a_dst), (1, "b", b_src, b_dst), (2, "c", c_src, c_dst),
        (3, "b", gb_src, gb_dst), (4, "a", ga_src, ga_dst), (5, "a", la_src, la_dst),
        (6, "b", lb_src, lb_dst), (7, "c", lc_src, lc_dst), (8, "a", lg_src, lg_dst),
    ):
        for k in range(1, groups[name][0]):
            copy_to(stage, name, src, dst, k).wait_send()
    for r in range(8):
        pltpu.make_async_copy(res_v.at[r], result.at[0, r], out_sem.at[0, r]).wait()
        pltpu.make_async_copy(gi_v.at[r], gimages.at[0, r], out_sem.at[1, r]).wait()
    for c in outs:
        c.wait()


def store(*refs):
    ins, outs, held, (half, full, sem) = refs[:6], refs[6:17], refs[17:23], refs[23:]
    vec = held[5]
    parts = []
    for k in range(2):
        for r in range(4):
            rows = pl.ds(2 * r, 2)
            parts.append((ins[k].at[0, rows], held[k].at[0, rows], outs[k].at[0, rows]))
    parts += [(ins[k], held[k], outs[k]) for k in range(2, 5)]
    fetches = [pltpu.make_async_copy(p[0], p[1], sem.at[0, k]) for k, p in enumerate(parts)]
    fetches.append(pltpu.make_async_copy(ins[5], vec, sem.at[0, 11]))
    for c in fetches:
        c.start()
    copies = []
    for k, p in enumerate(parts):
        fetches[k].wait()
        copies.append(pltpu.make_async_copy(p[1], p[2], sem.at[1, k]))
        copies[-1].start()
    fetches[-1].wait()
    for k, row in enumerate((5, 4)):
        v = vec[row : row + 1, :]
        half[2 * k] = v[:, 0:64]
        half[2 * k + 1] = pltpu.roll(jnp.broadcast_to(v, (8, 128)), 64, 1)[0:1, 0:64]
    for k in range(2):
        full[k] = jnp.concatenate([vec[2 * k : 2 * k + 1, :], vec[2 * k + 1 : 2 * k + 2, :]], axis=1)
    for k in range(4):
        copies.append(pltpu.make_async_copy(half.at[k], outs[5 + k], sem.at[1, 11 + k]))
        copies[-1].start()
    for k in range(2):
        copies.append(pltpu.make_async_copy(full.at[k], outs[9 + k], sem.at[1, 15 + k]))
        copies[-1].start()
    for c in copies:
        c.wait()


def solution(mesh):
    splits = SPLITS[mesh.shape["dp"]]
    ends, ys, highs = splits
    zs = highs * mesh.shape["space"]
    main_rows = MAIN_ROWS // ends
    late_rows = LATE_ROWS // ends
    sub = main_rows // ys

    def shards(images, wr, wd, we, g1, s1, g2, s2, g3, s3, cot):
        vmem = pl.BlockSpec(memory_space=pltpu.VMEM)
        hbm = pl.BlockSpec(memory_space=pltpu.HBM)
        big = jax.ShapeDtypeStruct(images.shape, bf16)
        maps = lambda: pltpu.VMEM((4, 288, 128), f32)
        outs = pl.pallas_call(
            functools.partial(kernel, splits),
            out_shape=(
                big, big,
                jax.ShapeDtypeStruct((64, 256), f32),
                jax.ShapeDtypeStruct((9, 64, 64), f32),
                jax.ShapeDtypeStruct((64, 256), f32),
                jax.ShapeDtypeStruct((8, 128), f32),
            ),
            in_specs=[hbm] * 11,
            out_specs=(hbm,) * 6,
            scratch_shapes=[
                pltpu.VMEM((8, 288, 256), bf16),
                pltpu.VMEM((8, 288, 256), bf16),
                pltpu.VMEM((64, 256), f32),
                pltpu.VMEM((9, 64, 64), f32),
                pltpu.VMEM((64, 256), f32),
                pltpu.VMEM((8, 128), f32),
                pltpu.VMEM((2, 4, 288, 256), bf16),
                pltpu.VMEM((8, 288, 256), bf16),
                pltpu.VMEM((64, 256), bf16),
                pltpu.VMEM((3, 3, 64, 64), bf16),
                pltpu.VMEM((64, 256), bf16),
                pltpu.VMEM((1, 64), f32), pltpu.VMEM((1, 64), f32),
                pltpu.VMEM((1, 64), f32), pltpu.VMEM((1, 64), f32),
                pltpu.VMEM((1, 256), f32), pltpu.VMEM((1, 256), f32),
                pltpu.VMEM((2, 128, 256), bf16),
                pltpu.VMEM((2, 128, 256), bf16),
                pltpu.VMEM((3, 384, 128), bf16),
                pltpu.VMEM((3, 128, 384), bf16),
                maps(), maps(), maps(), maps(),
                pltpu.VMEM((4, 288, 128), bf16),
                pltpu.VMEM((8, 288, 256), f32),
                pltpu.VMEM((8, 288, 256), f32),
                pltpu.VMEM((2, 4, 288, 256), bf16),
                maps(), maps(),
                pltpu.VMEM((4, 288, 128), bf16),
                pltpu.VMEM((2, 288, 128), bf16),
                pltpu.VMEM((2, 288, 128), bf16),
                pltpu.VMEM((2, 288, 128), bf16),
                pltpu.VMEM((2, 288, 128), bf16),
                pltpu.VMEM((6 * 288, 384), bf16),
                pltpu.VMEM((6 * 288, 384), bf16),
                pltpu.VMEM((6, 3, 8, 256), f32),
                pltpu.VMEM((3, 72, 256), f32),
                pltpu.VMEM((ends, main_rows, 128), bf16),
                pltpu.VMEM((ends, main_rows, 128), bf16),
                pltpu.VMEM((ys, sub, 128), f32),
                pltpu.VMEM((ys, sub, 128), f32),
                pltpu.VMEM((zs, sub, 128), f32),
                pltpu.VMEM((ys, sub, 128), f32),
                pltpu.VMEM((ends, main_rows, 128), bf16),
                pltpu.VMEM((ends, late_rows, 128), bf16),
                pltpu.VMEM((ends, late_rows, 128), bf16),
                pltpu.VMEM((ys, late_rows, 128), bf16),
                pltpu.VMEM((zs, late_rows, 128), bf16),
                pltpu.VMEM((ends, late_rows, 128), bf16),
                pltpu.SemaphoreType.DMA((18,)),
                pltpu.SemaphoreType.DMA((3, 8)),
                pltpu.SemaphoreType.DMA((2, 2)),
                pltpu.SemaphoreType.DMA((2, 2)),
                pltpu.SemaphoreType.DMA((6, 2)),
                pltpu.SemaphoreType.DMA((6, 3)),
                pltpu.SemaphoreType.DMA((3,)),
                pltpu.SemaphoreType.DMA((3,)),
                pltpu.SemaphoreType.DMA((9, 12)),
                pltpu.SemaphoreType.DMA((9, 12)),
            ],
            compiler_params=pltpu.CompilerParams(
                collective_id=0, has_side_effects=True, vmem_limit_bytes=60 * 1024 * 1024
            ),
        )(
            images, wr.T, wd, we,
            g1.reshape(1, 64), s1.reshape(1, 64), g2.reshape(1, 64), s2.reshape(1, 64),
            g3.reshape(1, 256), s3.reshape(1, 256), cot,
        )
        res, gi, g_reduce, g_dilated, g_expand, v1, v2, v3, v4, v5, v6 = pl.pallas_call(
            store,
            out_shape=tuple(jax.ShapeDtypeStruct(x.shape, x.dtype) for x in outs[:5])
            + (jax.ShapeDtypeStruct((1, 64), f32),) * 4
            + (jax.ShapeDtypeStruct((1, 256), f32),) * 2,
            in_specs=[hbm] * 6,
            out_specs=(hbm,) * 11,
            scratch_shapes=[pltpu.VMEM(x.shape, x.dtype) for x in outs] + [
                pltpu.VMEM((4, 1, 64), f32),
                pltpu.VMEM((2, 1, 256), f32),
                pltpu.SemaphoreType.DMA((2, 17)),
            ],
            compiler_params=pltpu.CompilerParams(vmem_limit_bytes=60 * 1024 * 1024),
        )(*outs)
        return (
            res, gi, g_reduce.T, g_dilated.reshape(3, 3, 64, 64), g_expand,
            v1.reshape(64), v2.reshape(64), v3.reshape(64), v4.reshape(64),
            v5.reshape(256), v6.reshape(256),
        )

    placed = (P("dp", "space", None, None),) + (P(),) * 9 + (P("dp", "space", None, None),)
    return jax.shard_map(
        shards,
        mesh=mesh,
        in_specs=placed,
        out_specs=(P("dp", "space", None, None),) * 2 + (P(),) * 9,
        check_vma=False,
    )
```

```python
import functools

import jax
import jax.numpy as jnp
from jax import lax
from jax.experimental import pallas as pl
from jax.experimental.pallas import tpu as pltpu
from jax.sharding import PartitionSpec as P

MESH = pl.DeviceIdType.MESH
f32 = jnp.float32
bf16 = jnp.bfloat16
epsilon = 1e-05

SPLITS = {256: (8, 8, 4), 4: (2, 2, 1)}
MAIN_ROWS = 512
LATE_ROWS = 128


def part_sum(x):
    n, lanes = x.shape
    return jnp.sum(x.reshape(n // 8, 8, lanes), axis=0)


def both(v8):
    v8 = v8 + pltpu.roll(v8, 64, 1)
    return jnp.sum(v8, axis=0, keepdims=True)


def total(v8):
    return jnp.sum(v8, axis=0, keepdims=True)


def gates(v):
    half = 0.5 * v
    t = jnp.tanh(half)
    act = half * t + half
    sig = 0.5 * t + 0.5
    slope = sig + act * (0.5 - 0.5 * t)
    return act, slope


def dotf(a, b):
    return jnp.dot(a, b, preferred_element_type=f32)


def dot_t(a, b):
    return lax.dot_general(a, b, (((1,), (1,)), ((), ())), preferred_element_type=f32)


def kernel(
    splits,
    images, wr_h, wd_h, we_h, g1_h, s1_h, g2_h, s2_h, g3_h, s3_h, cot,
    result, gimages, h_reduce, h_dilated, h_expand, h_vec,
    res_v, gi_v, o_reduce, o_dilated, o_expand, o_vec, img_v, cot_v, wr, wd, we, g1, s1, g2, s2, g3, s3,
    w_in, w_out, w_fwd, w_bwd,
    pre1, slope1, pre2, slope2, act2, x3, e3, dh3, grad2, grad1, dh1,
    edge1, edge2, edge3, halo1, halo2, halo3, wide1, wide2,
    xbuf, cross, cross2, excess1, excess2,
    main_a, main_ra, main_b, main_rb, main_c, main_gb, main_ga,
    late_a, late_ra, late_b, late_c, late_ga,
    vec_a, vec_b, vec_c,
    in_sem, out_sem, hs_sem, hr_sem, xs_sem, xr_sem, cs_sem, cr_sem, send_sem, recv_sem,
):
    ends, ys, highs = splits
    spaces = lax.axis_size("space")
    zs = highs * spaces
    d = lax.axis_index("dp")
    s = lax.axis_index("space")
    end = lax.rem(d, ends)
    upper = lax.rem(lax.div(d, ends), highs)
    y = lax.div(d, ends * highs)
    z = upper * spaces + s
    cols = 288
    before, after = s - 1, s + 1
    local = 2304.0
    count = local * spaces

    def id_a(k):
        return (d - end + k, s)

    def id_b(k):
        return (d + (k - y) * (ends * highs), s)

    def id_c(k):
        kh = lax.div(k, spaces)
        return (d + (kh - upper) * ends, lax.rem(k, spaces))

    groups = {"a": (ends, end, id_a), "b": (ys, y, id_b), "c": (zs, z, id_c)}

    in_copies = []
    for r in range(8):
        c = pltpu.make_async_copy(images.at[0, r], img_v.at[r % 2, r // 2], in_sem.at[r])
        c.start()
        in_copies.append(c)
    small = []
    pairs = (
        (wr_h, wr), (wd_h, wd), (we_h, we), (g1_h, g1), (s1_h, s1),
        (g2_h, g2), (s2_h, s2), (g3_h, g3), (s3_h, s3),
    )
    for k, (src, dst) in enumerate(pairs):
        c = pltpu.make_async_copy(src, dst, in_sem.at[9 + k])
        c.start()
        small.append(c)
    cot_copy = pltpu.make_async_copy(cot.at[0], cot_v, in_sem.at[8])
    cot_copy.start()

    barrier = pltpu.get_barrier_semaphore()
    partners = 0
    for name in "cba":
        n, me, ident = groups[name]
        for k in sorted(range(1, n), key=lambda k: -min(k, n - k)):
            pl.semaphore_signal(
                barrier, inc=1, device_id=ident(lax.rem(me + k, n)), device_id_type=MESH
            )
            partners += 1

    for c in small:
        c.wait()
    zero_out = jnp.zeros((64, 256), bf16)
    w_in[0] = jnp.concatenate([wr[...], zero_out], axis=0)
    w_in[1] = jnp.concatenate([zero_out, wr[...]], axis=0)
    w_out[0] = jnp.concatenate([we[...], zero_out], axis=0)
    w_out[1] = jnp.concatenate([zero_out, we[...]], axis=0)
    zero_mid = jnp.zeros((64, 64), bf16)
    for a in range(3):
        for b in range(3):
            w = wd[a, b]
            diag = jnp.concatenate(
                [
                    jnp.concatenate([w, zero_mid], axis=1),
                    jnp.concatenate([zero_mid, w], axis=1),
                ],
                axis=0,
            )
            w_fwd[a, b * 128 : (b + 1) * 128, :] = diag
            w_bwd[2 - a, :, (2 - b) * 128 : (3 - b) * 128] = diag

    @pl.when(s == 0)
    def _():
        wide1[0:cols, :] = jnp.zeros((cols, 384), bf16)
        wide2[0:cols, :] = jnp.zeros((cols, 384), bf16)

    @pl.when(s == spaces - 1)
    def _():
        wide1[5 * cols : 6 * cols, :] = jnp.zeros((cols, 384), bf16)
        wide2[5 * cols : 6 * cols, :] = jnp.zeros((cols, 384), bf16)

    def twice(ref):
        v = ref[...]
        return jnp.concatenate([v, v], axis=1)

    def send_stats(idx, first, second):
        lanes = first.shape[1]
        xbuf[idx, s, 0:1, 0:lanes] = first
        xbuf[idx, s, 1:2, 0:lanes] = second
        for k in range(1, 3):
            pltpu.make_async_remote_copy(
                src_ref=xbuf.at[idx, s],
                dst_ref=xbuf.at[idx, s],
                send_sem=xs_sem.at[idx, k - 1],
                recv_sem=xr_sem.at[idx, s],
                device_id=(d, lax.rem(s + k, spaces)),
                device_id_type=MESH,
            ).start()

    def wait_stats(idx, lanes):
        for k in range(1, 3):
            f = lax.rem(s + k, spaces)
            pltpu.make_async_remote_copy(
                src_ref=xbuf.at[idx, f],
                dst_ref=xbuf.at[idx, f],
                send_sem=xs_sem.at[idx, k - 1],
                recv_sem=xr_sem.at[idx, f],
                device_id=(d, f),
                device_id_type=MESH,
            ).wait_recv()
        firsts = [xbuf[idx, j, 0:1, 0:lanes] for j in range(3)]
        seconds = [xbuf[idx, j, 1:2, 0:lanes] for j in range(3)]
        return firsts, seconds

    def moments(idx, lanes):
        means, squares = wait_stats(idx, lanes)
        mu = (means[0] + means[1] + means[2]) * (1.0 / 3.0)
        spread = sum((m - mu) * (m - mu) for m in means)
        var = (squares[0] + squares[1] + squares[2] + local * spread) * (1.0 / count)
        return mu, lax.rsqrt(var + epsilon)

    def sums(idx, lanes):
        firsts, seconds = wait_stats(idx, lanes)
        return firsts[0] + firsts[1] + firsts[2], seconds[0] + seconds[1] + seconds[2]

    def halo(edge, halos, which):
        @pl.when(s > 0)
        def _():
            pltpu.make_async_remote_copy(
                src_ref=edge.at[0], dst_ref=halos.at[1],
                send_sem=hs_sem.at[which, 0], recv_sem=hr_sem.at[which, 1],
                device_id=(d, s - 1), device_id_type=MESH,
            ).start()

        @pl.when(s < spaces - 1)
        def _():
            pltpu.make_async_remote_copy(
                src_ref=edge.at[1], dst_ref=halos.at[0],
                send_sem=hs_sem.at[which, 1], recv_sem=hr_sem.at[which, 0],
                device_id=(d, s + 1), device_id_type=MESH,
            ).start()

    def widen(wide, pair, x):
        at = pair * cols
        spot = lax.broadcasted_iota(jnp.int32, (cols, 128), 0)
        left = jnp.where(spot >= 2, pltpu.roll(x, 2, 0), 0.0)
        right = jnp.where(spot < cols - 2, pltpu.roll(x, cols - 2, 0), 0.0)
        wide[at : at + cols, 0:128] = left.astype(bf16)
        wide[at : at + cols, 128:256] = x.astype(bf16)
        wide[at : at + cols, 256:384] = right.astype(bf16)

    def take_halo(edge, halos, wide, which, finish):
        @pl.when(s > 0)
        def _():
            pltpu.make_async_remote_copy(
                src_ref=edge.at[1], dst_ref=halos.at[0],
                send_sem=hs_sem.at[which, 0], recv_sem=hr_sem.at[which, 0],
                device_id=(d, s - 1), device_id_type=MESH,
            ).wait_recv()
            if wide is not None:
                widen(wide, 0, finish(halos[0].astype(f32), before))

        @pl.when(s < spaces - 1)
        def _():
            pltpu.make_async_remote_copy(
                src_ref=edge.at[0], dst_ref=halos.at[1],
                send_sem=hs_sem.at[which, 1], recv_sem=hr_sem.at[which, 1],
                device_id=(d, s + 1), device_id_type=MESH,
            ).wait_recv()
            if wide is not None:
                widen(wide, 5, finish(halos[1].astype(f32), after))

    def end_halo(edge, halos, which):
        @pl.when(s > 0)
        def _():
            pltpu.make_async_remote_copy(
                src_ref=edge.at[0], dst_ref=halos.at[1],
                send_sem=hs_sem.at[which, 0], recv_sem=hr_sem.at[which, 1],
                device_id=(d, s - 1), device_id_type=MESH,
            ).wait_send()

        @pl.when(s < spaces - 1)
        def _():
            pltpu.make_async_remote_copy(
                src_ref=edge.at[1], dst_ref=halos.at[0],
                send_sem=hs_sem.at[which, 1], recv_sem=hr_sem.at[which, 0],
                device_id=(d, s + 1), device_id_type=MESH,
            ).wait_send()

    def conv_fwd(pair, n):
        acc = dotf(wide1[pair * cols : (pair + n) * cols, :], w_fwd[0])
        for a in range(1, 3):
            acc += dotf(wide1[(pair + a) * cols : (pair + a + n) * cols, :], w_fwd[a])
        return acc

    def conv_bwd(pair, n):
        acc = dot_t(wide2[pair * cols : (pair + n) * cols, :], w_bwd[0])
        for a in range(1, 3):
            acc += dot_t(wide2[(pair + a) * cols : (pair + a + n) * cols, :], w_bwd[a])
        return acc

    def local_moments(idx, pre, acc, early=None):
        mean = both(acc) * (1.0 / local)
        if early is not None:
            early(mean)
        sq = jnp.zeros((8, 128), f32)
        for p in range(4):
            c = pre[p] - mean
            sq += part_sum(c * c)
        send_stats(idx, mean, both(sq))
        return mean

    def high_low(x):
        high = x.astype(bf16)
        low = (x - high.astype(f32)).astype(bf16)
        return high.T, low.T

    def folded(g):
        taps = []
        for t in range(9):
            a, b = divmod(t, 3)
            block = g[a][:, b * 128 : (b + 1) * 128]
            n = block.shape[0] // 2 if block.shape[0] > 8 else 8
            even, odd = block[0:n], block[block.shape[0] - n :]
            if t % 2 == 0:
                taps.append(even + pltpu.roll(odd, 64, 1))
            else:
                taps.append(pltpu.roll(even, 64, 1) + odd)
        taps.append(jnp.zeros_like(taps[0]))
        low = lax.broadcasted_iota(jnp.int32, taps[0].shape, 1) < 64
        return [jnp.where(low, taps[2 * u], taps[2 * u + 1]) for u in range(5)]

    def down(row):
        return jnp.broadcast_to(row, (128, 128)).T[0:64]

    def down2(row):
        return jnp.concatenate([down(row)] * 2, axis=1)

    def cross_copy(which, buf, k):
        return pltpu.make_async_remote_copy(
            src_ref=buf.at[s], dst_ref=buf.at[s],
            send_sem=cs_sem.at[which, k], recv_sem=cr_sem.at[which, s],
            device_id=(d, lax.rem(s + k, spaces)), device_id_type=MESH,
        )

    def take_cross(which, buf):
        for k in range(1, 3):
            f = lax.rem(s + k, spaces)
            pltpu.make_async_remote_copy(
                src_ref=buf.at[f], dst_ref=buf.at[f],
                send_sem=cs_sem.at[which, k], recv_sem=cr_sem.at[which, f],
                device_id=(d, f), device_id_type=MESH,
            ).wait_recv()

    rows = 4 * cols
    ones = jnp.ones((16, rows), bf16)

    def copy_to(stage, name, src, dst, k):
        n, me, ident = groups[name]
        t = lax.rem(me + k, n)
        return pltpu.make_async_remote_copy(
            src_ref=src(t), dst_ref=dst(me),
            send_sem=send_sem.at[stage, k], recv_sem=recv_sem.at[stage, me],
            device_id=ident(t), device_id_type=MESH,
        )

    def spread_out(stage, name, src, dst):
        for k in range(1, groups[name][0]):
            copy_to(stage, name, src, dst, k).start()

    def collect(stage, name, src, dst):
        n, me, ident = groups[name]
        for k in range(1, n):
            f = lax.rem(me + k, n)
            pltpu.make_async_remote_copy(
                src_ref=src(f), dst_ref=dst(f),
                send_sem=send_sem.at[stage, k], recv_sem=recv_sem.at[stage, f],
                device_id=ident(f), device_id_type=MESH,
            ).wait_recv()

    def added(ref, n):
        acc = ref[0].astype(f32)
        for k in range(1, n):
            acc += ref[k].astype(f32)
        return acc

    acc = jnp.zeros((8, 128), f32)
    for p in range(4):
        in_copies[2 * p].wait()
        in_copies[2 * p + 1].wait()
        v = dot_t(img_v[0, p], w_in[0]) + dot_t(img_v[1, p], w_in[1])
        pre1[p] = v
        acc += part_sum(v)
    gain1, shift1 = twice(g1), twice(s1)
    gain2, shift2 = twice(g2), twice(s2)
    pl.semaphore_wait(barrier, partners)

    def early(mean):
        edge1[0] = (pre1[0] - mean).astype(bf16)
        edge1[1] = (pre1[3] - mean).astype(bf16)
        halo(edge1, halo1, 0)

    mean1 = local_moments(0, pre1, acc, early)

    high, low = high_low(pre1[...].reshape(rows, 128) - mean1)
    crossed = jnp.zeros((144, 256), f32)
    for q in range(2):
        left = jnp.concatenate([high[64 * q : 64 * q + 64], low[64 * q : 64 * q + 64], ones], axis=0)
        crossed += dotf(left, img_v[q].reshape(rows, 256))
    cross[s, 0:64, :] = crossed[0:64] + crossed[64:128]
    cross[s, 64:72, :] = crossed[128:136]
    for k in range(1, 3):
        cross_copy(0, cross, k).start()
    mu1, istd1 = moments(0, 128)
    mu = mu1
    for p in range(4):
        xhat = (pre1[p] - mu) * istd1
        act, slope = gates(gain1 * xhat + shift1)
        pre1[p] = xhat
        slope1[p] = slope
        widen(wide1, p + 1, act)

    v = conv_fwd(1, 2)
    pre2[1] = v[0:cols]
    pre2[2] = v[cols : 2 * cols]
    acc = part_sum(v)

    def halo_act(c, f):
        xhat = (c + (xbuf[0, f, 0:1, 0:128] - mu1)) * istd1
        return gates(gain1 * xhat + shift1)[0]

    take_halo(edge1, halo1, wide1, 0, halo_act)
    for p in (0, 3):
        v = conv_fwd(p, 1)
        pre2[p] = v
        acc += part_sum(v)
    mean2 = local_moments(1, pre2, acc)

    high, low = high_low(pre2[...].reshape(rows, 128) - mean2)
    left = jnp.concatenate([high, low, ones], axis=0)
    crossed = [dotf(left, wide1[a * cols : a * cols + rows, :]) for a in range(3)]
    sides = folded([c[0:128] + c[128:256] for c in crossed])
    plain = folded([c[256:264] for c in crossed])
    for u in range(5):
        cross2[s, u, 0:64, :] = sides[u]
        cross2[s, u, 64:72, :] = plain[u]
    for k in range(1, 3):
        cross_copy(1, cross2, k).start()
    mu2, istd2 = moments(1, 128)
    mu = mu2
    acc3 = jnp.zeros((8, 256), f32)
    for p in range(4):
        xhat = (pre2[p] - mu) * istd2
        act, slope = gates(gain2 * xhat + shift2)
        pre2[p] = xhat
        slope2[p] = slope
        if p == 0:
            edge3[0] = xhat.astype(bf16)
        if p == 3:
            edge3[1] = xhat.astype(bf16)
        act = act.astype(bf16)
        act2[p] = act
        for q in range(2):
            v = dotf(act, w_out[q])
            x3[2 * p + q] = v
            acc3 += part_sum(v)

    mean = total(acc3) * (1.0 / local)

    def square(r, acc):
        c = x3[r] - mean
        return acc + part_sum(c * c)

    sq = lax.fori_loop(0, 8, square, jnp.zeros((8, 256), f32))
    send_stats(2, mean, total(sq))
    halo(edge3, halo3, 2)
    cot_copy.wait()
    gain3, shift3 = g3[...], s3[...]
    mu, istd3 = moments(2, 256)

    def third(r, carry):
        sd, sx = carry
        p, q = lax.div(r, 2), lax.rem(r, 2)
        xhat = (x3[r] - mu) * istd3
        act, slope = gates(gain3 * xhat + shift3 + img_v[q, p].astype(f32))
        res_v[r] = act.astype(bf16)
        pltpu.make_async_copy(res_v.at[r], result.at[0, r], out_sem.at[0, r]).start()
        e = cot_v[r].astype(f32) * slope
        x3[r] = xhat
        e3[r] = e
        return sd + part_sum(e), sx + part_sum(e * xhat)

    zero8 = jnp.zeros((8, 256), f32)
    sd, sx = lax.fori_loop(0, 8, third, (zero8, zero8))
    sd3, sx3 = total(sd), total(sx)
    send_stats(3, sd3, sx3)

    take_cross(0, cross)
    shifts = [down2(xbuf[0, j, 0:1, 0:128] - mu1) for j in range(3)]
    excess1[...] = cross[s] * (1.0 / local) - (cross[0] + cross[1] + cross[2]) * (1.0 / count)
    own = down2(xbuf[0, s, 0:1, 0:128] - mu1) * cross[s, 64:65, :]
    whole = sum(shifts[j] * cross[j, 64:65, :] for j in range(3))
    excess1[0:64, :] = down2(istd1) * (
        excess1[0:64, :] + own * (1.0 / local) - whole * (1.0 / count)
    )
    take_cross(1, cross2)
    shifts = [down(xbuf[1, j, 0:1, 0:128] - mu2) for j in range(3)]
    own_shift = down(xbuf[1, s, 0:1, 0:128] - mu2)
    scale2 = down(istd2)
    for u in range(5):
        excess2[u] = cross2[s, u] * (1.0 / local) - (
            cross2[0, u] + cross2[1, u] + cross2[2, u]
        ) * (1.0 / count)
        own = own_shift * cross2[s, u, 64:65, :]
        whole = sum(shifts[j] * cross2[j, u, 64:65, :] for j in range(3))
        excess2[u, 0:64, :] = scale2 * (
            excess2[u, 0:64, :] + own * (1.0 / local) - whole * (1.0 / count)
        )
    sd, sx = sums(3, 256)
    k0 = gain3 * istd3
    k1 = k0 * sd * (1.0 / count)
    k2 = k0 * sx * (1.0 / count)
    sd_acc = jnp.zeros((8, 128), f32)
    sx_acc = jnp.zeros((8, 128), f32)
    for p in range(4):
        for q in range(2):
            r = 2 * p + q
            dh3[q, p] = (k0 * e3[r] - k1 - k2 * x3[r]).astype(bf16)
        back = dot_t(dh3[0, p], w_out[0]) + dot_t(dh3[1, p], w_out[1])
        g = back * slope2[p]
        grad2[p] = g
        sd_acc += part_sum(g)
        sx_acc += part_sum(g * pre2[p])
    sd2, sx2 = both(sd_acc), both(sx_acc)
    send_stats(4, sd2, sx2)
    k0 = gain2 * istd2
    own_sd = sd2 * (1.0 / local)
    own_sx = sx2 * (1.0 / local)
    for p in (0, 3, 1, 2):
        rest = grad2[p] - own_sd - pre2[p] * own_sx
        if p == 0:
            edge2[0] = rest.astype(bf16)
        if p == 3:
            edge2[1] = rest.astype(bf16)
            halo(edge2, halo2, 1)
        dh1[p] = (k0 * rest).astype(bf16)

    main_rows = MAIN_ROWS // ends
    late_rows = LATE_ROWS // ends

    def put_main(row, block):
        n = block.shape[0]
        done = 0
        while done < n:
            piece, off = divmod(row + done, main_rows)
            size = min(n - done, main_rows - off)
            main_a[piece, off : off + size, :] = block[done : done + size].astype(bf16)
            done += size

    rest_t = dh1[...].reshape(rows, 128).T
    taps = folded([dotf(rest_t, wide1[a * cols : a * cols + rows, :]) for a in range(3)])
    by_sd, by_sx = down(k0 * sd2), down(k0 * sx2)
    for u in range(5):
        put_main(64 * u, taps[u] + by_sd * excess2[u, 64:65, :] + by_sx * excess2[u, 0:64, :])
    act_t = act2[...].reshape(rows, 128).T
    expand = dotf(act_t[0:64], dh3[0].reshape(rows, 256)) + dotf(
        act_t[64:128], dh3[1].reshape(rows, 256)
    )
    put_main(320, expand[:, 0:128])
    put_main(384, expand[:, 128:256])
    put_main(448, jnp.zeros((64, 128), f32))
    main_ra[end] = main_a[end]

    a_src, a_dst = (lambda t: main_a.at[t]), (lambda me: main_ra.at[me])
    spread_out(0, "a", a_src, a_dst)

    sd, sx = sums(4, 128)
    k1 = k0 * sd * (1.0 / count)
    k2 = k0 * sx * (1.0 / count)
    for p in range(4):
        widen(wide2, p + 1, k0 * grad2[p] - k1 - k2 * pre2[p])

    sd_acc = jnp.zeros((8, 128), f32)
    sx_acc = jnp.zeros((8, 128), f32)

    def first_back(p, v, sd_acc, sx_acc):
        g = v * slope1[p]
        grad1[p] = g
        return sd_acc + part_sum(g), sx_acc + part_sum(g * pre1[p])

    v = conv_bwd(1, 2)
    sd_acc, sx_acc = first_back(1, v[0:cols], sd_acc, sx_acc)
    sd_acc, sx_acc = first_back(2, v[cols : 2 * cols], sd_acc, sx_acc)
    take_halo(edge3, halo3, None, 2, None)

    def halo_grad(c, f):
        xhat = halo3[0 if f is before else 1].astype(f32)
        by_one = xbuf[4, f, 0:1, 0:128] * (1.0 / local) - sd * (1.0 / count)
        by_xhat = xbuf[4, f, 1:2, 0:128] * (1.0 / local) - sx * (1.0 / count)
        return k0 * (c + by_one + xhat * by_xhat)

    take_halo(edge2, halo2, wide2, 1, halo_grad)
    for p in (0, 3):
        sd_acc, sx_acc = first_back(p, conv_bwd(p, 1), sd_acc, sx_acc)
    sd1, sx1 = both(sd_acc), both(sx_acc)
    send_stats(5, sd1, sx1)

    k0 = gain1 * istd1
    own_sd = sd1 * (1.0 / local)
    own_sx = sx1 * (1.0 / local)
    for p in range(4):
        dh1[p] = (k0 * (grad1[p] - own_sd - pre1[p] * own_sx)).astype(bf16)
    rest_t = dh1[...].reshape(rows, 128).T
    reduce = dotf(rest_t[0:64], img_v[0].reshape(rows, 256)) + dotf(
        rest_t[64:128], img_v[1].reshape(rows, 256)
    )
    reduce += down2(k0 * sd1) * excess1[64:65, :] + down2(k0 * sx1) * excess1[0:64, :]
    for h in range(2):
        for piece in range(ends):
            lo, hi = piece * late_rows, (piece + 1) * late_rows
            a, b = max(lo, 64 * h), min(hi, 64 * h + 64)
            if a < b:
                late_a[piece, a - lo : b - lo, :] = reduce[
                    a - 64 * h : b - 64 * h, 128 * h : 128 * h + 128
                ].astype(bf16)
    late_ra[end] = late_a[end]
    la_src, la_dst = (lambda t: late_a.at[t]), (lambda me: late_ra.at[me])
    spread_out(5, "a", la_src, la_dst)

    low1 = lax.broadcasted_iota(jnp.int32, (1, 128), 1) < 64
    vec_a[end] = jnp.concatenate(
        [
            sx3[:, 0:128], sx3[:, 128:256], sd3[:, 0:128], sd3[:, 128:256],
            jnp.where(low1, sx2, sd2), jnp.where(low1, sx1, sd1),
            jnp.zeros((2, 128), f32),
        ],
        axis=0,
    )
    va_src, va_dst = (lambda t: vec_a.at[end]), (lambda me: vec_a.at[me])
    vb_src, vb_dst = (lambda t: vec_b.at[y]), (lambda me: vec_b.at[me])
    vc_src, vc_dst = (lambda t: vec_c.at[z]), (lambda me: vec_c.at[me])
    spread_out(9, "a", va_src, va_dst)

    collect(0, "a", a_src, a_dst)
    part = added(main_ra, ends)
    sub = main_rows // ys
    for k in range(ys):
        main_b[k] = part[k * sub : (k + 1) * sub]
    main_rb[y] = main_b[y]
    b_src, b_dst = (lambda t: main_b.at[t]), (lambda me: main_rb.at[me])
    spread_out(1, "b", b_src, b_dst)

    sd, sx = sums(5, 128)
    k1 = k0 * sd * (1.0 / count)
    k2 = k0 * sx * (1.0 / count)

    def last(p, carry):
        dh = (k0 * grad1[p] - k1 - k2 * pre1[p]).astype(bf16)
        for q in range(2):
            r = 2 * p + q
            gi_v[r] = (dotf(dh, w_in[q]) + e3[r]).astype(bf16)
            pltpu.make_async_copy(gi_v.at[r], gimages.at[0, r], out_sem.at[1, r]).start()
        return carry

    lax.fori_loop(0, 2, last, 0)

    collect(9, "a", va_src, va_dst)
    vec_b[y] = added(vec_a, ends)
    spread_out(10, "b", vb_src, vb_dst)
    collect(5, "a", la_src, la_dst)
    late_b[y] = added(late_ra, ends).astype(bf16)
    lb_src, lb_dst = (lambda t: late_b.at[y]), (lambda me: late_b.at[me])
    spread_out(6, "b", lb_src, lb_dst)

    collect(1, "b", b_src, b_dst)
    main_c[z] = added(main_rb, ys)
    c_src, c_dst = (lambda t: main_c.at[z]), (lambda me: main_c.at[me])
    spread_out(2, "c", c_src, c_dst)

    lax.fori_loop(2, 4, last, 0)

    collect(10, "b", vb_src, vb_dst)
    vec_c[z] = added(vec_b, ys)
    spread_out(11, "c", vc_src, vc_dst)
    collect(6, "b", lb_src, lb_dst)
    late_c[z] = added(late_b, ys).astype(bf16)
    lc_src, lc_dst = (lambda t: late_c.at[z]), (lambda me: late_c.at[me])
    spread_out(7, "c", lc_src, lc_dst)

    collect(2, "c", c_src, c_dst)
    main_gb[y] = added(main_c, zs)
    gb_src, gb_dst = (lambda t: main_gb.at[y]), (lambda me: main_gb.at[me])
    spread_out(3, "b", gb_src, gb_dst)

    collect(7, "c", lc_src, lc_dst)
    late_ga[end] = added(late_c, zs).astype(bf16)
    lg_src, lg_dst = (lambda t: late_ga.at[end]), (lambda me: late_ga.at[me])
    spread_out(8, "a", lg_src, lg_dst)

    collect(3, "b", gb_src, gb_dst)
    main_ga[end] = main_gb[...].reshape(main_rows, 128).astype(bf16)
    ga_src, ga_dst = (lambda t: main_ga.at[end]), (lambda me: main_ga.at[me])
    spread_out(4, "a", ga_src, ga_dst)

    scale = 1.0 / lax.axis_size("dp")
    collect(11, "c", vc_src, vc_dst)
    o_vec[...] = added(vec_c, zs) * scale
    collect(8, "a", lg_src, lg_dst)
    late = late_ga[...].reshape(LATE_ROWS, 128).astype(f32) * scale
    o_reduce[:, 0:128] = late[0:64]
    o_reduce[:, 128:256] = late[64:128]
    collect(4, "a", ga_src, ga_dst)
    main = main_ga[...].reshape(MAIN_ROWS, 128).astype(f32) * scale
    for u in range(5):
        pair = main[64 * u : 64 * u + 64]
        pair = jnp.concatenate([pair, pair], axis=0).T
        o_dilated[2 * u] = pair[0:64, 0:64]
        if u < 4:
            o_dilated[2 * u + 1] = pair[64:128, 0:64]
    o_expand[:, 0:128] = main[320:384]
    o_expand[:, 128:256] = main[384:448]
    outs = []
    for k, (src, dst) in enumerate(
        ((o_reduce, h_reduce), (o_dilated, h_dilated), (o_expand, h_expand), (o_vec, h_vec))
    ):
        outs.append(pltpu.make_async_copy(src, dst, out_sem.at[2, k]))
        outs[-1].start()

    for idx in range(6):
        for k in range(1, 3):
            pltpu.make_async_remote_copy(
                src_ref=xbuf.at[idx, s], dst_ref=xbuf.at[idx, s],
                send_sem=xs_sem.at[idx, k - 1], recv_sem=xr_sem.at[idx, s],
                device_id=(d, lax.rem(s + k, spaces)), device_id_type=MESH,
            ).wait_send()
    for k in range(1, 3):
        cross_copy(0, cross, k).wait_send()
        cross_copy(1, cross2, k).wait_send()
    end_halo(edge1, halo1, 0)
    end_halo(edge2, halo2, 1)
    end_halo(edge3, halo3, 2)
    for stage, name, src, dst in (
        (0, "a", a_src, a_dst), (1, "b", b_src, b_dst), (2, "c", c_src, c_dst),
        (3, "b", gb_src, gb_dst), (4, "a", ga_src, ga_dst), (5, "a", la_src, la_dst),
        (6, "b", lb_src, lb_dst), (7, "c", lc_src, lc_dst), (8, "a", lg_src, lg_dst),
        (9, "a", va_src, va_dst), (10, "b", vb_src, vb_dst), (11, "c", vc_src, vc_dst),
    ):
        for k in range(1, groups[name][0]):
            copy_to(stage, name, src, dst, k).wait_send()
    for r in range(8):
        pltpu.make_async_copy(res_v.at[r], result.at[0, r], out_sem.at[0, r]).wait()
        pltpu.make_async_copy(gi_v.at[r], gimages.at[0, r], out_sem.at[1, r]).wait()
    for c in outs:
        c.wait()


def store(*refs):
    ins, outs, held, (half, full, sem) = refs[:6], refs[6:17], refs[17:23], refs[23:]
    vec = held[5]
    parts = []
    for k in range(2):
        for r in range(4):
            rows = pl.ds(2 * r, 2)
            parts.append((ins[k].at[0, rows], held[k].at[0, rows], outs[k].at[0, rows]))
    parts += [(ins[k], held[k], outs[k]) for k in range(2, 5)]
    fetches = [pltpu.make_async_copy(p[0], p[1], sem.at[0, k]) for k, p in enumerate(parts)]
    fetches.append(pltpu.make_async_copy(ins[5], vec, sem.at[0, 11]))
    for c in fetches:
        c.start()
    copies = []
    for k, p in enumerate(parts):
        fetches[k].wait()
        copies.append(pltpu.make_async_copy(p[1], p[2], sem.at[1, k]))
        copies[-1].start()
    fetches[-1].wait()
    for k, row in enumerate((5, 4)):
        v = vec[row : row + 1, :]
        half[2 * k] = v[:, 0:64]
        half[2 * k + 1] = pltpu.roll(jnp.broadcast_to(v, (8, 128)), 64, 1)[0:1, 0:64]
    for k in range(2):
        full[k] = jnp.concatenate([vec[2 * k : 2 * k + 1, :], vec[2 * k + 1 : 2 * k + 2, :]], axis=1)
    for k in range(4):
        copies.append(pltpu.make_async_copy(half.at[k], outs[5 + k], sem.at[1, 11 + k]))
        copies[-1].start()
    for k in range(2):
        copies.append(pltpu.make_async_copy(full.at[k], outs[9 + k], sem.at[1, 15 + k]))
        copies[-1].start()
    for c in copies:
        c.wait()


def solution(mesh):
    splits = SPLITS[mesh.shape["dp"]]
    ends, ys, highs = splits
    zs = highs * mesh.shape["space"]
    main_rows = MAIN_ROWS // ends
    late_rows = LATE_ROWS // ends
    sub = main_rows // ys

    def shards(images, wr, wd, we, g1, s1, g2, s2, g3, s3, cot):
        vmem = pl.BlockSpec(memory_space=pltpu.VMEM)
        hbm = pl.BlockSpec(memory_space=pltpu.HBM)
        big = jax.ShapeDtypeStruct(images.shape, bf16)
        maps = lambda: pltpu.VMEM((4, 288, 128), f32)
        outs = pl.pallas_call(
            functools.partial(kernel, splits),
            out_shape=(
                big, big,
                jax.ShapeDtypeStruct((64, 256), f32),
                jax.ShapeDtypeStruct((9, 64, 64), f32),
                jax.ShapeDtypeStruct((64, 256), f32),
                jax.ShapeDtypeStruct((8, 128), f32),
            ),
            in_specs=[hbm] * 11,
            out_specs=(hbm,) * 6,
            scratch_shapes=[
                pltpu.VMEM((8, 288, 256), bf16),
                pltpu.VMEM((8, 288, 256), bf16),
                pltpu.VMEM((64, 256), f32),
                pltpu.VMEM((9, 64, 64), f32),
                pltpu.VMEM((64, 256), f32),
                pltpu.VMEM((8, 128), f32),
                pltpu.VMEM((2, 4, 288, 256), bf16),
                pltpu.VMEM((8, 288, 256), bf16),
                pltpu.VMEM((64, 256), bf16),
                pltpu.VMEM((3, 3, 64, 64), bf16),
                pltpu.VMEM((64, 256), bf16),
                pltpu.VMEM((1, 64), f32), pltpu.VMEM((1, 64), f32),
                pltpu.VMEM((1, 64), f32), pltpu.VMEM((1, 64), f32),
                pltpu.VMEM((1, 256), f32), pltpu.VMEM((1, 256), f32),
                pltpu.VMEM((2, 128, 256), bf16),
                pltpu.VMEM((2, 128, 256), bf16),
                pltpu.VMEM((3, 384, 128), bf16),
                pltpu.VMEM((3, 128, 384), bf16),
                maps(), maps(), maps(), maps(),
                pltpu.VMEM((4, 288, 128), bf16),
                pltpu.VMEM((8, 288, 256), f32),
                pltpu.VMEM((8, 288, 256), f32),
                pltpu.VMEM((2, 4, 288, 256), bf16),
                maps(), maps(),
                pltpu.VMEM((4, 288, 128), bf16),
                pltpu.VMEM((2, 288, 128), bf16),
                pltpu.VMEM((2, 288, 128), bf16),
                pltpu.VMEM((2, 288, 128), bf16),
                pltpu.VMEM((2, 288, 128), bf16),
                pltpu.VMEM((2, 288, 128), bf16),
                pltpu.VMEM((2, 288, 128), bf16),
                pltpu.VMEM((6 * 288, 384), bf16),
                pltpu.VMEM((6 * 288, 384), bf16),
                pltpu.VMEM((6, 3, 8, 256), f32),
                pltpu.VMEM((3, 72, 256), f32),
                pltpu.VMEM((3, 5, 72, 128), f32),
                pltpu.VMEM((72, 256), f32),
                pltpu.VMEM((5, 72, 128), f32),
                pltpu.VMEM((ends, main_rows, 128), bf16),
                pltpu.VMEM((ends, main_rows, 128), bf16),
                pltpu.VMEM((ys, sub, 128), f32),
                pltpu.VMEM((ys, sub, 128), f32),
                pltpu.VMEM((zs, sub, 128), f32),
                pltpu.VMEM((ys, sub, 128), f32),
                pltpu.VMEM((ends, main_rows, 128), bf16),
                pltpu.VMEM((ends, late_rows, 128), bf16),
                pltpu.VMEM((ends, late_rows, 128), bf16),
                pltpu.VMEM((ys, late_rows, 128), bf16),
                pltpu.VMEM((zs, late_rows, 128), bf16),
                pltpu.VMEM((ends, late_rows, 128), bf16),
                pltpu.VMEM((ends, 8, 128), f32),
                pltpu.VMEM((ys, 8, 128), f32),
                pltpu.VMEM((zs, 8, 128), f32),
                pltpu.SemaphoreType.DMA((18,)),
                pltpu.SemaphoreType.DMA((3, 8)),
                pltpu.SemaphoreType.DMA((3, 2)),
                pltpu.SemaphoreType.DMA((3, 2)),
                pltpu.SemaphoreType.DMA((6, 2)),
                pltpu.SemaphoreType.DMA((6, 3)),
                pltpu.SemaphoreType.DMA((2, 3)),
                pltpu.SemaphoreType.DMA((2, 3)),
                pltpu.SemaphoreType.DMA((12, 12)),
                pltpu.SemaphoreType.DMA((12, 12)),
            ],
            compiler_params=pltpu.CompilerParams(
                collective_id=0, has_side_effects=True, vmem_limit_bytes=60 * 1024 * 1024
            ),
        )(
            images, wr.T, wd, we,
            g1.reshape(1, 64), s1.reshape(1, 64), g2.reshape(1, 64), s2.reshape(1, 64),
            g3.reshape(1, 256), s3.reshape(1, 256), cot,
        )
        res, gi, g_reduce, g_dilated, g_expand, v1, v2, v3, v4, v5, v6 = pl.pallas_call(
            store,
            out_shape=tuple(jax.ShapeDtypeStruct(x.shape, x.dtype) for x in outs[:5])
            + (jax.ShapeDtypeStruct((1, 64), f32),) * 4
            + (jax.ShapeDtypeStruct((1, 256), f32),) * 2,
            in_specs=[hbm] * 6,
            out_specs=(hbm,) * 11,
            scratch_shapes=[pltpu.VMEM(x.shape, x.dtype) for x in outs] + [
                pltpu.VMEM((4, 1, 64), f32),
                pltpu.VMEM((2, 1, 256), f32),
                pltpu.SemaphoreType.DMA((2, 17)),
            ],
            compiler_params=pltpu.CompilerParams(vmem_limit_bytes=60 * 1024 * 1024),
        )(*outs)
        return (
            res, gi, g_reduce.T, g_dilated.reshape(3, 3, 64, 64), g_expand,
            v1.reshape(64), v2.reshape(64), v3.reshape(64), v4.reshape(64),
            v5.reshape(256), v6.reshape(256),
        )

    placed = (P("dp", "space", None, None),) + (P(),) * 9 + (P("dp", "space", None, None),)
    return jax.shard_map(
        shards,
        mesh=mesh,
        in_specs=placed,
        out_specs=(P("dp", "space", None, None),) * 2 + (P(),) * 9,
        check_vma=False,
    )
```

```python
import functools

import jax
import jax.numpy as jnp
from jax import lax
from jax.experimental import pallas as pl
from jax.experimental.pallas import tpu as pltpu
from jax.sharding import PartitionSpec as P

MESH = pl.DeviceIdType.MESH
f32 = jnp.float32
bf16 = jnp.bfloat16
epsilon = 1e-05

SPLITS = {256: (8, 8, 4), 4: (2, 2, 1)}
MAIN_ROWS = 512
LATE_ROWS = 128


def part_sum(x):
    n, lanes = x.shape
    return jnp.sum(x.reshape(n // 8, 8, lanes), axis=0)


def both(v8):
    v8 = v8 + pltpu.roll(v8, 64, 1)
    return jnp.sum(v8, axis=0, keepdims=True)


def total(v8):
    return jnp.sum(v8, axis=0, keepdims=True)


def gates(v):
    half = 0.5 * v
    t = jnp.tanh(half)
    act = half * t + half
    sig = 0.5 * t + 0.5
    slope = sig + act * (0.5 - 0.5 * t)
    return act, slope


def dotf(a, b):
    return jnp.dot(a, b, preferred_element_type=f32)


def dot_t(a, b):
    return lax.dot_general(a, b, (((1,), (1,)), ((), ())), preferred_element_type=f32)


def kernel(
    splits,
    images, wr_h, wd_h, we_h, g1_h, s1_h, g2_h, s2_h, g3_h, s3_h, cot,
    result, gimages, h_reduce, h_dilated, h_expand, h_vec,
    res_v, gi_v, o_reduce, o_dilated, o_expand, o_vec, img_v, cot_v, wr, wd, we, g1, s1, g2, s2, g3, s3,
    w_in, w_out, w_fwd, w_bwd,
    pre1, slope1, pre2, slope2, act2, x3, e3, dh3, grad2, grad1, dh1,
    edge1, edge2, edge3, halo1, halo2, halo3, wide1, wide2,
    xbuf, cross, cross2, excess1, excess2,
    main_a, main_ra, main_b, main_rb, main_c, main_gb, main_ga,
    late_a, late_ra, late_b, late_c, late_ga,
    in_sem, out_sem, hs_sem, hr_sem, xs_sem, xr_sem, cs_sem, cr_sem, send_sem, recv_sem,
):
    ends, ys, highs = splits
    spaces = lax.axis_size("space")
    zs = highs * spaces
    d = lax.axis_index("dp")
    s = lax.axis_index("space")
    end = lax.rem(d, ends)
    upper = lax.rem(lax.div(d, ends), highs)
    y = lax.div(d, ends * highs)
    z = upper * spaces + s
    cols = 288
    before, after = s - 1, s + 1
    local = 2304.0
    count = local * spaces

    def id_a(k):
        return (d - end + k, s)

    def id_b(k):
        return (d + (k - y) * (ends * highs), s)

    def id_c(k):
        kh = lax.div(k, spaces)
        return (d + (kh - upper) * ends, lax.rem(k, spaces))

    groups = {"a": (ends, end, id_a), "b": (ys, y, id_b), "c": (zs, z, id_c)}

    in_copies = []
    for r in range(8):
        c = pltpu.make_async_copy(images.at[0, r], img_v.at[r % 2, r // 2], in_sem.at[r])
        c.start()
        in_copies.append(c)
    small = []
    pairs = (
        (wr_h, wr), (wd_h, wd), (we_h, we), (g1_h, g1), (s1_h, s1),
        (g2_h, g2), (s2_h, s2), (g3_h, g3), (s3_h, s3),
    )
    for k, (src, dst) in enumerate(pairs):
        c = pltpu.make_async_copy(src, dst, in_sem.at[9 + k])
        c.start()
        small.append(c)
    cot_copy = pltpu.make_async_copy(cot.at[0], cot_v, in_sem.at[8])
    cot_copy.start()

    barrier = pltpu.get_barrier_semaphore()
    partners = 0
    for name in "cba":
        n, me, ident = groups[name]
        for k in sorted(range(1, n), key=lambda k: -min(k, n - k)):
            pl.semaphore_signal(
                barrier, inc=1, device_id=ident(lax.rem(me + k, n)), device_id_type=MESH
            )
            partners += 1

    for c in small:
        c.wait()
    zero_out = jnp.zeros((64, 256), bf16)
    w_in[0] = jnp.concatenate([wr[...], zero_out], axis=0)
    w_in[1] = jnp.concatenate([zero_out, wr[...]], axis=0)
    def twice(ref):
        v = ref[...]
        return jnp.concatenate([v, v], axis=1)

    def send_stats(idx, first, second):
        lanes = first.shape[1]
        xbuf[idx, s, 0:1, 0:lanes] = first
        xbuf[idx, s, 1:2, 0:lanes] = second
        for k in range(1, 3):
            pltpu.make_async_remote_copy(
                src_ref=xbuf.at[idx, s],
                dst_ref=xbuf.at[idx, s],
                send_sem=xs_sem.at[idx, k - 1],
                recv_sem=xr_sem.at[idx, s],
                device_id=(d, lax.rem(s + k, spaces)),
                device_id_type=MESH,
            ).start()

    def wait_stats(idx, lanes):
        for k in range(1, 3):
            f = lax.rem(s + k, spaces)
            pltpu.make_async_remote_copy(
                src_ref=xbuf.at[idx, f],
                dst_ref=xbuf.at[idx, f],
                send_sem=xs_sem.at[idx, k - 1],
                recv_sem=xr_sem.at[idx, f],
                device_id=(d, f),
                device_id_type=MESH,
            ).wait_recv()
        firsts = [xbuf[idx, j, 0:1, 0:lanes] for j in range(3)]
        seconds = [xbuf[idx, j, 1:2, 0:lanes] for j in range(3)]
        return firsts, seconds

    def moments(idx, lanes):
        means, squares = wait_stats(idx, lanes)
        mu = (means[0] + means[1] + means[2]) * (1.0 / 3.0)
        spread = sum((m - mu) * (m - mu) for m in means)
        var = (squares[0] + squares[1] + squares[2] + local * spread) * (1.0 / count)
        return mu, lax.rsqrt(var + epsilon)

    def sums(idx, lanes):
        firsts, seconds = wait_stats(idx, lanes)
        return firsts[0] + firsts[1] + firsts[2], seconds[0] + seconds[1] + seconds[2]

    def halo(edge, halos, which):
        @pl.when(s > 0)
        def _():
            pltpu.make_async_remote_copy(
                src_ref=edge.at[0], dst_ref=halos.at[1],
                send_sem=hs_sem.at[which, 0], recv_sem=hr_sem.at[which, 1],
                device_id=(d, s - 1), device_id_type=MESH,
            ).start()

        @pl.when(s < spaces - 1)
        def _():
            pltpu.make_async_remote_copy(
                src_ref=edge.at[1], dst_ref=halos.at[0],
                send_sem=hs_sem.at[which, 1], recv_sem=hr_sem.at[which, 0],
                device_id=(d, s + 1), device_id_type=MESH,
            ).start()

    def widen(wide, pair, x):
        at = pair * cols
        spot = lax.broadcasted_iota(jnp.int32, (cols, 128), 0)
        left = jnp.where(spot >= 2, pltpu.roll(x, 2, 0), 0.0)
        right = jnp.where(spot < cols - 2, pltpu.roll(x, cols - 2, 0), 0.0)
        wide[at : at + cols, 0:128] = left.astype(bf16)
        wide[at : at + cols, 128:256] = x.astype(bf16)
        wide[at : at + cols, 256:384] = right.astype(bf16)

    def take_halo(edge, halos, wide, which, finish):
        @pl.when(s > 0)
        def _():
            pltpu.make_async_remote_copy(
                src_ref=edge.at[1], dst_ref=halos.at[0],
                send_sem=hs_sem.at[which, 0], recv_sem=hr_sem.at[which, 0],
                device_id=(d, s - 1), device_id_type=MESH,
            ).wait_recv()
            if wide is not None:
                widen(wide, 0, finish(halos[0].astype(f32), before))

        @pl.when(s < spaces - 1)
        def _():
            pltpu.make_async_remote_copy(
                src_ref=edge.at[0], dst_ref=halos.at[1],
                send_sem=hs_sem.at[which, 1], recv_sem=hr_sem.at[which, 1],
                device_id=(d, s + 1), device_id_type=MESH,
            ).wait_recv()
            if wide is not None:
                widen(wide, 5, finish(halos[1].astype(f32), after))

    def end_halo(edge, halos, which):
        @pl.when(s > 0)
        def _():
            pltpu.make_async_remote_copy(
                src_ref=edge.at[0], dst_ref=halos.at[1],
                send_sem=hs_sem.at[which, 0], recv_sem=hr_sem.at[which, 1],
                device_id=(d, s - 1), device_id_type=MESH,
            ).wait_send()

        @pl.when(s < spaces - 1)
        def _():
            pltpu.make_async_remote_copy(
                src_ref=edge.at[1], dst_ref=halos.at[0],
                send_sem=hs_sem.at[which, 1], recv_sem=hr_sem.at[which, 0],
                device_id=(d, s + 1), device_id_type=MESH,
            ).wait_send()

    def conv_fwd(pair, n):
        acc = dotf(wide1[pair * cols : (pair + n) * cols, :], w_fwd[0])
        for a in range(1, 3):
            acc += dotf(wide1[(pair + a) * cols : (pair + a + n) * cols, :], w_fwd[a])
        return acc

    def conv_bwd(pair, n):
        acc = dot_t(wide2[pair * cols : (pair + n) * cols, :], w_bwd[0])
        for a in range(1, 3):
            acc += dot_t(wide2[(pair + a) * cols : (pair + a + n) * cols, :], w_bwd[a])
        return acc

    def local_moments(idx, pre, acc, early=None):
        mean = both(acc) * (1.0 / local)
        if early is not None:
            early(mean)
        sq = jnp.zeros((8, 128), f32)
        for p in range(4):
            c = pre[p] - mean
            sq += part_sum(c * c)
        send_stats(idx, mean, both(sq))
        return mean

    def high_low(x):
        high = x.astype(bf16)
        low = (x - high.astype(f32)).astype(bf16)
        return high.T, low.T

    def folded(g):
        taps = []
        for t in range(9):
            a, b = divmod(t, 3)
            block = g[a][:, b * 128 : (b + 1) * 128]
            n = block.shape[0] // 2 if block.shape[0] > 8 else 8
            even, odd = block[0:n], block[block.shape[0] - n :]
            if t % 2 == 0:
                taps.append(even + pltpu.roll(odd, 64, 1))
            else:
                taps.append(pltpu.roll(even, 64, 1) + odd)
        taps.append(jnp.zeros_like(taps[0]))
        low = lax.broadcasted_iota(jnp.int32, taps[0].shape, 1) < 64
        return [jnp.where(low, taps[2 * u], taps[2 * u + 1]) for u in range(5)]

    def down(row):
        return jnp.broadcast_to(row, (128, 128)).T[0:64]

    def down2(row):
        return jnp.concatenate([down(row)] * 2, axis=1)

    def cross_copy(which, buf, k):
        return pltpu.make_async_remote_copy(
            src_ref=buf.at[s], dst_ref=buf.at[s],
            send_sem=cs_sem.at[which, k], recv_sem=cr_sem.at[which, s],
            device_id=(d, lax.rem(s + k, spaces)), device_id_type=MESH,
        )

    def take_cross(which, buf):
        for k in range(1, 3):
            f = lax.rem(s + k, spaces)
            pltpu.make_async_remote_copy(
                src_ref=buf.at[f], dst_ref=buf.at[f],
                send_sem=cs_sem.at[which, k], recv_sem=cr_sem.at[which, f],
                device_id=(d, f), device_id_type=MESH,
            ).wait_recv()

    rows = 4 * cols
    ones = jnp.ones((16, rows), bf16)

    def copy_to(stage, name, src, dst, k):
        n, me, ident = groups[name]
        t = lax.rem(me + k, n)
        return pltpu.make_async_remote_copy(
            src_ref=src(t), dst_ref=dst(me),
            send_sem=send_sem.at[stage, k], recv_sem=recv_sem.at[stage, me],
            device_id=ident(t), device_id_type=MESH,
        )

    def spread_out(stage, name, src, dst):
        for k in range(1, groups[name][0]):
            copy_to(stage, name, src, dst, k).start()

    def collect(stage, name, src, dst):
        n, me, ident = groups[name]
        for k in range(1, n):
            f = lax.rem(me + k, n)
            pltpu.make_async_remote_copy(
                src_ref=src(f), dst_ref=dst(f),
                send_sem=send_sem.at[stage, k], recv_sem=recv_sem.at[stage, f],
                device_id=ident(f), device_id_type=MESH,
            ).wait_recv()

    def added(ref, n):
        acc = ref[0].astype(f32)
        for k in range(1, n):
            acc += ref[k].astype(f32)
        return acc

    acc = jnp.zeros((8, 128), f32)
    for p in range(4):
        in_copies[2 * p].wait()
        in_copies[2 * p + 1].wait()
        v = dot_t(img_v[0, p], w_in[0]) + dot_t(img_v[1, p], w_in[1])
        pre1[p] = v
        acc += part_sum(v)
    gain1, shift1 = twice(g1), twice(s1)
    gain2, shift2 = twice(g2), twice(s2)
    pl.semaphore_wait(barrier, partners)

    def early(mean):
        edge1[0] = (pre1[0] - mean).astype(bf16)
        edge1[1] = (pre1[3] - mean).astype(bf16)
        halo(edge1, halo1, 0)

    mean1 = local_moments(0, pre1, acc, early)

    w_out[0] = jnp.concatenate([we[...], zero_out], axis=0)
    w_out[1] = jnp.concatenate([zero_out, we[...]], axis=0)
    zero_mid = jnp.zeros((64, 64), bf16)
    for a in range(3):
        for b in range(3):
            w = wd[a, b]
            diag = jnp.concatenate(
                [
                    jnp.concatenate([w, zero_mid], axis=1),
                    jnp.concatenate([zero_mid, w], axis=1),
                ],
                axis=0,
            )
            w_fwd[a, b * 128 : (b + 1) * 128, :] = diag
            w_bwd[2 - a, :, (2 - b) * 128 : (3 - b) * 128] = diag

    @pl.when(s == 0)
    def _():
        wide1[0:cols, :] = jnp.zeros((cols, 384), bf16)
        wide2[0:cols, :] = jnp.zeros((cols, 384), bf16)

    @pl.when(s == spaces - 1)
    def _():
        wide1[5 * cols : 6 * cols, :] = jnp.zeros((cols, 384), bf16)
        wide2[5 * cols : 6 * cols, :] = jnp.zeros((cols, 384), bf16)

    high, low = high_low(pre1[...].reshape(rows, 128) - mean1)
    crossed = jnp.zeros((144, 256), f32)
    for q in range(2):
        left = jnp.concatenate([high[64 * q : 64 * q + 64], low[64 * q : 64 * q + 64], ones], axis=0)
        crossed += dotf(left, img_v[q].reshape(rows, 256))
    cross[s, 0:64, :] = crossed[0:64] + crossed[64:128]
    cross[s, 64:72, :] = crossed[128:136]
    for k in range(1, 3):
        cross_copy(0, cross, k).start()
    mu1, istd1 = moments(0, 128)
    mu = mu1
    for p in range(4):
        xhat = (pre1[p] - mu) * istd1
        act, slope = gates(gain1 * xhat + shift1)
        pre1[p] = xhat
        slope1[p] = slope
        widen(wide1, p + 1, act)

    v = conv_fwd(1, 2)
    pre2[1] = v[0:cols]
    pre2[2] = v[cols : 2 * cols]
    acc = part_sum(v)

    def halo_act(c, f):
        xhat = (c + (xbuf[0, f, 0:1, 0:128] - mu1)) * istd1
        return gates(gain1 * xhat + shift1)[0]

    take_halo(edge1, halo1, wide1, 0, halo_act)
    for p in (0, 3):
        v = conv_fwd(p, 1)
        pre2[p] = v
        acc += part_sum(v)
    mean2 = local_moments(1, pre2, acc)

    high, low = high_low(pre2[...].reshape(rows, 128) - mean2)
    left = jnp.concatenate([high, low, ones], axis=0)
    crossed = [dotf(left, wide1[a * cols : a * cols + rows, :]) for a in range(3)]
    sides = folded([c[0:128] + c[128:256] for c in crossed])
    plain = folded([c[256:264] for c in crossed])
    for u in range(5):
        cross2[s, u, 0:64, :] = sides[u]
        cross2[s, u, 64:72, :] = plain[u]
    mu2, istd2 = moments(1, 128)
    mu = mu2
    acc3 = jnp.zeros((8, 256), f32)
    for p in range(4):
        xhat = (pre2[p] - mu) * istd2
        act, slope = gates(gain2 * xhat + shift2)
        pre2[p] = xhat
        slope2[p] = slope
        if p == 0:
            edge3[0] = xhat.astype(bf16)
        if p == 3:
            edge3[1] = xhat.astype(bf16)
        act = act.astype(bf16)
        act2[p] = act
        for q in range(2):
            v = dotf(act, w_out[q])
            x3[2 * p + q] = v
            acc3 += part_sum(v)

    mean = total(acc3) * (1.0 / local)

    def square(r, acc):
        c = x3[r] - mean
        return acc + part_sum(c * c)

    sq = lax.fori_loop(0, 8, square, jnp.zeros((8, 256), f32))
    send_stats(2, mean, total(sq))
    halo(edge3, halo3, 2)
    for k in range(1, 3):
        cross_copy(1, cross2, k).start()
    cot_copy.wait()
    gain3, shift3 = g3[...], s3[...]
    mu, istd3 = moments(2, 256)

    def third(r, carry):
        sd, sx = carry
        p, q = lax.div(r, 2), lax.rem(r, 2)
        xhat = (x3[r] - mu) * istd3
        act, slope = gates(gain3 * xhat + shift3 + img_v[q, p].astype(f32))
        res_v[r] = act.astype(bf16)
        pltpu.make_async_copy(res_v.at[r], result.at[0, r], out_sem.at[0, r]).start()
        e = cot_v[r].astype(f32) * slope
        x3[r] = xhat
        e3[r] = e
        return sd + part_sum(e), sx + part_sum(e * xhat)

    zero8 = jnp.zeros((8, 256), f32)
    sd, sx = lax.fori_loop(0, 8, third, (zero8, zero8))
    sd3, sx3 = total(sd), total(sx)
    send_stats(3, sd3, sx3)

    take_cross(0, cross)
    shifts = [down2(xbuf[0, j, 0:1, 0:128] - mu1) for j in range(3)]
    excess1[...] = cross[s] * (1.0 / local) - (cross[0] + cross[1] + cross[2]) * (1.0 / count)
    own = down2(xbuf[0, s, 0:1, 0:128] - mu1) * cross[s, 64:65, :]
    whole = sum(shifts[j] * cross[j, 64:65, :] for j in range(3))
    excess1[0:64, :] = down2(istd1) * (
        excess1[0:64, :] + own * (1.0 / local) - whole * (1.0 / count)
    )
    take_cross(1, cross2)
    shifts = [down(xbuf[1, j, 0:1, 0:128] - mu2) for j in range(3)]
    own_shift = down(xbuf[1, s, 0:1, 0:128] - mu2)
    scale2 = down(istd2)
    for u in range(5):
        excess2[u] = cross2[s, u] * (1.0 / local) - (
            cross2[0, u] + cross2[1, u] + cross2[2, u]
        ) * (1.0 / count)
        own = own_shift * cross2[s, u, 64:65, :]
        whole = sum(shifts[j] * cross2[j, u, 64:65, :] for j in range(3))
        excess2[u, 0:64, :] = scale2 * (
            excess2[u, 0:64, :] + own * (1.0 / local) - whole * (1.0 / count)
        )
    sd, sx = sums(3, 256)
    k0 = gain3 * istd3
    k1 = k0 * sd * (1.0 / count)
    k2 = k0 * sx * (1.0 / count)
    sd_acc = jnp.zeros((8, 128), f32)
    sx_acc = jnp.zeros((8, 128), f32)
    for p in range(4):
        for q in range(2):
            r = 2 * p + q
            dh3[q, p] = (k0 * e3[r] - k1 - k2 * x3[r]).astype(bf16)
        back = dot_t(dh3[0, p], w_out[0]) + dot_t(dh3[1, p], w_out[1])
        g = back * slope2[p]
        grad2[p] = g
        sd_acc += part_sum(g)
        sx_acc += part_sum(g * pre2[p])
    sd2, sx2 = both(sd_acc), both(sx_acc)
    send_stats(4, sd2, sx2)
    k0 = gain2 * istd2
    own_sd = sd2 * (1.0 / local)
    own_sx = sx2 * (1.0 / local)
    for p in (0, 3, 1, 2):
        rest = grad2[p] - own_sd - pre2[p] * own_sx
        if p == 0:
            edge2[0] = rest.astype(bf16)
        if p == 3:
            edge2[1] = rest.astype(bf16)
            halo(edge2, halo2, 1)
        dh1[p] = (k0 * rest).astype(bf16)

    main_rows = MAIN_ROWS // ends
    late_rows = LATE_ROWS // ends

    def put_main(row, block):
        n = block.shape[0]
        done = 0
        while done < n:
            piece, off = divmod(row + done, main_rows)
            size = min(n - done, main_rows - off)
            main_a[piece, off : off + size, :] = block[done : done + size].astype(bf16)
            done += size

    rest_t = dh1[...].reshape(rows, 128).T
    taps = folded([dotf(rest_t, wide1[a * cols : a * cols + rows, :]) for a in range(3)])
    by_sd, by_sx = down(k0 * sd2), down(k0 * sx2)
    for u in range(5):
        put_main(64 * u, taps[u] + by_sd * excess2[u, 64:65, :] + by_sx * excess2[u, 0:64, :])
    act_t = act2[...].reshape(rows, 128).T
    expand = dotf(act_t[0:64], dh3[0].reshape(rows, 256)) + dotf(
        act_t[64:128], dh3[1].reshape(rows, 256)
    )
    put_main(320, expand[:, 0:128])
    put_main(384, expand[:, 128:256])
    put_main(448, jnp.zeros((64, 128), f32))
    main_ra[end] = main_a[end]

    a_src, a_dst = (lambda t: main_a.at[t]), (lambda me: main_ra.at[me])
    spread_out(0, "a", a_src, a_dst)

    sd, sx = sums(4, 128)
    k1 = k0 * sd * (1.0 / count)
    k2 = k0 * sx * (1.0 / count)
    for p in range(4):
        widen(wide2, p + 1, k0 * grad2[p] - k1 - k2 * pre2[p])

    sd_acc = jnp.zeros((8, 128), f32)
    sx_acc = jnp.zeros((8, 128), f32)

    def first_back(p, v, sd_acc, sx_acc):
        g = v * slope1[p]
        grad1[p] = g
        return sd_acc + part_sum(g), sx_acc + part_sum(g * pre1[p])

    v = conv_bwd(1, 2)
    sd_acc, sx_acc = first_back(1, v[0:cols], sd_acc, sx_acc)
    sd_acc, sx_acc = first_back(2, v[cols : 2 * cols], sd_acc, sx_acc)
    take_halo(edge3, halo3, None, 2, None)

    def halo_grad(c, f):
        xhat = halo3[0 if f is before else 1].astype(f32)
        by_one = xbuf[4, f, 0:1, 0:128] * (1.0 / local) - sd * (1.0 / count)
        by_xhat = xbuf[4, f, 1:2, 0:128] * (1.0 / local) - sx * (1.0 / count)
        return k0 * (c + by_one + xhat * by_xhat)

    take_halo(edge2, halo2, wide2, 1, halo_grad)
    for p in (0, 3):
        sd_acc, sx_acc = first_back(p, conv_bwd(p, 1), sd_acc, sx_acc)
    sd1, sx1 = both(sd_acc), both(sx_acc)
    send_stats(5, sd1, sx1)

    k0 = gain1 * istd1
    own_sd = sd1 * (1.0 / local)
    own_sx = sx1 * (1.0 / local)
    for p in range(4):
        dh1[p] = (k0 * (grad1[p] - own_sd - pre1[p] * own_sx)).astype(bf16)
    rest_t = dh1[...].reshape(rows, 128).T
    reduce = dotf(rest_t[0:64], img_v[0].reshape(rows, 256)) + dotf(
        rest_t[64:128], img_v[1].reshape(rows, 256)
    )
    reduce += down2(k0 * sd1) * excess1[64:65, :] + down2(k0 * sx1) * excess1[0:64, :]
    for h in range(2):
        for piece in range(ends):
            lo, hi = piece * late_rows, (piece + 1) * late_rows
            a, b = max(lo, 64 * h), min(hi, 64 * h + 64)
            if a < b:
                late_a[piece, a - lo : b - lo, :] = reduce[
                    a - 64 * h : b - 64 * h, 128 * h : 128 * h + 128
                ].astype(bf16)
    low1 = lax.broadcasted_iota(jnp.int32, (1, 128), 1) < 64
    vec = jnp.concatenate(
        [
            sx3[:, 0:128], sx3[:, 128:256], sd3[:, 0:128], sd3[:, 128:256],
            jnp.where(low1, sx2, sd2), jnp.where(low1, sx1, sd1),
            jnp.zeros((2, 128), f32),
        ],
        axis=0,
    )

    def parts(v):
        v_high = v.astype(bf16).astype(f32)
        return jnp.concatenate([v_high, v - v_high], axis=0).astype(bf16)

    def packed(v):
        at = late_rows
        return jnp.concatenate(
            [v[0:at].astype(bf16), parts(v[at : at + 8] + v[at + 8 : at + 16])], axis=0
        )

    vec = parts(vec)
    for piece in range(ends):
        late_a[piece, late_rows : late_rows + 16, :] = vec
    late_ra[end] = late_a[end]
    la_src, la_dst = (lambda t: late_a.at[t]), (lambda me: late_ra.at[me])
    spread_out(5, "a", la_src, la_dst)

    collect(0, "a", a_src, a_dst)
    part = added(main_ra, ends)
    sub = main_rows // ys
    for k in range(ys):
        main_b[k] = part[k * sub : (k + 1) * sub]
    main_rb[y] = main_b[y]
    b_src, b_dst = (lambda t: main_b.at[t]), (lambda me: main_rb.at[me])
    spread_out(1, "b", b_src, b_dst)

    sd, sx = sums(5, 128)
    k1 = k0 * sd * (1.0 / count)
    k2 = k0 * sx * (1.0 / count)

    def last(p, carry):
        dh = (k0 * grad1[p] - k1 - k2 * pre1[p]).astype(bf16)
        for q in range(2):
            r = 2 * p + q
            gi_v[r] = (dotf(dh, w_in[q]) + e3[r]).astype(bf16)
            pltpu.make_async_copy(gi_v.at[r], gimages.at[0, r], out_sem.at[1, r]).start()
        return carry

    lax.fori_loop(0, 2, last, 0)

    collect(5, "a", la_src, la_dst)
    late_b[y] = packed(added(late_ra, ends))
    lb_src, lb_dst = (lambda t: late_b.at[y]), (lambda me: late_b.at[me])
    spread_out(6, "b", lb_src, lb_dst)

    collect(1, "b", b_src, b_dst)
    main_c[z] = added(main_rb, ys)
    c_src, c_dst = (lambda t: main_c.at[z]), (lambda me: main_c.at[me])
    spread_out(2, "c", c_src, c_dst)

    lax.fori_loop(2, 4, last, 0)

    collect(6, "b", lb_src, lb_dst)
    late_c[z] = packed(added(late_b, ys))
    lc_src, lc_dst = (lambda t: late_c.at[z]), (lambda me: late_c.at[me])
    spread_out(7, "c", lc_src, lc_dst)

    collect(2, "c", c_src, c_dst)
    main_gb[y] = added(main_c, zs)
    gb_src, gb_dst = (lambda t: main_gb.at[y]), (lambda me: main_gb.at[me])
    spread_out(3, "b", gb_src, gb_dst)

    collect(7, "c", lc_src, lc_dst)
    whole = added(late_c, zs)
    late_ga[end] = whole[0:late_rows].astype(bf16)
    lg_src, lg_dst = (lambda t: late_ga.at[end]), (lambda me: late_ga.at[me])
    spread_out(8, "a", lg_src, lg_dst)

    collect(3, "b", gb_src, gb_dst)
    main_ga[end] = main_gb[...].reshape(main_rows, 128).astype(bf16)
    ga_src, ga_dst = (lambda t: main_ga.at[end]), (lambda me: main_ga.at[me])
    spread_out(4, "a", ga_src, ga_dst)

    def sent(*stages):
        for stage, name, src, dst in stages:
            for k in range(1, groups[name][0]):
                copy_to(stage, name, src, dst, k).wait_send()

    for idx in range(6):
        for k in range(1, 3):
            pltpu.make_async_remote_copy(
                src_ref=xbuf.at[idx, s], dst_ref=xbuf.at[idx, s],
                send_sem=xs_sem.at[idx, k - 1], recv_sem=xr_sem.at[idx, s],
                device_id=(d, lax.rem(s + k, spaces)), device_id_type=MESH,
            ).wait_send()
    for k in range(1, 3):
        cross_copy(0, cross, k).wait_send()
        cross_copy(1, cross2, k).wait_send()
    end_halo(edge1, halo1, 0)
    end_halo(edge2, halo2, 1)
    end_halo(edge3, halo3, 2)
    sent(
        (0, "a", a_src, a_dst), (1, "b", b_src, b_dst), (2, "c", c_src, c_dst), (3, "b", gb_src, gb_dst),
        (5, "a", la_src, la_dst), (6, "b", lb_src, lb_dst), (7, "c", lc_src, lc_dst),
    )
    for r in range(8):
        pltpu.make_async_copy(res_v.at[r], result.at[0, r], out_sem.at[0, r]).wait()
        pltpu.make_async_copy(gi_v.at[r], gimages.at[0, r], out_sem.at[1, r]).wait()
    scale = 1.0 / lax.axis_size("dp")
    o_vec[...] = (whole[late_rows : late_rows + 8] + whole[late_rows + 8 : late_rows + 16]) * scale
    collect(8, "a", lg_src, lg_dst)
    late = late_ga[...].reshape(LATE_ROWS, 128).astype(f32) * scale
    o_reduce[:, 0:128] = late[0:64]
    o_reduce[:, 128:256] = late[64:128]
    collect(4, "a", ga_src, ga_dst)
    main = main_ga[...].reshape(MAIN_ROWS, 128).astype(f32) * scale
    for u in range(5):
        pair = main[64 * u : 64 * u + 64]
        pair = jnp.concatenate([pair, pair], axis=0).T
        o_dilated[2 * u] = pair[0:64, 0:64]
        if u < 4:
            o_dilated[2 * u + 1] = pair[64:128, 0:64]
    o_expand[:, 0:128] = main[320:384]
    o_expand[:, 128:256] = main[384:448]
    outs = []
    for k, (src, dst) in enumerate(
        ((o_reduce, h_reduce), (o_dilated, h_dilated), (o_expand, h_expand), (o_vec, h_vec))
    ):
        outs.append(pltpu.make_async_copy(src, dst, out_sem.at[2, k]))
        outs[-1].start()

    sent((4, "a", ga_src, ga_dst), (8, "a", lg_src, lg_dst))
    for c in outs:
        c.wait()


def store(*refs):
    ins, outs, held, (half, full, sem) = refs[:6], refs[6:17], refs[17:23], refs[23:]
    vec = held[5]
    parts = []
    for k in range(2):
        for r in range(4):
            rows = pl.ds(2 * r, 2)
            parts.append((ins[k].at[0, rows], held[k].at[0, rows], outs[k].at[0, rows]))
    parts += [(ins[k], held[k], outs[k]) for k in range(2, 5)]
    fetches = [pltpu.make_async_copy(p[0], p[1], sem.at[0, k]) for k, p in enumerate(parts)]
    fetches.append(pltpu.make_async_copy(ins[5], vec, sem.at[0, 11]))
    for c in fetches:
        c.start()
    copies = []
    for k, p in enumerate(parts):
        fetches[k].wait()
        copies.append(pltpu.make_async_copy(p[1], p[2], sem.at[1, k]))
        copies[-1].start()
    fetches[-1].wait()
    for k, row in enumerate((5, 4)):
        v = vec[row : row + 1, :]
        half[2 * k] = v[:, 0:64]
        half[2 * k + 1] = pltpu.roll(jnp.broadcast_to(v, (8, 128)), 64, 1)[0:1, 0:64]
    for k in range(2):
        full[k] = jnp.concatenate([vec[2 * k : 2 * k + 1, :], vec[2 * k + 1 : 2 * k + 2, :]], axis=1)
    for k in range(4):
        copies.append(pltpu.make_async_copy(half.at[k], outs[5 + k], sem.at[1, 11 + k]))
        copies[-1].start()
    for k in range(2):
        copies.append(pltpu.make_async_copy(full.at[k], outs[9 + k], sem.at[1, 15 + k]))
        copies[-1].start()
    for c in copies:
        c.wait()


def solution(mesh):
    splits = SPLITS[mesh.shape["dp"]]
    ends, ys, highs = splits
    zs = highs * mesh.shape["space"]
    main_rows = MAIN_ROWS // ends
    late_rows = LATE_ROWS // ends
    sub = main_rows // ys

    def shards(images, wr, wd, we, g1, s1, g2, s2, g3, s3, cot):
        vmem = pl.BlockSpec(memory_space=pltpu.VMEM)
        hbm = pl.BlockSpec(memory_space=pltpu.HBM)
        big = jax.ShapeDtypeStruct(images.shape, bf16)
        maps = lambda: pltpu.VMEM((4, 288, 128), f32)
        outs = pl.pallas_call(
            functools.partial(kernel, splits),
            out_shape=(
                big, big,
                jax.ShapeDtypeStruct((64, 256), f32),
                jax.ShapeDtypeStruct((9, 64, 64), f32),
                jax.ShapeDtypeStruct((64, 256), f32),
                jax.ShapeDtypeStruct((8, 128), f32),
            ),
            in_specs=[hbm] * 11,
            out_specs=(hbm,) * 6,
            scratch_shapes=[
                pltpu.VMEM((8, 288, 256), bf16),
                pltpu.VMEM((8, 288, 256), bf16),
                pltpu.VMEM((64, 256), f32),
                pltpu.VMEM((9, 64, 64), f32),
                pltpu.VMEM((64, 256), f32),
                pltpu.VMEM((8, 128), f32),
                pltpu.VMEM((2, 4, 288, 256), bf16),
                pltpu.VMEM((8, 288, 256), bf16),
                pltpu.VMEM((64, 256), bf16),
                pltpu.VMEM((3, 3, 64, 64), bf16),
                pltpu.VMEM((64, 256), bf16),
                pltpu.VMEM((1, 64), f32), pltpu.VMEM((1, 64), f32),
                pltpu.VMEM((1, 64), f32), pltpu.VMEM((1, 64), f32),
                pltpu.VMEM((1, 256), f32), pltpu.VMEM((1, 256), f32),
                pltpu.VMEM((2, 128, 256), bf16),
                pltpu.VMEM((2, 128, 256), bf16),
                pltpu.VMEM((3, 384, 128), bf16),
                pltpu.VMEM((3, 128, 384), bf16),
                maps(), maps(), maps(), maps(),
                pltpu.VMEM((4, 288, 128), bf16),
                pltpu.VMEM((8, 288, 256), f32),
                pltpu.VMEM((8, 288, 256), f32),
                pltpu.VMEM((2, 4, 288, 256), bf16),
                maps(), maps(),
                pltpu.VMEM((4, 288, 128), bf16),
                pltpu.VMEM((2, 288, 128), bf16),
                pltpu.VMEM((2, 288, 128), bf16),
                pltpu.VMEM((2, 288, 128), bf16),
                pltpu.VMEM((2, 288, 128), bf16),
                pltpu.VMEM((2, 288, 128), bf16),
                pltpu.VMEM((2, 288, 128), bf16),
                pltpu.VMEM((6 * 288, 384), bf16),
                pltpu.VMEM((6 * 288, 384), bf16),
                pltpu.VMEM((6, 3, 8, 256), f32),
                pltpu.VMEM((3, 72, 256), f32),
                pltpu.VMEM((3, 5, 72, 128), f32),
                pltpu.VMEM((72, 256), f32),
                pltpu.VMEM((5, 72, 128), f32),
                pltpu.VMEM((ends, main_rows, 128), bf16),
                pltpu.VMEM((ends, main_rows, 128), bf16),
                pltpu.VMEM((ys, sub, 128), f32),
                pltpu.VMEM((ys, sub, 128), f32),
                pltpu.VMEM((zs, sub, 128), f32),
                pltpu.VMEM((ys, sub, 128), f32),
                pltpu.VMEM((ends, main_rows, 128), bf16),
                pltpu.VMEM((ends, late_rows + 16, 128), bf16),
                pltpu.VMEM((ends, late_rows + 16, 128), bf16),
                pltpu.VMEM((ys, late_rows + 16, 128), bf16),
                pltpu.VMEM((zs, late_rows + 16, 128), bf16),
                pltpu.VMEM((ends, late_rows, 128), bf16),
                pltpu.SemaphoreType.DMA((18,)),
                pltpu.SemaphoreType.DMA((3, 8)),
                pltpu.SemaphoreType.DMA((3, 2)),
                pltpu.SemaphoreType.DMA((3, 2)),
                pltpu.SemaphoreType.DMA((6, 2)),
                pltpu.SemaphoreType.DMA((6, 3)),
                pltpu.SemaphoreType.DMA((2, 3)),
                pltpu.SemaphoreType.DMA((2, 3)),
                pltpu.SemaphoreType.DMA((9, 12)),
                pltpu.SemaphoreType.DMA((9, 12)),
            ],
            compiler_params=pltpu.CompilerParams(
                collective_id=0, has_side_effects=True, vmem_limit_bytes=60 * 1024 * 1024
            ),
        )(
            images, wr.T, wd, we,
            g1.reshape(1, 64), s1.reshape(1, 64), g2.reshape(1, 64), s2.reshape(1, 64),
            g3.reshape(1, 256), s3.reshape(1, 256), cot,
        )
        res, gi, g_reduce, g_dilated, g_expand, v1, v2, v3, v4, v5, v6 = pl.pallas_call(
            store,
            out_shape=tuple(jax.ShapeDtypeStruct(x.shape, x.dtype) for x in outs[:5])
            + (jax.ShapeDtypeStruct((1, 64), f32),) * 4
            + (jax.ShapeDtypeStruct((1, 256), f32),) * 2,
            in_specs=[hbm] * 6,
            out_specs=(hbm,) * 11,
            scratch_shapes=[pltpu.VMEM(x.shape, x.dtype) for x in outs] + [
                pltpu.VMEM((4, 1, 64), f32),
                pltpu.VMEM((2, 1, 256), f32),
                pltpu.SemaphoreType.DMA((2, 17)),
            ],
            compiler_params=pltpu.CompilerParams(vmem_limit_bytes=60 * 1024 * 1024),
        )(*outs)
        return (
            res, gi, g_reduce.T, g_dilated.reshape(3, 3, 64, 64), g_expand,
            v1.reshape(64), v2.reshape(64), v3.reshape(64), v4.reshape(64),
            v5.reshape(256), v6.reshape(256),
        )

    placed = (P("dp", "space", None, None),) + (P(),) * 9 + (P("dp", "space", None, None),)
    return jax.shard_map(
        shards,
        mesh=mesh,
        in_specs=placed,
        out_specs=(P("dp", "space", None, None),) * 2 + (P(),) * 9,
        check_vma=False,
    )
```

```python
import functools

import jax
import jax.numpy as jnp
from jax import lax
from jax.experimental import pallas as pl
from jax.experimental.pallas import tpu as pltpu
from jax.sharding import PartitionSpec as P

MESH = pl.DeviceIdType.MESH
f32 = jnp.float32
bf16 = jnp.bfloat16
epsilon = 1e-05

SPLITS = {256: (8, 8, 4), 4: (2, 2, 1)}
MAIN_ROWS = 512
LATE_ROWS = 128


def part_sum(x):
    n, lanes = x.shape
    return jnp.sum(x.reshape(n // 8, 8, lanes), axis=0)


def both(v8):
    v8 = v8 + pltpu.roll(v8, 64, 1)
    return jnp.sum(v8, axis=0, keepdims=True)


def total(v8):
    return jnp.sum(v8, axis=0, keepdims=True)


def gates(v):
    half = 0.5 * v
    t = jnp.tanh(half)
    act = half * t + half
    sig = 0.5 * t + 0.5
    slope = sig + act * (0.5 - 0.5 * t)
    return act, slope


def dotf(a, b):
    return jnp.dot(a, b, preferred_element_type=f32)


def dot_t(a, b):
    return lax.dot_general(a, b, (((1,), (1,)), ((), ())), preferred_element_type=f32)


def kernel(
    splits,
    images, wr_h, wd_h, we_h, g1_h, s1_h, g2_h, s2_h, g3_h, s3_h, cot,
    result, gimages, h_reduce, h_dilated, h_expand, h_vec,
    res_v, gi_v, o_reduce, o_dilated, o_expand, o_vec, img_v, cot_v, wr, wd, we, g1, s1, g2, s2, g3, s3,
    w_in, w_out, w_fwd, w_bwd,
    pre1, slope1, pre2, slope2, act2, x3, e3, dh3, grad2, grad1, dh1,
    edge1, edge2, edge3, halo1, halo2, halo3, wide1, wide2,
    xbuf, cross, cross2, excess1, excess2,
    main_a, main_ra, main_b, main_rb, main_c, main_gb, main_ga,
    late_a, late_ra, late_b, late_c, late_ga,
    in_sem, out_sem, hs_sem, hr_sem, xs_sem, xr_sem, cs_sem, cr_sem, send_sem, recv_sem,
):
    ends, ys, highs = splits
    spaces = lax.axis_size("space")
    zs = highs * spaces
    d = lax.axis_index("dp")
    s = lax.axis_index("space")
    end = lax.rem(d, ends)
    upper = lax.rem(lax.div(d, ends), highs)
    y = lax.div(d, ends * highs)
    z = upper * spaces + s
    cols = 288
    before, after = s - 1, s + 1
    local = 2304.0
    count = local * spaces

    def id_a(k):
        return (d - end + k, s)

    def id_b(k):
        return (d + (k - y) * (ends * highs), s)

    def id_c(k):
        kh = lax.div(k, spaces)
        return (d + (kh - upper) * ends, lax.rem(k, spaces))

    groups = {"a": (ends, end, id_a), "b": (ys, y, id_b), "c": (zs, z, id_c)}

    barrier = pltpu.get_barrier_semaphore()
    partners = 0
    for name in "cba":
        n, me, ident = groups[name]
        for k in sorted(range(1, n), key=lambda k: -min(k, n - k)):
            pl.semaphore_signal(
                barrier, inc=1, device_id=ident(lax.rem(me + k, n)), device_id_type=MESH
            )
            partners += 1

    in_copies = []
    for r in range(8):
        c = pltpu.make_async_copy(images.at[0, r], img_v.at[r % 2, r // 2], in_sem.at[r])
        c.start()
        in_copies.append(c)
    small = []
    pairs = (
        (wr_h, wr), (wd_h, wd), (we_h, we), (g1_h, g1), (s1_h, s1),
        (g2_h, g2), (s2_h, s2), (g3_h, g3), (s3_h, s3),
    )
    for k, (src, dst) in enumerate(pairs):
        c = pltpu.make_async_copy(src, dst, in_sem.at[9 + k])
        c.start()
        small.append(c)
    cot_copy = pltpu.make_async_copy(cot.at[0], cot_v, in_sem.at[8])
    cot_copy.start()

    for c in small:
        c.wait()
    zero_out = jnp.zeros((64, 256), bf16)
    w_in[0] = jnp.concatenate([wr[...], zero_out], axis=0)
    w_in[1] = jnp.concatenate([zero_out, wr[...]], axis=0)
    def twice(ref):
        v = ref[...]
        return jnp.concatenate([v, v], axis=1)

    def send_stats(idx, first, second):
        lanes = first.shape[1]
        xbuf[idx, s, 0:1, 0:lanes] = first
        xbuf[idx, s, 1:2, 0:lanes] = second
        for k in range(1, 3):
            pltpu.make_async_remote_copy(
                src_ref=xbuf.at[idx, s],
                dst_ref=xbuf.at[idx, s],
                send_sem=xs_sem.at[idx, k - 1],
                recv_sem=xr_sem.at[idx, s],
                device_id=(d, lax.rem(s + k, spaces)),
                device_id_type=MESH,
            ).start()

    def wait_stats(idx, lanes):
        for k in range(1, 3):
            f = lax.rem(s + k, spaces)
            pltpu.make_async_remote_copy(
                src_ref=xbuf.at[idx, f],
                dst_ref=xbuf.at[idx, f],
                send_sem=xs_sem.at[idx, k - 1],
                recv_sem=xr_sem.at[idx, f],
                device_id=(d, f),
                device_id_type=MESH,
            ).wait_recv()
        firsts = [xbuf[idx, j, 0:1, 0:lanes] for j in range(3)]
        seconds = [xbuf[idx, j, 1:2, 0:lanes] for j in range(3)]
        return firsts, seconds

    def moments(idx, lanes):
        means, squares = wait_stats(idx, lanes)
        mu = (means[0] + means[1] + means[2]) * (1.0 / 3.0)
        spread = sum((m - mu) * (m - mu) for m in means)
        var = (squares[0] + squares[1] + squares[2] + local * spread) * (1.0 / count)
        return mu, lax.rsqrt(var + epsilon)

    def sums(idx, lanes):
        firsts, seconds = wait_stats(idx, lanes)
        return firsts[0] + firsts[1] + firsts[2], seconds[0] + seconds[1] + seconds[2]

    def halo(edge, halos, which):
        @pl.when(s > 0)
        def _():
            pltpu.make_async_remote_copy(
                src_ref=edge.at[0], dst_ref=halos.at[1],
                send_sem=hs_sem.at[which, 0], recv_sem=hr_sem.at[which, 1],
                device_id=(d, s - 1), device_id_type=MESH,
            ).start()

        @pl.when(s < spaces - 1)
        def _():
            pltpu.make_async_remote_copy(
                src_ref=edge.at[1], dst_ref=halos.at[0],
                send_sem=hs_sem.at[which, 1], recv_sem=hr_sem.at[which, 0],
                device_id=(d, s + 1), device_id_type=MESH,
            ).start()

    def widen(wide, pair, x):
        at = pair * cols
        spot = lax.broadcasted_iota(jnp.int32, (cols, 128), 0)
        left = jnp.where(spot >= 2, pltpu.roll(x, 2, 0), 0.0)
        right = jnp.where(spot < cols - 2, pltpu.roll(x, cols - 2, 0), 0.0)
        wide[at : at + cols, 0:128] = left.astype(bf16)
        wide[at : at + cols, 128:256] = x.astype(bf16)
        wide[at : at + cols, 256:384] = right.astype(bf16)

    def take_halo(edge, halos, wide, which, finish):
        @pl.when(s > 0)
        def _():
            pltpu.make_async_remote_copy(
                src_ref=edge.at[1], dst_ref=halos.at[0],
                send_sem=hs_sem.at[which, 0], recv_sem=hr_sem.at[which, 0],
                device_id=(d, s - 1), device_id_type=MESH,
            ).wait_recv()
            if wide is not None:
                widen(wide, 0, finish(halos[0].astype(f32), before))

        @pl.when(s < spaces - 1)
        def _():
            pltpu.make_async_remote_copy(
                src_ref=edge.at[0], dst_ref=halos.at[1],
                send_sem=hs_sem.at[which, 1], recv_sem=hr_sem.at[which, 1],
                device_id=(d, s + 1), device_id_type=MESH,
            ).wait_recv()
            if wide is not None:
                widen(wide, 5, finish(halos[1].astype(f32), after))

    def end_halo(edge, halos, which):
        @pl.when(s > 0)
        def _():
            pltpu.make_async_remote_copy(
                src_ref=edge.at[0], dst_ref=halos.at[1],
                send_sem=hs_sem.at[which, 0], recv_sem=hr_sem.at[which, 1],
                device_id=(d, s - 1), device_id_type=MESH,
            ).wait_send()

        @pl.when(s < spaces - 1)
        def _():
            pltpu.make_async_remote_copy(
                src_ref=edge.at[1], dst_ref=halos.at[0],
                send_sem=hs_sem.at[which, 1], recv_sem=hr_sem.at[which, 0],
                device_id=(d, s + 1), device_id_type=MESH,
            ).wait_send()

    def conv_fwd(pair, n):
        acc = dotf(wide1[pair * cols : (pair + n) * cols, :], w_fwd[0])
        for a in range(1, 3):
            acc += dotf(wide1[(pair + a) * cols : (pair + a + n) * cols, :], w_fwd[a])
        return acc

    def conv_bwd(pair, n):
        acc = dot_t(wide2[pair * cols : (pair + n) * cols, :], w_bwd[0])
        for a in range(1, 3):
            acc += dot_t(wide2[(pair + a) * cols : (pair + a + n) * cols, :], w_bwd[a])
        return acc

    def local_moments(idx, pre, acc, early=None):
        mean = both(acc) * (1.0 / local)
        if early is not None:
            early(mean)
        sq = jnp.zeros((8, 128), f32)
        for p in range(4):
            c = pre[p] - mean
            sq += part_sum(c * c)
        send_stats(idx, mean, both(sq))
        return mean

    def high_low(x):
        high = x.astype(bf16)
        low = (x - high.astype(f32)).astype(bf16)
        return high.T, low.T

    def folded(g):
        taps = []
        for t in range(9):
            a, b = divmod(t, 3)
            block = g[a][:, b * 128 : (b + 1) * 128]
            n = block.shape[0] // 2 if block.shape[0] > 8 else 8
            even, odd = block[0:n], block[block.shape[0] - n :]
            if t % 2 == 0:
                taps.append(even + pltpu.roll(odd, 64, 1))
            else:
                taps.append(pltpu.roll(even, 64, 1) + odd)
        taps.append(jnp.zeros_like(taps[0]))
        low = lax.broadcasted_iota(jnp.int32, taps[0].shape, 1) < 64
        return [jnp.where(low, taps[2 * u], taps[2 * u + 1]) for u in range(5)]

    def down(row):
        return jnp.broadcast_to(row, (128, 128)).T[0:64]

    def down2(row):
        return jnp.concatenate([down(row)] * 2, axis=1)

    def cross_copy(which, buf, k):
        return pltpu.make_async_remote_copy(
            src_ref=buf.at[s], dst_ref=buf.at[s],
            send_sem=cs_sem.at[which, k], recv_sem=cr_sem.at[which, s],
            device_id=(d, lax.rem(s + k, spaces)), device_id_type=MESH,
        )

    def take_cross(which, buf):
        for k in range(1, 3):
            f = lax.rem(s + k, spaces)
            pltpu.make_async_remote_copy(
                src_ref=buf.at[f], dst_ref=buf.at[f],
                send_sem=cs_sem.at[which, k], recv_sem=cr_sem.at[which, f],
                device_id=(d, f), device_id_type=MESH,
            ).wait_recv()

    rows = 4 * cols
    ones = jnp.ones((16, rows), bf16)

    def copy_to(stage, name, src, dst, k):
        n, me, ident = groups[name]
        t = lax.rem(me + k, n)
        return pltpu.make_async_remote_copy(
            src_ref=src(t), dst_ref=dst(me),
            send_sem=send_sem.at[stage, k], recv_sem=recv_sem.at[stage, me],
            device_id=ident(t), device_id_type=MESH,
        )

    def spread_out(stage, name, src, dst):
        n = groups[name][0]
        for k in sorted(range(1, n), key=lambda k: -min(k, n - k)):
            copy_to(stage, name, src, dst, k).start()

    def collect(stage, name, src, dst):
        n, me, ident = groups[name]
        for k in range(1, n):
            f = lax.rem(me + k, n)
            pltpu.make_async_remote_copy(
                src_ref=src(f), dst_ref=dst(f),
                send_sem=send_sem.at[stage, k], recv_sem=recv_sem.at[stage, f],
                device_id=ident(f), device_id_type=MESH,
            ).wait_recv()

    def added(ref, n):
        acc = ref[0].astype(f32)
        for k in range(1, n):
            acc += ref[k].astype(f32)
        return acc

    acc = jnp.zeros((8, 128), f32)
    for p in range(4):
        in_copies[2 * p].wait()
        in_copies[2 * p + 1].wait()
        v = dot_t(img_v[0, p], w_in[0]) + dot_t(img_v[1, p], w_in[1])
        pre1[p] = v
        acc += part_sum(v)
    gain1, shift1 = twice(g1), twice(s1)
    gain2, shift2 = twice(g2), twice(s2)
    pl.semaphore_wait(barrier, partners)

    def early(mean):
        edge1[0] = (pre1[0] - mean).astype(bf16)
        edge1[1] = (pre1[3] - mean).astype(bf16)
        halo(edge1, halo1, 0)

    mean1 = local_moments(0, pre1, acc, early)

    w_out[0] = jnp.concatenate([we[...], zero_out], axis=0)
    w_out[1] = jnp.concatenate([zero_out, we[...]], axis=0)
    zero_mid = jnp.zeros((64, 64), bf16)
    for a in range(3):
        for b in range(3):
            w = wd[a, b]
            diag = jnp.concatenate(
                [
                    jnp.concatenate([w, zero_mid], axis=1),
                    jnp.concatenate([zero_mid, w], axis=1),
                ],
                axis=0,
            )
            w_fwd[a, b * 128 : (b + 1) * 128, :] = diag
            w_bwd[2 - a, :, (2 - b) * 128 : (3 - b) * 128] = diag

    @pl.when(s == 0)
    def _():
        wide1[0:cols, :] = jnp.zeros((cols, 384), bf16)
        wide2[0:cols, :] = jnp.zeros((cols, 384), bf16)

    @pl.when(s == spaces - 1)
    def _():
        wide1[5 * cols : 6 * cols, :] = jnp.zeros((cols, 384), bf16)
        wide2[5 * cols : 6 * cols, :] = jnp.zeros((cols, 384), bf16)

    high, low = high_low(pre1[...].reshape(rows, 128) - mean1)
    crossed = jnp.zeros((144, 256), f32)
    for q in range(2):
        left = jnp.concatenate([high[64 * q : 64 * q + 64], low[64 * q : 64 * q + 64], ones], axis=0)
        crossed += dotf(left, img_v[q].reshape(rows, 256))
    cross[s, 0:64, :] = crossed[0:64] + crossed[64:128]
    cross[s, 64:72, :] = crossed[128:136]
    for k in range(1, 3):
        cross_copy(0, cross, k).start()
    mu1, istd1 = moments(0, 128)
    mu = mu1
    for p in range(4):
        xhat = (pre1[p] - mu) * istd1
        act, slope = gates(gain1 * xhat + shift1)
        pre1[p] = xhat
        slope1[p] = slope
        widen(wide1, p + 1, act)

    v = conv_fwd(1, 2)
    pre2[1] = v[0:cols]
    pre2[2] = v[cols : 2 * cols]
    acc = part_sum(v)

    def halo_act(c, f):
        xhat = (c + (xbuf[0, f, 0:1, 0:128] - mu1)) * istd1
        return gates(gain1 * xhat + shift1)[0]

    take_halo(edge1, halo1, wide1, 0, halo_act)
    for p in (0, 3):
        v = conv_fwd(p, 1)
        pre2[p] = v
        acc += part_sum(v)
    mean2 = local_moments(1, pre2, acc)

    high, low = high_low(pre2[...].reshape(rows, 128) - mean2)
    left = jnp.concatenate([high, low, ones], axis=0)
    crossed = [dotf(left, wide1[a * cols : a * cols + rows, :]) for a in range(3)]
    sides = folded([c[0:128] + c[128:256] for c in crossed])
    plain = folded([c[256:264] for c in crossed])
    for u in range(5):
        cross2[s, u, 0:64, :] = sides[u]
        cross2[s, u, 64:72, :] = plain[u]
    mu2, istd2 = moments(1, 128)
    mu = mu2
    acc3 = jnp.zeros((8, 256), f32)
    for p in range(4):
        xhat = (pre2[p] - mu) * istd2
        act, slope = gates(gain2 * xhat + shift2)
        pre2[p] = xhat
        slope2[p] = slope
        if p == 0:
            edge3[0] = xhat.astype(bf16)
        if p == 3:
            edge3[1] = xhat.astype(bf16)
        act = act.astype(bf16)
        act2[p] = act
        for q in range(2):
            v = dotf(act, w_out[q])
            x3[2 * p + q] = v
            acc3 += part_sum(v)

    mean = total(acc3) * (1.0 / local)

    def square(r, acc):
        c = x3[r] - mean
        return acc + part_sum(c * c)

    sq = lax.fori_loop(0, 8, square, jnp.zeros((8, 256), f32), unroll=4)
    send_stats(2, mean, total(sq))
    halo(edge3, halo3, 2)
    for k in range(1, 3):
        cross_copy(1, cross2, k).start()
    cot_copy.wait()
    gain3, shift3 = g3[...], s3[...]
    mu, istd3 = moments(2, 256)

    def third(r, carry):
        sd, sx = carry
        p, q = lax.div(r, 2), lax.rem(r, 2)
        xhat = (x3[r] - mu) * istd3
        act, slope = gates(gain3 * xhat + shift3 + img_v[q, p].astype(f32))
        res_v[r] = act.astype(bf16)
        pltpu.make_async_copy(res_v.at[r], result.at[0, r], out_sem.at[0, r]).start()
        e = cot_v[r].astype(f32) * slope
        x3[r] = xhat
        e3[r] = e
        return sd + part_sum(e), sx + part_sum(e * xhat)

    zero8 = jnp.zeros((8, 256), f32)
    sd, sx = lax.fori_loop(0, 8, third, (zero8, zero8))
    sd3, sx3 = total(sd), total(sx)
    send_stats(3, sd3, sx3)

    take_cross(0, cross)
    shifts = [down2(xbuf[0, j, 0:1, 0:128] - mu1) for j in range(3)]
    excess1[...] = cross[s] * (1.0 / local) - (cross[0] + cross[1] + cross[2]) * (1.0 / count)
    own = down2(xbuf[0, s, 0:1, 0:128] - mu1) * cross[s, 64:65, :]
    whole = sum(shifts[j] * cross[j, 64:65, :] for j in range(3))
    excess1[0:64, :] = down2(istd1) * (
        excess1[0:64, :] + own * (1.0 / local) - whole * (1.0 / count)
    )
    take_cross(1, cross2)
    shifts = [down(xbuf[1, j, 0:1, 0:128] - mu2) for j in range(3)]
    own_shift = down(xbuf[1, s, 0:1, 0:128] - mu2)
    scale2 = down(istd2)
    for u in range(5):
        excess2[u] = cross2[s, u] * (1.0 / local) - (
            cross2[0, u] + cross2[1, u] + cross2[2, u]
        ) * (1.0 / count)
        own = own_shift * cross2[s, u, 64:65, :]
        whole = sum(shifts[j] * cross2[j, u, 64:65, :] for j in range(3))
        excess2[u, 0:64, :] = scale2 * (
            excess2[u, 0:64, :] + own * (1.0 / local) - whole * (1.0 / count)
        )
    sd, sx = sums(3, 256)
    k0 = gain3 * istd3
    k1 = k0 * sd * (1.0 / count)
    k2 = k0 * sx * (1.0 / count)
    sd_acc = jnp.zeros((8, 128), f32)
    sx_acc = jnp.zeros((8, 128), f32)
    for p in range(4):
        for q in range(2):
            r = 2 * p + q
            dh3[q, p] = (k0 * e3[r] - k1 - k2 * x3[r]).astype(bf16)
        back = dot_t(dh3[0, p], w_out[0]) + dot_t(dh3[1, p], w_out[1])
        g = back * slope2[p]
        grad2[p] = g
        sd_acc += part_sum(g)
        sx_acc += part_sum(g * pre2[p])
    sd2, sx2 = both(sd_acc), both(sx_acc)
    send_stats(4, sd2, sx2)
    k0 = gain2 * istd2
    own_sd = sd2 * (1.0 / local)
    own_sx = sx2 * (1.0 / local)
    for p in (0, 3, 1, 2):
        rest = grad2[p] - own_sd - pre2[p] * own_sx
        if p == 0:
            edge2[0] = rest.astype(bf16)
        if p == 3:
            edge2[1] = rest.astype(bf16)
            halo(edge2, halo2, 1)
        dh1[p] = (k0 * rest).astype(bf16)

    main_rows = MAIN_ROWS // ends
    late_rows = LATE_ROWS // ends

    def put_main(row, block):
        n = block.shape[0]
        done = 0
        while done < n:
            piece, off = divmod(row + done, main_rows)
            size = min(n - done, main_rows - off)
            main_a[piece, off : off + size, :] = block[done : done + size].astype(bf16)
            done += size

    rest_t = dh1[...].reshape(rows, 128).T
    taps = folded([dotf(rest_t, wide1[a * cols : a * cols + rows, :]) for a in range(3)])
    by_sd, by_sx = down(k0 * sd2), down(k0 * sx2)
    for u in range(5):
        put_main(64 * u, taps[u] + by_sd * excess2[u, 64:65, :] + by_sx * excess2[u, 0:64, :])
    act_t = act2[...].reshape(rows, 128).T
    expand = dotf(act_t[0:64], dh3[0].reshape(rows, 256)) + dotf(
        act_t[64:128], dh3[1].reshape(rows, 256)
    )
    put_main(320, expand[:, 0:128])
    put_main(384, expand[:, 128:256])
    put_main(448, jnp.zeros((64, 128), f32))
    main_ra[end] = main_a[end]

    a_src, a_dst = (lambda t: main_a.at[t]), (lambda me: main_ra.at[me])
    spread_out(0, "a", a_src, a_dst)

    sd, sx = sums(4, 128)
    k1 = k0 * sd * (1.0 / count)
    k2 = k0 * sx * (1.0 / count)
    for p in range(4):
        widen(wide2, p + 1, k0 * grad2[p] - k1 - k2 * pre2[p])

    sd_acc = jnp.zeros((8, 128), f32)
    sx_acc = jnp.zeros((8, 128), f32)

    def first_back(p, v, sd_acc, sx_acc):
        g = v * slope1[p]
        grad1[p] = g
        return sd_acc + part_sum(g), sx_acc + part_sum(g * pre1[p])

    v = conv_bwd(1, 2)
    sd_acc, sx_acc = first_back(1, v[0:cols], sd_acc, sx_acc)
    sd_acc, sx_acc = first_back(2, v[cols : 2 * cols], sd_acc, sx_acc)
    take_halo(edge3, halo3, None, 2, None)

    def halo_grad(c, f):
        xhat = halo3[0 if f is before else 1].astype(f32)
        by_one = xbuf[4, f, 0:1, 0:128] * (1.0 / local) - sd * (1.0 / count)
        by_xhat = xbuf[4, f, 1:2, 0:128] * (1.0 / local) - sx * (1.0 / count)
        return k0 * (c + by_one + xhat * by_xhat)

    take_halo(edge2, halo2, wide2, 1, halo_grad)
    for p in (0, 3):
        sd_acc, sx_acc = first_back(p, conv_bwd(p, 1), sd_acc, sx_acc)
    sd1, sx1 = both(sd_acc), both(sx_acc)
    send_stats(5, sd1, sx1)

    k0 = gain1 * istd1
    own_sd = sd1 * (1.0 / local)
    own_sx = sx1 * (1.0 / local)
    for p in range(4):
        dh1[p] = (k0 * (grad1[p] - own_sd - pre1[p] * own_sx)).astype(bf16)
    rest_t = dh1[...].reshape(rows, 128).T
    reduce = dotf(rest_t[0:64], img_v[0].reshape(rows, 256)) + dotf(
        rest_t[64:128], img_v[1].reshape(rows, 256)
    )
    reduce += down2(k0 * sd1) * excess1[64:65, :] + down2(k0 * sx1) * excess1[0:64, :]
    for h in range(2):
        for piece in range(ends):
            lo, hi = piece * late_rows, (piece + 1) * late_rows
            a, b = max(lo, 64 * h), min(hi, 64 * h + 64)
            if a < b:
                late_a[piece, a - lo : b - lo, :] = reduce[
                    a - 64 * h : b - 64 * h, 128 * h : 128 * h + 128
                ].astype(bf16)
    low1 = lax.broadcasted_iota(jnp.int32, (1, 128), 1) < 64
    vec = jnp.concatenate(
        [
            sx3[:, 0:128], sx3[:, 128:256], sd3[:, 0:128], sd3[:, 128:256],
            jnp.where(low1, sx2, sd2), jnp.where(low1, sx1, sd1),
            jnp.zeros((2, 128), f32),
        ],
        axis=0,
    )

    def parts(v):
        v_high = v.astype(bf16).astype(f32)
        return jnp.concatenate([v_high, v - v_high], axis=0).astype(bf16)

    def packed(v):
        at = late_rows
        return jnp.concatenate(
            [v[0:at].astype(bf16), parts(v[at : at + 8] + v[at + 8 : at + 16])], axis=0
        )

    vec = parts(vec)
    for piece in range(ends):
        late_a[piece, late_rows : late_rows + 16, :] = vec
    late_ra[end] = late_a[end]
    la_src, la_dst = (lambda t: late_a.at[t]), (lambda me: late_ra.at[me])
    spread_out(5, "a", la_src, la_dst)

    collect(0, "a", a_src, a_dst)
    part = added(main_ra, ends)
    sub = main_rows // ys
    for k in range(ys):
        main_b[k] = part[k * sub : (k + 1) * sub]
    main_rb[y] = main_b[y]
    b_src, b_dst = (lambda t: main_b.at[t]), (lambda me: main_rb.at[me])
    spread_out(1, "b", b_src, b_dst)

    sd, sx = sums(5, 128)
    k1 = k0 * sd * (1.0 / count)
    k2 = k0 * sx * (1.0 / count)

    def last(p, carry):
        dh = (k0 * grad1[p] - k1 - k2 * pre1[p]).astype(bf16)
        for q in range(2):
            r = 2 * p + q
            gi_v[r] = (dotf(dh, w_in[q]) + e3[r]).astype(bf16)
            pltpu.make_async_copy(gi_v.at[r], gimages.at[0, r], out_sem.at[1, r]).start()
        return carry

    lax.fori_loop(0, 2, last, 0)

    collect(5, "a", la_src, la_dst)
    late_b[y] = packed(added(late_ra, ends))
    lb_src, lb_dst = (lambda t: late_b.at[y]), (lambda me: late_b.at[me])
    spread_out(6, "b", lb_src, lb_dst)

    collect(1, "b", b_src, b_dst)
    main_c[z] = added(main_rb, ys)
    c_src, c_dst = (lambda t: main_c.at[z]), (lambda me: main_c.at[me])
    spread_out(2, "c", c_src, c_dst)

    lax.fori_loop(2, 4, last, 0)

    collect(6, "b", lb_src, lb_dst)
    late_c[z] = packed(added(late_b, ys))
    lc_src, lc_dst = (lambda t: late_c.at[z]), (lambda me: late_c.at[me])
    spread_out(7, "c", lc_src, lc_dst)

    collect(2, "c", c_src, c_dst)
    main_gb[y] = added(main_c, zs)
    gb_src, gb_dst = (lambda t: main_gb.at[y]), (lambda me: main_gb.at[me])
    spread_out(3, "b", gb_src, gb_dst)

    collect(7, "c", lc_src, lc_dst)
    whole = added(late_c, zs)
    late_ga[end] = whole[0:late_rows].astype(bf16)
    lg_src, lg_dst = (lambda t: late_ga.at[end]), (lambda me: late_ga.at[me])
    spread_out(8, "a", lg_src, lg_dst)

    collect(3, "b", gb_src, gb_dst)
    main_ga[end] = main_gb[...].reshape(main_rows, 128).astype(bf16)
    ga_src, ga_dst = (lambda t: main_ga.at[end]), (lambda me: main_ga.at[me])
    spread_out(4, "a", ga_src, ga_dst)

    def sent(*stages):
        for stage, name, src, dst in stages:
            for k in range(1, groups[name][0]):
                copy_to(stage, name, src, dst, k).wait_send()

    for idx in range(6):
        for k in range(1, 3):
            pltpu.make_async_remote_copy(
                src_ref=xbuf.at[idx, s], dst_ref=xbuf.at[idx, s],
                send_sem=xs_sem.at[idx, k - 1], recv_sem=xr_sem.at[idx, s],
                device_id=(d, lax.rem(s + k, spaces)), device_id_type=MESH,
            ).wait_send()
    for k in range(1, 3):
        cross_copy(0, cross, k).wait_send()
        cross_copy(1, cross2, k).wait_send()
    end_halo(edge1, halo1, 0)
    end_halo(edge2, halo2, 1)
    end_halo(edge3, halo3, 2)
    sent(
        (0, "a", a_src, a_dst), (1, "b", b_src, b_dst), (2, "c", c_src, c_dst), (3, "b", gb_src, gb_dst),
        (5, "a", la_src, la_dst), (6, "b", lb_src, lb_dst), (7, "c", lc_src, lc_dst),
    )
    for r in range(8):
        pltpu.make_async_copy(res_v.at[r], result.at[0, r], out_sem.at[0, r]).wait()
        pltpu.make_async_copy(gi_v.at[r], gimages.at[0, r], out_sem.at[1, r]).wait()
    scale = 1.0 / lax.axis_size("dp")
    o_vec[...] = (whole[late_rows : late_rows + 8] + whole[late_rows + 8 : late_rows + 16]) * scale
    collect(8, "a", lg_src, lg_dst)
    late = late_ga[...].reshape(LATE_ROWS, 128).astype(f32) * scale
    o_reduce[:, 0:128] = late[0:64]
    o_reduce[:, 128:256] = late[64:128]
    collect(4, "a", ga_src, ga_dst)
    main = main_ga[...].reshape(MAIN_ROWS, 128).astype(f32) * scale
    for u in range(3):
        pair = main[128 * u : 128 * u + 128].T
        for t in range(4 if u < 2 else 1):
            a, b = 64 * (t % 2), 64 * (t // 2)
            o_dilated[4 * u + t] = pair[a : a + 64, b : b + 64]
    o_expand[:, 0:128] = main[320:384]
    o_expand[:, 128:256] = main[384:448]
    outs = []
    for k, (src, dst) in enumerate(
        ((o_reduce, h_reduce), (o_dilated, h_dilated), (o_expand, h_expand), (o_vec, h_vec))
    ):
        outs.append(pltpu.make_async_copy(src, dst, out_sem.at[2, k]))
        outs[-1].start()

    sent((4, "a", ga_src, ga_dst), (8, "a", lg_src, lg_dst))
    for c in outs:
        c.wait()


def store(*refs):
    ins, outs, held, (half, full, sem) = refs[:6], refs[6:17], refs[17:23], refs[23:]
    vec = held[5]
    parts = []
    for k in range(2):
        for r in range(4):
            rows = pl.ds(2 * r, 2)
            parts.append((ins[k].at[0, rows], held[k].at[0, rows], outs[k].at[0, rows]))
    parts += [(ins[k], held[k], outs[k]) for k in range(2, 5)]
    fetches = [pltpu.make_async_copy(p[0], p[1], sem.at[0, k]) for k, p in enumerate(parts)]
    fetches.append(pltpu.make_async_copy(ins[5], vec, sem.at[0, 11]))
    for c in fetches:
        c.start()
    copies = []
    for k, p in enumerate(parts):
        fetches[k].wait()
        copies.append(pltpu.make_async_copy(p[1], p[2], sem.at[1, k]))
        copies[-1].start()
    fetches[-1].wait()
    for k, row in enumerate((5, 4)):
        v = vec[row : row + 1, :]
        half[2 * k] = v[:, 0:64]
        half[2 * k + 1] = pltpu.roll(jnp.broadcast_to(v, (8, 128)), 64, 1)[0:1, 0:64]
    for k in range(2):
        full[k] = jnp.concatenate([vec[2 * k : 2 * k + 1, :], vec[2 * k + 1 : 2 * k + 2, :]], axis=1)
    for k in range(4):
        copies.append(pltpu.make_async_copy(half.at[k], outs[5 + k], sem.at[1, 11 + k]))
        copies[-1].start()
    for k in range(2):
        copies.append(pltpu.make_async_copy(full.at[k], outs[9 + k], sem.at[1, 15 + k]))
        copies[-1].start()
    for c in copies:
        c.wait()


def solution(mesh):
    splits = SPLITS[mesh.shape["dp"]]
    ends, ys, highs = splits
    zs = highs * mesh.shape["space"]
    main_rows = MAIN_ROWS // ends
    late_rows = LATE_ROWS // ends
    sub = main_rows // ys

    def shards(images, wr, wd, we, g1, s1, g2, s2, g3, s3, cot):
        vmem = pl.BlockSpec(memory_space=pltpu.VMEM)
        hbm = pl.BlockSpec(memory_space=pltpu.HBM)
        big = jax.ShapeDtypeStruct(images.shape, bf16)
        maps = lambda: pltpu.VMEM((4, 288, 128), f32)
        outs = pl.pallas_call(
            functools.partial(kernel, splits),
            out_shape=(
                big, big,
                jax.ShapeDtypeStruct((64, 256), f32),
                jax.ShapeDtypeStruct((9, 64, 64), f32),
                jax.ShapeDtypeStruct((64, 256), f32),
                jax.ShapeDtypeStruct((8, 128), f32),
            ),
            in_specs=[hbm] * 11,
            out_specs=(hbm,) * 6,
            scratch_shapes=[
                pltpu.VMEM((8, 288, 256), bf16),
                pltpu.VMEM((8, 288, 256), bf16),
                pltpu.VMEM((64, 256), f32),
                pltpu.VMEM((9, 64, 64), f32),
                pltpu.VMEM((64, 256), f32),
                pltpu.VMEM((8, 128), f32),
                pltpu.VMEM((2, 4, 288, 256), bf16),
                pltpu.VMEM((8, 288, 256), bf16),
                pltpu.VMEM((64, 256), bf16),
                pltpu.VMEM((3, 3, 64, 64), bf16),
                pltpu.VMEM((64, 256), bf16),
                pltpu.VMEM((1, 64), f32), pltpu.VMEM((1, 64), f32),
                pltpu.VMEM((1, 64), f32), pltpu.VMEM((1, 64), f32),
                pltpu.VMEM((1, 256), f32), pltpu.VMEM((1, 256), f32),
                pltpu.VMEM((2, 128, 256), bf16),
                pltpu.VMEM((2, 128, 256), bf16),
                pltpu.VMEM((3, 384, 128), bf16),
                pltpu.VMEM((3, 128, 384), bf16),
                maps(), maps(), maps(), maps(),
                pltpu.VMEM((4, 288, 128), bf16),
                pltpu.VMEM((8, 288, 256), f32),
                pltpu.VMEM((8, 288, 256), f32),
                pltpu.VMEM((2, 4, 288, 256), bf16),
                maps(), maps(),
                pltpu.VMEM((4, 288, 128), bf16),
                pltpu.VMEM((2, 288, 128), bf16),
                pltpu.VMEM((2, 288, 128), bf16),
                pltpu.VMEM((2, 288, 128), bf16),
                pltpu.VMEM((2, 288, 128), bf16),
                pltpu.VMEM((2, 288, 128), bf16),
                pltpu.VMEM((2, 288, 128), bf16),
                pltpu.VMEM((6 * 288, 384), bf16),
                pltpu.VMEM((6 * 288, 384), bf16),
                pltpu.VMEM((6, 3, 8, 256), f32),
                pltpu.VMEM((3, 72, 256), f32),
                pltpu.VMEM((3, 5, 72, 128), f32),
                pltpu.VMEM((72, 256), f32),
                pltpu.VMEM((5, 72, 128), f32),
                pltpu.VMEM((ends, main_rows, 128), bf16),
                pltpu.VMEM((ends, main_rows, 128), bf16),
                pltpu.VMEM((ys, sub, 128), f32),
                pltpu.VMEM((ys, sub, 128), f32),
                pltpu.VMEM((zs, sub, 128), f32),
                pltpu.VMEM((ys, sub, 128), f32),
                pltpu.VMEM((ends, main_rows, 128), bf16),
                pltpu.VMEM((ends, late_rows + 16, 128), bf16),
                pltpu.VMEM((ends, late_rows + 16, 128), bf16),
                pltpu.VMEM((ys, late_rows + 16, 128), bf16),
                pltpu.VMEM((zs, late_rows + 16, 128), bf16),
                pltpu.VMEM((ends, late_rows, 128), bf16),
                pltpu.SemaphoreType.DMA((18,)),
                pltpu.SemaphoreType.DMA((3, 8)),
                pltpu.SemaphoreType.DMA((3, 2)),
                pltpu.SemaphoreType.DMA((3, 2)),
                pltpu.SemaphoreType.DMA((6, 2)),
                pltpu.SemaphoreType.DMA((6, 3)),
                pltpu.SemaphoreType.DMA((2, 3)),
                pltpu.SemaphoreType.DMA((2, 3)),
                pltpu.SemaphoreType.DMA((9, 12)),
                pltpu.SemaphoreType.DMA((9, 12)),
            ],
            compiler_params=pltpu.CompilerParams(
                collective_id=0, has_side_effects=True, vmem_limit_bytes=60 * 1024 * 1024
            ),
        )(
            images, wr.T, wd, we,
            g1.reshape(1, 64), s1.reshape(1, 64), g2.reshape(1, 64), s2.reshape(1, 64),
            g3.reshape(1, 256), s3.reshape(1, 256), cot,
        )
        res, gi, g_reduce, g_dilated, g_expand, v1, v2, v3, v4, v5, v6 = pl.pallas_call(
            store,
            out_shape=tuple(jax.ShapeDtypeStruct(x.shape, x.dtype) for x in outs[:5])
            + (jax.ShapeDtypeStruct((1, 64), f32),) * 4
            + (jax.ShapeDtypeStruct((1, 256), f32),) * 2,
            in_specs=[hbm] * 6,
            out_specs=(hbm,) * 11,
            scratch_shapes=[pltpu.VMEM(x.shape, x.dtype) for x in outs] + [
                pltpu.VMEM((4, 1, 64), f32),
                pltpu.VMEM((2, 1, 256), f32),
                pltpu.SemaphoreType.DMA((2, 17)),
            ],
            compiler_params=pltpu.CompilerParams(vmem_limit_bytes=60 * 1024 * 1024),
        )(*outs)
        return (
            res, gi, g_reduce.T, g_dilated.reshape(3, 3, 64, 64), g_expand,
            v1.reshape(64), v2.reshape(64), v3.reshape(64), v4.reshape(64),
            v5.reshape(256), v6.reshape(256),
        )

    placed = (P("dp", "space", None, None),) + (P(),) * 9 + (P("dp", "space", None, None),)
    return jax.shard_map(
        shards,
        mesh=mesh,
        in_specs=placed,
        out_specs=(P("dp", "space", None, None),) * 2 + (P(),) * 9,
        check_vma=False,
    )
```
